32 devices in a mesh: groups: 2 (over y), row: 4 (over x, core), col: 4 (over z).
Axes of the slice: x: 2, y: 2, z: 4, core: 2. Of those that a mesh axis runs over, the one named last changes fastest.
Arguments:
- right_sides: float32 [32, 16384], P(None, ('groups', 'row')), parts along dimension 1
- nugget: float32 [16384], P(('groups', 'row')), parts along dimension 0, may hold values from 1 to 4
- cov_blocks: bfloat16 [8, 4, 32, 256, 256], P(('groups', 'row'), 'col'), parts along dimension 0
- block_rows: int32 [8, 4, 32], P(('groups', 'row'), 'col'), parts along dimension 0, may hold values from 0 to 7, as said below
- block_cols: int32 [8, 4, 32], P(('groups', 'row'), 'col'), parts along dimension 0, may hold values from 0 to 7, as said below
- block_count: int32 [8, 4], P(('groups', 'row'), 'col'), parts along dimension 0, may hold values from 4 to 32, as said below
Outputs:
- solution: float32 [32, 16384], P(None, ('groups', 'row')), parts along dimension 1
- residual: float32 [32, 16384], P(None, ('groups', 'row')), parts along dimension 1
The draws below stay inside these ranges and needn't reach their ends.
There are 2 independent parts, one for each index of `groups`. The reference program is written for one: setup_inputs(seed, part) draws one part's arguments, and reference() takes and returns one part's arrays. A program takes and returns all parts, laid end to end along the dimension named above; each array names one. Nothing has to cross between parts.
Inputs may be any that keep to these rules, and one draw needn't show every extreme that they name: On each device the pairs (block_rows, block_cols) of all 32 slots are distinct; no stored block position of a problem is the mirror image of another (no pair is stored both as (g, h) and as (h, g)); on devices whose row and col index are equal, block_rows <= block_cols. `block_cols`: see block_rows. `block_count`: slots at or beyond the count are empty; some device of every problem has exactly 32 live slots.
All inputs are finite; a program needn't handle non-finite values.
Results may differ from the reference program's by a relative error of at most 0.0003.
Values sent between devices are 32-bit elements; how exact they have to be, the bound alone decides.
No kernel may reach another device: no remote copies, remote signals or barrier semaphores. Data moves between devices by JAX's collectives and lax.ppermute only.
A program may use at most 64 MiB of HBM per device.

```python
import math
import jax
import jax.numpy as jnp
from jax import lax

BLOCK = 256
RHS = 32
BR = 8
SLOTS = 32
ITERS = 2
STATIONS = 8192
N_ROW = 4
N_COL = 4


def placed_pairs(key):
    base_key = jax.random.fold_in(key, 11)
    cell_total = BR * BR
    position = jnp.arange(cell_total, dtype=jnp.int32)
    local_row = position // BR
    local_col = position % BR
    row_ids = jnp.arange(N_ROW, dtype=jnp.int32)[:, None, None]
    col_ids = jnp.arange(N_COL, dtype=jnp.int32)[None, :, None]
    parity = (local_row + local_col) % 2
    usable = jnp.where(row_ids < col_ids, parity == 0, jnp.where(row_ids > col_ids, parity == 1, local_row <= local_col))
    scores = jax.random.randint(base_key, (N_ROW, N_COL, cell_total), 0, 4096, dtype=jnp.int32) * cell_total + position
    scores = jnp.where(usable, scores, scores + 4096 * cell_total)
    ranked = jnp.argsort(scores, axis=-1, stable=True)[..., :SLOTS].astype(jnp.int32)
    return (ranked // BR, ranked % BR)


def draw_block_rows(key, part):
    return placed_pairs(key)[0]


def draw_block_cols(key, part):
    return placed_pairs(key)[1]


def draw_block_count(key, part):
    key_one = jax.random.fold_in(key, 21)
    key_two = jax.random.fold_in(key, 22)
    key_three = jax.random.fold_in(key, 23)
    lowest = SLOTS // 8
    spread_range = SLOTS - lowest
    first_draw = jax.random.randint(key_one, (N_ROW, N_COL), 0, spread_range + 1, dtype=jnp.int32)
    second_draw = jax.random.randint(key_two, (N_ROW, N_COL), 0, spread_range + 1, dtype=jnp.int32)
    counts = lowest + first_draw * second_draw // max(spread_range, 1)
    full_device = jax.random.randint(key_three, (), 0, N_ROW * N_COL, dtype=jnp.int32)
    flat_ids = jnp.arange(N_ROW * N_COL, dtype=jnp.int32).reshape(N_ROW, N_COL)
    return jnp.where(flat_ids == full_device, SLOTS, counts).astype(jnp.int32)


def draw_cov_blocks(key, part):
    base_key = jax.random.fold_in(key, 31)
    spread_scale = 0.3 * (2.0 * N_COL * SLOTS * BLOCK / BR) ** (-0.5)
    shape_all = (N_ROW, N_COL, SLOTS, BLOCK, BLOCK)
    noise_part = jax.random.normal(base_key, shape_all, jnp.float32)
    return (spread_scale * noise_part).astype(jnp.bfloat16)


def draw_right_sides(key, part):
    base_key = jax.random.fold_in(key, 41)
    ramped = 1.0 + 2.0 * jnp.arange(STATIONS, dtype=jnp.float32) / (STATIONS - 1)
    noise_part = jax.random.normal(base_key, (RHS, STATIONS), jnp.float32)
    return jnp.clip(noise_part, -6.0, 6.0) * ramped[None, :]


def block_scale(rng, dims, shards, smallest, largest):
    def one(dim, parts):
        heights = jax.random.uniform(jax.random.fold_in(jax.random.fold_in(rng, 6), dim), (parts,), jnp.float32, smallest / len(shards), largest / len(shards))
        return jnp.repeat(jnp.exp(heights), dims[dim] // parts).reshape((-1,) + (1,) * (len(dims) - dim - 1))

    loudness = one(*shards[0])
    for cut in shards[1:]:
        loudness = loudness * one(*cut)
    return loudness


def setup_inputs(seed: int = 0, part: int = 0) -> dict:
    arg_keys = jax.random.split(jax.random.key(seed), 7)
    part_keys = jax.random.split(jax.random.fold_in(arg_keys[6], part), 7)
    return {
        "right_sides": draw_right_sides(jax.random.fold_in(jax.random.fold_in(arg_keys[6], part), 71), part),
        "nugget": jnp.clip(jnp.exp(math.log(4.0) - 1.3862944 * jax.random.uniform(part_keys[1], (STATIONS,), jnp.float32) ** block_scale(part_keys[1], (STATIONS,), ((0, 4),), -0.2, 0.2)), 1.0, 4.0),
        "cov_blocks": draw_cov_blocks(jax.random.fold_in(jax.random.fold_in(arg_keys[6], part), 71), part),
        "block_rows": draw_block_rows(jax.random.fold_in(jax.random.fold_in(arg_keys[6], part), 71), part),
        "block_cols": draw_block_cols(jax.random.fold_in(jax.random.fold_in(arg_keys[6], part), 71), part),
        "block_count": draw_block_count(jax.random.fold_in(jax.random.fold_in(arg_keys[6], part), 71), part),
    }


def apply_cov(field, nugget, cov_blocks, block_rows, block_cols, block_count):
    tile_count = STATIONS // BLOCK
    tile_view = field.reshape(RHS, tile_count, BLOCK)
    col_ids = jnp.arange(N_COL, dtype=jnp.int32)
    slot_ids = jnp.arange(SLOTS, dtype=jnp.int32)

    def row_update(summed, items):
        row_index, blocks, slot_rows, slot_cols, live_count = items
        live_weight = (slot_ids[None, :] < live_count[:, None]).astype(jnp.float32).reshape(-1)
        glob_rows = (row_index * BR + slot_rows).reshape(-1).astype(jnp.int32)
        glob_cols = (col_ids[:, None] * BR + slot_cols).reshape(-1).astype(jnp.int32)
        matrices = blocks.reshape(N_COL * SLOTS, BLOCK, BLOCK).astype(jnp.float32)
        direct = jnp.einsum("rmk,mjk->rmj", tile_view[:, glob_cols], matrices,
                            precision=lax.Precision.HIGHEST) * live_weight[None, :, None]
        mirror = jnp.einsum("rmj,mjk->rmk", tile_view[:, glob_rows], matrices,
                            precision=lax.Precision.HIGHEST) * live_weight[None, :, None]
        summed = summed.at[:, glob_rows].add(direct)
        summed = summed.at[:, glob_cols].add(mirror)
        return summed, None

    empty_sum = jnp.zeros((RHS, tile_count, BLOCK), jnp.float32)
    summed, _ = lax.scan(row_update, empty_sum,
                         (jnp.arange(N_ROW, dtype=jnp.int32), cov_blocks, block_rows, block_cols, block_count))
    return nugget[None, :] * field + summed.reshape(RHS, STATIONS)


def reference(right_sides, nugget, cov_blocks, block_rows, block_cols, block_count):
    solution = jnp.zeros_like(right_sides)
    residual = right_sides
    direction = right_sides
    norm_now = jnp.sum(residual * residual, axis=1)
    for turn_index in range(ITERS):
        applied = apply_cov(direction, nugget, cov_blocks, block_rows, block_cols, block_count)
        step_size = norm_now / jnp.sum(direction * applied, axis=1)
        solution = solution + step_size[:, None] * direction
        residual = residual - step_size[:, None] * applied
        norm_next = jnp.sum(residual * residual, axis=1)
        direction = residual + (norm_next / norm_now)[:, None] * direction
        norm_now = norm_next
    return solution, residual
```

```python
import functools

import jax
import jax.numpy as jnp
from jax import lax
from jax.experimental import pallas as pl
from jax.experimental.pallas import tpu as pltpu
from jax.sharding import PartitionSpec as P

ITERS = 2
LANES = 128
GROUP = 8
BF16 = jnp.bfloat16
F32 = jnp.float32


def send_to(i, d, n):
    return i ^ d if n & (n - 1) == 0 else (i + d) % n


def shifted(value, axis, d, n):
    return lax.ppermute(value, axis, [(i, send_to(i, d, n)) for i in range(n)])


def transposed(value, n):
    pairs = [(r * n + c, c * n + r) for r in range(n) for c in range(n)]
    return lax.ppermute(value, ("row", "col"), pairs)


def load_pair(dst, tile, value):
    rhs = value.shape[0]
    high = value.astype(BF16)
    dst[tile, :rhs, :] = high
    dst[tile, rhs:, :] = (value - high.astype(F32)).astype(BF16)


def product(pair, block, contract):
    both = lax.dot_general(pair, block, (((1,), (contract,)), ((), ())), preferred_element_type=F32)
    rhs = both.shape[0] // 2
    return both[:rhs] + both[rhs:]


def pack_stats(columns, rhs):
    lane = lax.broadcasted_iota(jnp.int32, (8, LANES), 1)
    tile = jnp.zeros((8, LANES), F32)
    groups = rhs // 8
    for i, column in enumerate(columns):
        for g in range(groups):
            tile = jnp.where(lane == i * groups + g, column[g * 8:(g + 1) * 8], tile)
    return tile


def unpack_stat(tile, i, rhs):
    groups = rhs // 8
    return jnp.concatenate([tile[:, i * groups + g:i * groups + g + 1] for g in range(groups)], axis=0)


def accumulate(total, tile, value):
    width = value.shape[1] // LANES
    for part in range(width):
        total[tile * width + part] += value[:, part * LANES:(part + 1) * LANES]


def add_blocks(blocks, step, slot_of, live, pairs, total, read_index, write_index, contract):
    values = []
    for g in range(GROUP):
        slot = step * GROUP + g
        value = product(pairs[read_index[0, 0, slot]], blocks[g], contract)
        values.append((write_index[0, 0, slot], jnp.where(slot < live, value, 0.0)))
    for tile, value in values:
        accumulate(total, tile, value)


def write_chunks(outs, total, me, n, per, rhs):
    for d, out in enumerate(outs):
        first = send_to(me, d, n) * per
        for i in range(per):
            out[i * rhs:(i + 1) * rhs, :] = total[first + i]


def row_sums(value):
    return jnp.sum(value, axis=1, keepdims=True)


def first_kernel(n, per, mirror, slot_rows, slot_cols, live_ref, right, *rest):
    if mirror:
        blocks, (outs, (pairs, total)) = rest[0], (rest[1:1 + n], rest[1 + n:])
    else:
        near, nugget, blocks = rest[:3]
        outs, (pairs, total) = rest[3:3 + n], rest[3 + n:]
    step = pl.program_id(0)
    rhs = right.shape[0]
    tile_size = blocks.shape[1]
    tiles = right.shape[1] // tile_size

    @pl.when(step == 0)
    def _():
        total[...] = jnp.zeros_like(total)
        for tile in range(tiles):
            load_pair(pairs, tile, right[:, tile * tile_size:(tile + 1) * tile_size])

    live = live_ref[0, 0]

    @pl.when(step * GROUP < live)
    def _():
        if mirror:
            add_blocks(blocks, step, None, live, pairs, total, slot_rows, slot_cols, 0)
        else:
            add_blocks(blocks, step, None, live, pairs, total, slot_cols, slot_rows, 1)

    @pl.when(step == pl.num_programs(0) - 1)
    def _():
        data = per * rhs
        if mirror:
            write_chunks(outs, total, lax.axis_index("row"), n, per, rhs)
            value = right[...]
            stats = [row_sums(value * value)]
            tile = pack_stats(stats, rhs)
            for out in outs:
                out[data:, :] = tile
        else:
            write_chunks(outs, total, lax.axis_index("col"), n, per, rhs)
            value = near[...]
            cross = jnp.zeros((rhs, LANES), F32)
            for i in range(total.shape[0]):
                cross += total[i] * value[:, i * LANES:(i + 1) * LANES]
            cross = 2.0 * row_sums(cross)
            own = row_sums(value * value * nugget[...])
            tile = pack_stats([cross], rhs)
            outs[0][data:, :] = pack_stats([cross + own], rhs)
            for out in outs[1:]:
                out[data:, :] = tile


def add_all(refs):
    value = refs[0][...]
    for ref in refs[1:]:
        value += ref[...]
    return value


def sum_first_kernel(n, per, right, nugget, *refs):
    direct, mirror, out = refs[:n], refs[n:2 * n], refs[2 * n]
    rhs = right.shape[0]
    width = per * LANES
    size = direct[0].shape[0]
    out[:size, :] = add_all(direct)
    out[size:, :] = add_all(mirror)
    me = lax.axis_index("col")
    for k in range(n):
        @pl.when(me == k)
        def _():
            for i in range(per):
                lanes = slice(k * width + i * LANES, k * width + (i + 1) * LANES)
                out[i * rhs:(i + 1) * rhs, :] += right[:, lanes] * nugget[:, lanes]


def combine_first_kernel(data, mine, other, near, far, base):
    size = mine.shape[0] // 2
    near[...] = mine[:data, :] + other[size:size + data, :]
    far[:data, :] = other[:data, :] + mine[size:size + data, :]
    far[data:, :] = mine[data:size, :]
    base[...] = mine[size + data:, :]


def scatter_chunks(refs, me, n, per, rhs, total):
    for d in range(n):
        first = send_to(me, d, n) * per
        for i in range(per):
            total[first + i] = refs[d][i * rhs:(i + 1) * rhs, :]


def second_kernel(n, per, slot_rows, slot_cols, live_ref, near, far, nugget, base, *rest):
    near_parts, far_parts, blocks = rest[:n], rest[n:2 * n], rest[2 * n]
    direct, mirror = rest[2 * n + 1:3 * n + 1], rest[3 * n + 1:4 * n + 1]
    left, curve, near_pairs, far_pairs, direct_total, mirror_total = rest[4 * n + 1:]
    step = pl.program_id(0)
    rhs = near.shape[0]
    data = per * rhs
    tile_size = blocks.shape[1]
    width = tile_size // LANES
    tiles = near.shape[1] // tile_size

    @pl.when(step == 0)
    def _():
        norm = unpack_stat(base[...], 0, rhs)
        stat = far_parts[0][data:, :]
        for part in far_parts[1:]:
            stat += part[data:, :]
        curve[...] = stat
        size_now = norm / unpack_stat(stat, 0, rhs)
        scatter_chunks(near_parts, lax.axis_index("col"), n, per, rhs, direct_total)
        scatter_chunks(far_parts, lax.axis_index("row"), n, per, rhs, mirror_total)
        for source, image, pairs in ((near, direct_total, near_pairs), (far, mirror_total, far_pairs)):
            for tile in range(tiles):
                pieces = []
                for part in range(width):
                    i = tile * width + part
                    pieces.append(source[:, i * LANES:(i + 1) * LANES] - size_now * image[i])
                value = jnp.concatenate(pieces, axis=1)
                load_pair(pairs, tile, value)
                if source is near:
                    left[:, tile * tile_size:(tile + 1) * tile_size] = value
        direct_total[...] = jnp.zeros_like(direct_total)
        mirror_total[...] = jnp.zeros_like(mirror_total)

    live = live_ref[0, 0]

    @pl.when(step * GROUP < live)
    def _():
        add_blocks(blocks, step, None, live, near_pairs, mirror_total, slot_rows, slot_cols, 0)
        add_blocks(blocks, step, None, live, far_pairs, direct_total, slot_cols, slot_rows, 1)

    @pl.when(step == pl.num_programs(0) - 1)
    def _():
        write_chunks(direct, direct_total, lax.axis_index("col"), n, per, rhs)
        write_chunks(mirror, mirror_total, lax.axis_index("row"), n, per, rhs)
        value = left[...]
        cross = jnp.zeros((rhs, LANES), F32)
        for i in range(direct_total.shape[0]):
            cross += direct_total[i] * value[:, i * LANES:(i + 1) * LANES]
        square = value * value
        tile = pack_stats([row_sums(square), row_sums(square * nugget[...]), 2.0 * row_sums(cross)], rhs)
        for out in mirror:
            out[data:, :] = tile


def sum_second_kernel(n, data, *refs):
    direct, mirror, out_direct, out_mirror, stat = refs[:n], refs[n:2 * n], *refs[2 * n:]
    out_direct[...] = add_all(direct)
    value = add_all(mirror)
    out_mirror[...] = value[:data, :]
    stat[...] = value[data:, :]


def combine_second_kernel(data, mine, other, stat, out):
    out[:data, :] = mine[...] + other[...]
    out[data:, :] = stat[...]


def last_kernel(n, per, right, left, nugget, base, curve, *rest):
    parts, (solution, residual, total) = rest[:n], rest[n:]
    rhs = right.shape[0]
    data = per * rhs
    scatter_chunks(parts, lax.axis_index("col"), n, per, rhs, total)
    norm = unpack_stat(base[...], 0, rhs)
    size_now = norm / unpack_stat(curve[...], 0, rhs)
    stats = [part[data:, :] for part in parts]
    norm_next = unpack_stat(stats[0], 0, rhs)
    bend = unpack_stat(stats[0], 1, rhs)
    for stat in stats:
        bend += unpack_stat(stat, 2, rhs)
    ratio = norm_next / norm
    size_next = norm_next / (bend - ratio * norm_next / size_now)
    back = ratio / size_now
    for i in range(total.shape[0]):
        lanes = slice(i * LANES, (i + 1) * LANES)
        first = right[:, lanes]
        now = left[:, lanes]
        solution[:, lanes] = size_now * first + size_next * (now + ratio * first)
        image = nugget[:, lanes] * now + total[i] + back * (first - now)
        residual[:, lanes] = now - size_next * image


def whole(shape):
    return pl.BlockSpec(shape, lambda *_: (0,) * len(shape))


def shape_of(*shape):
    return jax.ShapeDtypeStruct(shape, F32)


def on_device(n, right_sides, nugget, cov_blocks, block_rows, block_cols, block_count):
    rhs, width = right_sides.shape
    slots, tile_size = cov_blocks.shape[2:4]
    per = width // n // LANES
    data = per * rhs
    size = data + 8
    tiles = width // tile_size
    steps = slots // GROUP
    noise = nugget.reshape(1, width)
    smem = [pl.BlockSpec(memory_space=pltpu.SMEM)] * 3
    index = (block_rows, block_cols, block_count)
    field = whole((rhs, width))
    thin = whole((1, width))
    chunk = whole((size, LANES))
    plain = whole((data, LANES))
    small = whole((8, LANES))
    block = pl.BlockSpec((None, None, GROUP, tile_size, tile_size), lambda i: (0, 0, i, 0, 0))
    pair = pltpu.VMEM((tiles, 2 * rhs, tile_size), BF16)
    total = pltpu.VMEM((width // LANES, rhs, LANES), F32)
    params = pltpu.CompilerParams(vmem_limit_bytes=32 * 1024 * 1024)
    cost = pl.CostEstimate(flops=4 * rhs * slots * tile_size * tile_size, transcendentals=0,
                           bytes_accessed=2 * slots * tile_size * tile_size)

    far_right = transposed(right_sides, n)
    mirror = pl.pallas_call(
        functools.partial(first_kernel, n, per, True),
        grid=(steps,),
        in_specs=smem + [field, block],
        out_specs=[chunk] * n,
        out_shape=[shape_of(size, LANES)] * n,
        scratch_shapes=[pair, total],
        compiler_params=params,
        cost_estimate=cost,
        name="mirror_first",
    )(*index, right_sides, cov_blocks)
    mirror = [mirror[0]] + [shifted(mirror[d], "row", d, n) for d in range(1, n)]
    direct = pl.pallas_call(
        functools.partial(first_kernel, n, per, False),
        grid=(steps,),
        in_specs=smem + [field, field, thin, block],
        out_specs=[chunk] * n,
        out_shape=[shape_of(size, LANES)] * n,
        scratch_shapes=[pair, total],
        compiler_params=params,
        cost_estimate=cost,
        name="direct_first",
    )(*index, far_right, right_sides, noise, cov_blocks)
    direct = [direct[0]] + [shifted(direct[d], "col", d, n) for d in range(1, n)]

    mine = pl.pallas_call(
        functools.partial(sum_first_kernel, n, per),
        out_shape=shape_of(2 * size, LANES),
        compiler_params=params,
        name="sum_first",
    )(right_sides, noise, *direct, *mirror)
    other = transposed(mine, n)
    near, far, base = pl.pallas_call(
        functools.partial(combine_first_kernel, data),
        out_shape=[shape_of(data, LANES), shape_of(size, LANES), shape_of(8, LANES)],
        compiler_params=params,
        name="combine_first",
    )(mine, other)
    near = [near] + [shifted(near, "col", d, n) for d in range(1, n)]
    far = [far] + [shifted(far, "row", d, n) for d in range(1, n)]

    out = pl.pallas_call(
        functools.partial(second_kernel, n, per),
        grid=(steps,),
        in_specs=smem + [field, field, thin, small] + [plain] * n + [chunk] * n + [block],
        out_specs=[plain] * n + [chunk] * n + [field, small],
        out_shape=[shape_of(data, LANES)] * n + [shape_of(size, LANES)] * n + [shape_of(rhs, width), shape_of(8, LANES)],
        scratch_shapes=[pair, pair, total, total],
        compiler_params=params,
        cost_estimate=cost,
        name="both_second",
    )(*index, right_sides, far_right, noise, base, *near, *far, cov_blocks)
    direct, mirror, left, curve = out[:n], out[n:2 * n], out[2 * n], out[2 * n + 1]
    direct = [direct[0]] + [shifted(direct[d], "col", d, n) for d in range(1, n)]
    mirror = [mirror[0]] + [shifted(mirror[d], "row", d, n) for d in range(1, n)]

    kept, sent, stat = pl.pallas_call(
        functools.partial(sum_second_kernel, n, data),
        out_shape=[shape_of(data, LANES), shape_of(data, LANES), shape_of(8, LANES)],
        compiler_params=params,
        name="sum_second",
    )(*direct, *mirror)
    other = transposed(sent, n)
    part = pl.pallas_call(
        functools.partial(combine_second_kernel, data),
        out_shape=shape_of(size, LANES),
        compiler_params=params,
        name="combine_second",
    )(kept, other, stat)
    parts = [part] + [shifted(part, "col", d, n) for d in range(1, n)]

    return pl.pallas_call(
        functools.partial(last_kernel, n, per),
        out_shape=(shape_of(rhs, width), shape_of(rhs, width)),
        scratch_shapes=[total],
        compiler_params=params,
        name="last",
    )(right_sides, left, noise, base, curve, *parts)


def solution(mesh):
    n = mesh.shape["row"]
    assert n == mesh.shape["col"]
    placed = (
        P(None, ("groups", "row")),
        P(("groups", "row")),
        P(("groups", "row"), "col", None, None, None),
        P(("groups", "row"), "col", None),
        P(("groups", "row"), "col", None),
        P(("groups", "row"), "col"),
    )
    return jax.shard_map(
        functools.partial(on_device, n),
        mesh=mesh,
        in_specs=placed,
        out_specs=(P(None, ("groups", "row")), P(None, ("groups", "row"))),
        check_vma=False,
    )
```

```python
import functools

import jax
import jax.numpy as jnp
from jax import lax
from jax.experimental import pallas as pl
from jax.experimental.pallas import tpu as pltpu
from jax.sharding import PartitionSpec as P

ITERS = 2
LANES = 128
GROUP = 8
BF16 = jnp.bfloat16
F32 = jnp.float32


def shifted(value, axis, d, n):
    return lax.ppermute(value, axis, [(i, i ^ d) for i in range(n)])


def to_all(value, axis, n):
    return [value] + [shifted(value, axis, d, n) for d in range(1, n)]


def to_owners(values, axis, n):
    return [values[0]] + [shifted(values[d], axis, d, n) for d in range(1, n)]


def transposed(value, n):
    pairs = [(r * n + c, c * n + r) for r in range(n) for c in range(n)]
    return lax.ppermute(value, ("row", "col"), pairs)


def from_diagonal(value, n):
    held = [value]
    for o in range(1, n):
        pairs = [(c * n + c, (c ^ o) * n + c) for c in range(n)]
        held.append(lax.ppermute(value, ("row", "col"), pairs))
    return held


def load_pair(dst, tile, value):
    rhs = value.shape[0]
    high = value.astype(BF16)
    dst[tile, :rhs, :] = high
    dst[tile, rhs:, :] = (value - high.astype(F32)).astype(BF16)


def product(pair, block, contract):
    both = lax.dot_general(pair, block, (((1,), (contract,)), ((), ())), preferred_element_type=F32)
    rhs = both.shape[0] // 2
    return both[:rhs] + both[rhs:]


def pack_stats(columns, rhs):
    lane = lax.broadcasted_iota(jnp.int32, (8, LANES), 1)
    tile = jnp.zeros((8, LANES), F32)
    groups = rhs // 8
    for i, column in enumerate(columns):
        for g in range(groups):
            tile = jnp.where(lane == i * groups + g, column[g * 8:(g + 1) * 8], tile)
    return tile


def unpack_stat(tile, i, rhs):
    groups = rhs // 8
    return jnp.concatenate([tile[:, i * groups + g:i * groups + g + 1] for g in range(groups)], axis=0)


def accumulate(total, tile, value):
    width = value.shape[1] // LANES
    for part in range(width):
        total[tile * width + part] += value[:, part * LANES:(part + 1) * LANES]


def add_blocks(blocks, slot_rows, slot_cols, live, pairs, total, mirror, ready=None):
    read, write, contract = (slot_rows, slot_cols, 0) if mirror else (slot_cols, slot_rows, 1)

    def body(step, carry):
        if ready is not None:
            ready(step)
        values = []
        for g in range(GROUP):
            slot = step * GROUP + g
            value = product(pairs[read[0, 0, slot]], blocks[slot], contract)
            values.append((write[0, 0, slot], jnp.where(slot < live, value, 0.0)))
        for tile, value in values:
            accumulate(total, tile, value)
        return carry

    lax.fori_loop(0, (live + GROUP - 1) // GROUP, body, 0)


def write_chunks(outs, total, me, per, rhs):
    for d, out in enumerate(outs):
        first = (me ^ d) * per
        for i in range(per):
            out[i * rhs:(i + 1) * rhs, :] = total[first + i]


def read_chunks(parts, total, me, per, rhs):
    for d, part in enumerate(parts):
        first = (me ^ d) * per
        for i in range(per):
            total[first + i] = part[i * rhs:(i + 1) * rhs, :]


def row_sums(value):
    return jnp.sum(value, axis=1, keepdims=True)


def cross_sums(total, value):
    rhs = value.shape[0]
    cross = jnp.zeros((rhs, LANES), F32)
    for i in range(total.shape[0]):
        cross += total[i] * value[:, i * LANES:(i + 1) * LANES]
    return row_sums(cross)


def tree_sum(values):
    values = list(values)
    while len(values) > 1:
        values = [a + b for a, b in zip(values[::2], values[1::2])]
    return values[0]


def fetch_index(sources, targets, sems):
    copies = [pltpu.make_async_copy(s, t, sems.at[i]) for i, (s, t) in enumerate(zip(sources, targets))]
    for copy in copies:
        copy.start()
    return copies


def mirror_first_kernel(n, per, *refs):
    index, count, right_hbm, cov = refs[:2], refs[2], refs[3], refs[4]
    outs, blocks = refs[5:5 + n], refs[5 + n]
    slot_rows, slot_cols, right, pairs, total, index_sems, right_sem, block_sems = refs[6 + n:]
    slots, tile_size = blocks.shape[:2]
    rhs = right.shape[0]

    def block_copy(i):
        part = pl.ds(i * GROUP, GROUP)
        return pltpu.make_async_copy(cov.at[0, 0, part], blocks.at[part], block_sems.at[i])

    copies = fetch_index(index, (slot_rows, slot_cols), index_sems)
    load = pltpu.make_async_copy(right_hbm, right, right_sem)
    load.start()
    block_copy(0).start()
    total[...] = jnp.zeros_like(total)
    for copy in copies:
        copy.wait()
    live = count[0, 0]
    for i in range(1, slots // GROUP):
        @pl.when(i * GROUP < live)
        def _():
            block_copy(i).start()
    load.wait()
    for tile in range(right.shape[1] // tile_size):
        load_pair(pairs, tile, right[:, tile * tile_size:(tile + 1) * tile_size])
    add_blocks(blocks, slot_rows, slot_cols, live, pairs, total, True, lambda i: block_copy(i).wait())
    write_chunks(outs, total, lax.axis_index("row"), per, rhs)


def direct_first_kernel(n, per, *refs):
    index, count, held, noise, blocks = refs[:2], refs[2], refs[3:3 + n], refs[3 + n], refs[4 + n]
    outs, (stat, far), scratch = refs[5 + n:5 + 2 * n], refs[5 + 2 * n:7 + 2 * n], refs[7 + 2 * n:]
    slot_rows, slot_cols, pairs, total, index_sems = scratch
    tile_size = blocks.shape[1]
    rhs, width = far.shape
    copies = fetch_index(index, (slot_rows, slot_cols), index_sems)
    offset = lax.axis_index("row") ^ lax.axis_index("col")
    for o in range(n):
        @pl.when(offset == o)
        def _():
            for tile in range(width // tile_size):
                value = held[o][:, tile * tile_size:(tile + 1) * tile_size]
                load_pair(pairs, tile, value)
                far[:, tile * tile_size:(tile + 1) * tile_size] = value
    total[...] = jnp.zeros_like(total)
    for copy in copies:
        copy.wait()
    add_blocks(blocks, slot_rows, slot_cols, count[0, 0], pairs, total, False)
    write_chunks(outs, total, lax.axis_index("col"), per, rhs)
    right = held[0][...]
    square = right * right
    stat[...] = pack_stats([row_sums(square), row_sums(square * noise[...]), 2.0 * cross_sums(total, right)], rhs)


def sum_kernel(*refs):
    refs[-1][...] = tree_sum(ref[...] for ref in refs[:-1])


def combine_first_kernel(n, per, right, noise, other, *refs):
    direct, stats, (payload, finished) = refs[:n], refs[n:2 * n], refs[2 * n:]
    rhs = right.shape[0]
    data = per * rhs
    width = per * LANES
    finished[...] = tree_sum(ref[...] for ref in direct) + other[...]
    me = lax.axis_index("col")
    for k in range(n):
        @pl.when(me == k)
        def _():
            for i in range(per):
                lanes = slice(k * width + i * LANES, k * width + (i + 1) * LANES)
                finished[i * rhs:(i + 1) * rhs, :] += right[:, lanes] * noise[:, lanes]
    payload[:data, :] = finished[...]
    payload[data:, :] = tree_sum(ref[...] for ref in stats)


def mirror_second_kernel(n, per, *refs):
    index, count, right, parts, blocks = refs[:2], refs[2], refs[3], refs[4:4 + n], refs[4 + n]
    outs, (left, base), scratch = refs[5 + n:5 + 2 * n], refs[5 + 2 * n:7 + 2 * n], refs[7 + 2 * n:]
    slot_rows, slot_cols, pairs, total, index_sems = scratch
    copies = fetch_index(index, (slot_rows, slot_cols), index_sems)
    tile_size = blocks.shape[1]
    rhs, width = right.shape
    data = per * rhs
    stats = [part[data:, :] for part in parts]
    norm = unpack_stat(stats[0], 0, rhs)
    bend = unpack_stat(stats[0], 1, rhs) + tree_sum(unpack_stat(stat, 2, rhs) for stat in stats)
    base[...] = pack_stats([norm, bend], rhs)
    size_now = norm / bend
    read_chunks(parts, total, lax.axis_index("col"), per, rhs)
    for i in range(width // LANES):
        lanes = slice(i * LANES, (i + 1) * LANES)
        left[:, lanes] = right[:, lanes] - size_now * total[i]
    for tile in range(width // tile_size):
        load_pair(pairs, tile, left[:, tile * tile_size:(tile + 1) * tile_size])
    total[...] = jnp.zeros_like(total)
    for copy in copies:
        copy.wait()
    add_blocks(blocks, slot_rows, slot_cols, count[0, 0], pairs, total, True)
    write_chunks(outs, total, lax.axis_index("row"), per, rhs)


def direct_second_kernel(n, per, *refs):
    index, count, far, left, noise, base = refs[:2], refs[2], refs[3], refs[4], refs[5], refs[6]
    parts, blocks = refs[7:7 + n], refs[7 + n]
    outs, stat, scratch = refs[8 + n:8 + 2 * n], refs[8 + 2 * n], refs[9 + 2 * n:]
    slot_rows, slot_cols, pairs, total, index_sems = scratch
    copies = fetch_index(index, (slot_rows, slot_cols), index_sems)
    tile_size = blocks.shape[1]
    rhs, width = far.shape
    size_now = unpack_stat(base[...], 0, rhs) / unpack_stat(base[...], 1, rhs)
    read_chunks(parts, total, lax.axis_index("row"), per, rhs)
    pieces = tile_size // LANES
    for tile in range(width // tile_size):
        image = jnp.concatenate([total[tile * pieces + i] for i in range(pieces)], axis=1)
        load_pair(pairs, tile, far[:, tile * tile_size:(tile + 1) * tile_size] - size_now * image)
    total[...] = jnp.zeros_like(total)
    for copy in copies:
        copy.wait()
    add_blocks(blocks, slot_rows, slot_cols, count[0, 0], pairs, total, False)
    write_chunks(outs, total, lax.axis_index("col"), per, rhs)
    value = left[...]
    square = value * value
    stat[...] = pack_stats([row_sums(square), row_sums(square * noise[...]), 2.0 * cross_sums(total, value)], rhs)


def combine_second_kernel(n, data, other, *refs):
    direct, stats, payload = refs[:n], refs[n:2 * n], refs[2 * n]
    payload[:data, :] = tree_sum(ref[...] for ref in direct) + other[...]
    payload[data:, :] = tree_sum(ref[...] for ref in stats)


def last_kernel(n, per, right, left, noise, base, *rest):
    parts, (solution, residual, total) = rest[:n], rest[n:]
    rhs = right.shape[0]
    data = per * rhs
    read_chunks(parts, total, lax.axis_index("col"), per, rhs)
    norm = unpack_stat(base[...], 0, rhs)
    size_now = norm / unpack_stat(base[...], 1, rhs)
    stats = [part[data:, :] for part in parts]
    norm_next = unpack_stat(stats[0], 0, rhs)
    bend = unpack_stat(stats[0], 1, rhs) + tree_sum(unpack_stat(stat, 2, rhs) for stat in stats)
    ratio = norm_next / norm
    size_next = norm_next / (bend - ratio * norm_next / size_now)
    back = ratio / size_now
    for i in range(total.shape[0]):
        lanes = slice(i * LANES, (i + 1) * LANES)
        first = right[:, lanes]
        now = left[:, lanes]
        solution[:, lanes] = size_now * first + size_next * (now + ratio * first)
        image = noise[:, lanes] * now + total[i] + back * (first - now)
        residual[:, lanes] = now - size_next * image


def shape_of(*shape):
    return jax.ShapeDtypeStruct(shape, F32)


def on_device(n, right_sides, nugget, cov_blocks, block_rows, block_cols, block_count):
    rhs, width = right_sides.shape
    slots, tile_size = cov_blocks.shape[2:4]
    per = width // n // LANES
    data = per * rhs
    size = data + 8
    noise = nugget.reshape(1, width)
    index = (block_rows, block_cols, block_count)
    pair = pltpu.VMEM((width // tile_size, 2 * rhs, tile_size), BF16)
    total = pltpu.VMEM((width // LANES, rhs, LANES), F32)
    index_scratch = [pltpu.SMEM(item.shape, item.dtype) for item in index[:2]]
    index_sems = pltpu.SemaphoreType.DMA((2,))
    vmem = pl.BlockSpec(memory_space=pltpu.VMEM)
    any_spec = pl.BlockSpec(memory_space=pl.ANY)
    smem = pl.BlockSpec(memory_space=pltpu.SMEM)
    hbm = pl.BlockSpec(memory_space=pltpu.HBM)
    params = pltpu.CompilerParams(vmem_limit_bytes=16 * 1024 * 1024)
    cost = pl.CostEstimate(flops=4 * rhs * slots * tile_size * tile_size, transcendentals=0,
                           bytes_accessed=2 * slots * tile_size * tile_size)
    field = shape_of(rhs, width)
    plain = shape_of(data, LANES)
    tile = shape_of(8, LANES)
    payload = shape_of(size, LANES)

    def call(kernel, name, specs, outs, scratch, args, heavy=False):
        return pl.pallas_call(
            kernel,
            in_specs=specs,
            out_specs=jax.tree.map(lambda _: vmem, outs),
            out_shape=outs,
            scratch_shapes=scratch,
            compiler_params=params,
            cost_estimate=cost if heavy else None,
            name=name,
        )(*args)

    in_hbm = functools.partial(pltpu.with_memory_space_constraint, memory_space=pltpu.HBM)
    held = from_diagonal(right_sides, n)
    out = call(
        functools.partial(mirror_first_kernel, n, per), "mirror_first",
        [hbm] * 2 + [smem] + [hbm] * 2,
        [plain] * n + [jax.ShapeDtypeStruct(cov_blocks.shape[2:], cov_blocks.dtype)],
        index_scratch + [pltpu.VMEM((rhs, width), F32), pair, total, index_sems,
                         pltpu.SemaphoreType.DMA, pltpu.SemaphoreType.DMA((slots // GROUP,))],
        (*map(in_hbm, index[:2]), block_count, in_hbm(right_sides), in_hbm(cov_blocks)), True)
    mirror, blocks = to_owners(out[:n], "row", n), out[n]

    out = call(
        functools.partial(direct_first_kernel, n, per), "direct_first",
        [any_spec] * 2 + [smem] + [vmem] * (n + 2),
        [plain] * n + [tile, field],
        index_scratch + [pair, total, index_sems],
        (*index, *held, noise, blocks), True)
    direct, stats, far = to_owners(out[:n], "col", n), to_all(out[n], "row", n), out[n + 1]

    summed = call(sum_kernel, "sum_first", [vmem] * n, plain, [], mirror)
    other = transposed(summed, n)
    near, finished = call(
        functools.partial(combine_first_kernel, n, per), "combine_first",
        [vmem] * (2 * n + 3), [payload, plain], [],
        (right_sides, noise, other, *direct, *stats))
    near_parts = to_all(near, "col", n)
    far_parts = to_all(transposed(finished, n), "row", n)

    out = call(
        functools.partial(mirror_second_kernel, n, per), "mirror_second",
        [any_spec] * 2 + [smem] + [vmem] * (n + 2),
        [plain] * n + [field, tile],
        index_scratch + [pair, total, index_sems],
        (*index, right_sides, *near_parts, blocks), True)
    mirror, left, base = to_owners(out[:n], "row", n), out[n], out[n + 1]

    out = call(
        functools.partial(direct_second_kernel, n, per), "direct_second",
        [any_spec] * 2 + [smem] + [vmem] * (n + 5),
        [plain] * n + [tile],
        index_scratch + [pair, total, index_sems],
        (*index, far, left, noise, base, *far_parts, blocks), True)
    direct, stats = to_owners(out[:n], "col", n), to_all(out[n], "row", n)

    summed = call(sum_kernel, "sum_second", [vmem] * n, plain, [], mirror)
    other = transposed(summed, n)
    part = call(functools.partial(combine_second_kernel, n, data), "combine_second",
                [vmem] * (2 * n + 1), payload, [], (other, *direct, *stats))
    parts = to_all(part, "col", n)

    return tuple(call(functools.partial(last_kernel, n, per), "last",
                      [vmem] * (n + 4), [field, field], [total],
                      (right_sides, left, noise, base, *parts)))


def solution(mesh):
    n = mesh.shape["row"]
    assert n == mesh.shape["col"] and n & (n - 1) == 0
    placed = (
        P(None, ("groups", "row")),
        P(("groups", "row")),
        P(("groups", "row"), "col", None, None, None),
        P(("groups", "row"), "col", None),
        P(("groups", "row"), "col", None),
        P(("groups", "row"), "col"),
    )
    return jax.shard_map(
        functools.partial(on_device, n),
        mesh=mesh,
        in_specs=placed,
        out_specs=(P(None, ("groups", "row")), P(None, ("groups", "row"))),
        check_vma=False,
    )
```

```python
import functools

import jax
import jax.numpy as jnp
from jax import lax
from jax.experimental import pallas as pl
from jax.experimental.pallas import tpu as pltpu
from jax.sharding import PartitionSpec as P

ITERS = 2
LANES = 128
GROUP = 8
BF16 = jnp.bfloat16
F32 = jnp.float32


def swapped(values, axis):
    return lax.all_to_all(values, axis, 0, 0)


def transposed(value, n):
    pairs = [(r * n + c, c * n + r) for r in range(n) for c in range(n)]
    return lax.ppermute(value, ("row", "col"), pairs)


def from_diagonal(value, n):
    held = [value]
    for o in range(1, n):
        pairs = [(c * n + c, (c ^ o) * n + c) for c in range(n)]
        held.append(lax.ppermute(value, ("row", "col"), pairs))
    return held


def load_pair(dst, tile, value):
    rhs = value.shape[0]
    high = value.astype(BF16)
    dst[tile, :rhs, :] = high
    dst[tile, rhs:, :] = (value - high.astype(F32)).astype(BF16)


def product(pair, block, contract):
    both = lax.dot_general(pair, block, (((1,), (contract,)), ((), ())), preferred_element_type=F32)
    rhs = both.shape[0] // 2
    return both[:rhs] + both[rhs:]


def pack_stats(columns, rhs):
    lane = lax.broadcasted_iota(jnp.int32, (8, LANES), 1)
    tile = jnp.zeros((8, LANES), F32)
    groups = rhs // 8
    for i, column in enumerate(columns):
        for g in range(groups):
            tile = jnp.where(lane == i * groups + g, column[g * 8:(g + 1) * 8], tile)
    return tile


def unpack_stat(tile, i, rhs):
    groups = rhs // 8
    return jnp.concatenate([tile[:, i * groups + g:i * groups + g + 1] for g in range(groups)], axis=0)


def accumulate(total, tile, value):
    width = value.shape[1] // LANES
    for part in range(width):
        total[tile * width + part] += value[:, part * LANES:(part + 1) * LANES]


def add_blocks(blocks, slot_rows, slot_cols, live, pairs, total, mirror, ready=None):
    read, write, contract = (slot_rows, slot_cols, 0) if mirror else (slot_cols, slot_rows, 1)

    def body(step, carry):
        if ready is not None:
            ready(step)
        values = []
        for g in range(GROUP):
            slot = step * GROUP + g
            value = product(pairs[read[0, 0, slot]], blocks[slot], contract)
            values.append((write[0, 0, slot], jnp.where(slot < live, value, 0.0)))
        for tile, value in values:
            accumulate(total, tile, value)
        return carry

    lax.fori_loop(0, (live + GROUP - 1) // GROUP, body, 0)


def write_chunks(out, total, per, rhs):
    for j in range(out.shape[0]):
        for i in range(per):
            out[j, i * rhs:(i + 1) * rhs, :] = total[j * per + i]


def image_part(parts, i, per, rhs):
    return parts[i // per, (i % per) * rhs:(i % per + 1) * rhs, :]


def row_sums(value):
    return jnp.sum(value, axis=1, keepdims=True)


def cross_sums(total, value):
    rhs = value.shape[0]
    cross = jnp.zeros((rhs, LANES), F32)
    for i in range(total.shape[0]):
        cross += total[i] * value[:, i * LANES:(i + 1) * LANES]
    return row_sums(cross)


def fetch_index(sources, targets, sems):
    copies = [pltpu.make_async_copy(s, t, sems.at[i]) for i, (s, t) in enumerate(zip(sources, targets))]
    for copy in copies:
        copy.start()
    return copies


def mirror_first_kernel(per, *refs):
    rows_hbm, cols_hbm, count, right_hbm, cov, out, blocks = refs[:7]
    slot_rows, slot_cols, right, pairs, total, index_sems, right_sem, block_sems = refs[7:]
    slots, tile_size = blocks.shape[:2]
    rhs = right.shape[0]

    def block_copy(i):
        part = pl.ds(i * GROUP, GROUP)
        return pltpu.make_async_copy(cov.at[0, 0, part], blocks.at[part], block_sems.at[i])

    copies = fetch_index((rows_hbm, cols_hbm), (slot_rows, slot_cols), index_sems)
    load = pltpu.make_async_copy(right_hbm, right, right_sem)
    load.start()
    live = count[0, 0]
    for i in range(slots // GROUP):
        @pl.when(i * GROUP < live)
        def _():
            block_copy(i).start()
    total[...] = jnp.zeros_like(total)
    for copy in copies:
        copy.wait()
    load.wait()
    for tile in range(right.shape[1] // tile_size):
        load_pair(pairs, tile, right[:, tile * tile_size:(tile + 1) * tile_size])
    add_blocks(blocks, slot_rows, slot_cols, live, pairs, total, True, lambda i: block_copy(i).wait())
    write_chunks(out, total, per, rhs)


def direct_first_kernel(n, per, *refs):
    rows_any, cols_any, count, noise, blocks = refs[:5]
    held, (out, far), scratch = refs[5:5 + n], refs[5 + n:7 + n], refs[7 + n:]
    slot_rows, slot_cols, pairs, total, index_sems = scratch
    tile_size = blocks.shape[1]
    rhs, width = far.shape
    copies = fetch_index((rows_any, cols_any), (slot_rows, slot_cols), index_sems)
    offset = lax.axis_index("row") ^ lax.axis_index("col")
    for o in range(n):
        @pl.when(offset == o)
        def _():
            for tile in range(width // tile_size):
                value = held[o][:, tile * tile_size:(tile + 1) * tile_size]
                load_pair(pairs, tile, value)
                far[:, tile * tile_size:(tile + 1) * tile_size] = value
    total[...] = jnp.zeros_like(total)
    for copy in copies:
        copy.wait()
    add_blocks(blocks, slot_rows, slot_cols, count[0, 0], pairs, total, False)
    write_chunks(out, total, per, rhs)
    right = held[0][...]
    square = right * right
    share = 1.0 / n
    norm = share * row_sums(square)
    bend = share * row_sums(square * noise[...]) + 2.0 * cross_sums(total, right)
    tile = pack_stats([norm, bend], rhs)
    for j in range(n):
        out[j, per * rhs:, :] = tile


def sum_kernel(parts, *outs):
    value = jnp.sum(parts[...], axis=0)
    first = 0
    for out in outs:
        out[...] = value[first:first + out.shape[0]]
        first += out.shape[0]


def combine_first_kernel(n, per, right, noise, other, direct, near, finished, stat):
    rhs = right.shape[0]
    data = per * rhs
    width = per * LANES
    value = jnp.sum(direct[...], axis=0)
    stat[...] = value[data:]
    finished[...] = value[:data] + other[...]
    me = lax.axis_index("col")
    for k in range(n):
        @pl.when(me == k)
        def _():
            for i in range(per):
                lanes = slice(k * width + i * LANES, k * width + (i + 1) * LANES)
                finished[i * rhs:(i + 1) * rhs, :] += right[:, lanes] * noise[:, lanes]
    for j in range(n):
        near[j] = finished[...]


def repeat_kernel(n, chunk, stat, out):
    data = chunk.shape[0]
    for j in range(n):
        out[j, :data, :] = chunk[...]
        out[j, data:, :] = stat[...]


def second_kernel(per, *refs):
    rows_any, cols_any, count, right, far, noise, near_parts, far_parts, blocks = refs[:9]
    direct, mirror, left, base = refs[9:13]
    slot_rows, slot_cols, near_pairs, far_pairs, direct_total, mirror_total, index_sems = refs[13:]
    copies = fetch_index((rows_any, cols_any), (slot_rows, slot_cols), index_sems)
    tile_size = blocks.shape[1]
    pieces = tile_size // LANES
    rhs, width = right.shape
    data = per * rhs
    stat = jnp.sum(far_parts[:, data:, :], axis=0)
    base[...] = stat
    size_now = unpack_stat(stat, 0, rhs) / unpack_stat(stat, 1, rhs)
    for tile in range(width // tile_size):
        lanes = slice(tile * tile_size, (tile + 1) * tile_size)
        image = [image_part(near_parts, tile * pieces + i, per, rhs) for i in range(pieces)]
        value = right[:, lanes] - size_now * jnp.concatenate(image, axis=1)
        left[:, lanes] = value
        load_pair(near_pairs, tile, value)
        image = [image_part(far_parts, tile * pieces + i, per, rhs) for i in range(pieces)]
        load_pair(far_pairs, tile, far[:, lanes] - size_now * jnp.concatenate(image, axis=1))
    direct_total[...] = jnp.zeros_like(direct_total)
    mirror_total[...] = jnp.zeros_like(mirror_total)
    for copy in copies:
        copy.wait()
    live = count[0, 0]
    add_blocks(blocks, slot_rows, slot_cols, live, near_pairs, mirror_total, True)
    add_blocks(blocks, slot_rows, slot_cols, live, far_pairs, direct_total, False)
    write_chunks(mirror, mirror_total, per, rhs)
    write_chunks(direct, direct_total, per, rhs)
    value = left[...]
    square = value * value
    cross = 2.0 * cross_sums(direct_total, value)
    tile = pack_stats([row_sums(square), row_sums(square * noise[...]), cross], rhs)
    for j in range(mirror.shape[0]):
        mirror[j, data:, :] = tile


def combine_second_kernel(n, other, stat, direct, out):
    data = other.shape[0]
    value = jnp.sum(direct[...], axis=0) + other[...]
    for j in range(n):
        out[j, :data, :] = value
        out[j, data:, :] = stat[...]


def last_kernel(per, right, left, noise, base, parts, solution, residual):
    rhs, width = right.shape
    data = per * rhs
    norm = unpack_stat(base[...], 0, rhs)
    size_now = norm / unpack_stat(base[...], 1, rhs)
    norm_next = unpack_stat(parts[0, data:, :], 0, rhs)
    cross = unpack_stat(jnp.sum(parts[:, data:, :], axis=0), 2, rhs)
    bend = unpack_stat(parts[0, data:, :], 1, rhs) + cross
    ratio = norm_next / norm
    size_next = norm_next / (bend - ratio * norm_next / size_now)
    back = ratio / size_now
    for i in range(width // LANES):
        lanes = slice(i * LANES, (i + 1) * LANES)
        first = right[:, lanes]
        now = left[:, lanes]
        solution[:, lanes] = size_now * first + size_next * (now + ratio * first)
        image = noise[:, lanes] * now + image_part(parts, i, per, rhs) + back * (first - now)
        residual[:, lanes] = now - size_next * image


def shape_of(*shape):
    return jax.ShapeDtypeStruct(shape, F32)


def on_device(n, right_sides, nugget, cov_blocks, block_rows, block_cols, block_count):
    rhs, width = right_sides.shape
    slots, tile_size = cov_blocks.shape[2:4]
    per = width // n // LANES
    data = per * rhs
    size = data + 8
    noise = nugget.reshape(1, width)
    index = (block_rows, block_cols, block_count)
    pair = pltpu.VMEM((width // tile_size, 2 * rhs, tile_size), BF16)
    total = pltpu.VMEM((width // LANES, rhs, LANES), F32)
    index_scratch = [pltpu.SMEM(item.shape, item.dtype) for item in index[:2]]
    index_sems = pltpu.SemaphoreType.DMA((2,))
    vmem = pl.BlockSpec(memory_space=pltpu.VMEM)
    any_spec = pl.BlockSpec(memory_space=pl.ANY)
    smem = pl.BlockSpec(memory_space=pltpu.SMEM)
    hbm = pl.BlockSpec(memory_space=pltpu.HBM)
    params = pltpu.CompilerParams(vmem_limit_bytes=16 * 1024 * 1024)
    cost = pl.CostEstimate(flops=4 * rhs * slots * tile_size * tile_size, transcendentals=0,
                           bytes_accessed=2 * slots * tile_size * tile_size)
    field = shape_of(rhs, width)
    chunk = shape_of(data, LANES)
    tile = shape_of(8, LANES)
    chunks = shape_of(n, data, LANES)
    loaded = shape_of(n, size, LANES)

    def call(kernel, name, specs, outs, scratch, args, heavy=False):
        return pl.pallas_call(
            kernel,
            in_specs=specs,
            out_specs=jax.tree.map(lambda _: vmem, outs),
            out_shape=outs,
            scratch_shapes=scratch,
            compiler_params=params,
            cost_estimate=cost if heavy else None,
            name=name,
        )(*args)

    in_hbm = functools.partial(pltpu.with_memory_space_constraint, memory_space=pltpu.HBM)
    held = from_diagonal(right_sides, n)
    mirror, blocks = call(
        functools.partial(mirror_first_kernel, per), "mirror_first",
        [hbm] * 2 + [smem] + [hbm] * 2,
        [chunks, jax.ShapeDtypeStruct(cov_blocks.shape[2:], cov_blocks.dtype)],
        index_scratch + [pltpu.VMEM((rhs, width), F32), pair, total, index_sems,
                         pltpu.SemaphoreType.DMA, pltpu.SemaphoreType.DMA((slots // GROUP,))],
        (*map(in_hbm, index[:2]), block_count, in_hbm(right_sides), in_hbm(cov_blocks)), True)
    summed, = call(sum_kernel, "sum_first", [vmem], [chunk], [], (swapped(mirror, "row"),))
    other = transposed(summed, n)
    direct, far = call(
        functools.partial(direct_first_kernel, n, per), "direct_first",
        [any_spec] * 2 + [smem] + [vmem] * (n + 2),
        [loaded, field],
        index_scratch + [pair, total, index_sems],
        (*index, noise, blocks, *held), True)
    near, finished, stat = call(
        functools.partial(combine_first_kernel, n, per), "combine_first",
        [vmem] * 4, [chunks, chunk, tile], [],
        (right_sides, noise, other, swapped(direct, "col")))
    near_parts = swapped(near, "col")
    repeated, = call(functools.partial(repeat_kernel, n), "repeat_far", [vmem] * 2, [loaded], [],
                     (transposed(finished, n), stat))
    far_parts = swapped(repeated, "row")

    direct, mirror, left, base = call(
        functools.partial(second_kernel, per), "both_second",
        [any_spec] * 2 + [smem] + [vmem] * 6,
        [chunks, loaded, field, tile],
        index_scratch + [pair, pair, total, total, index_sems],
        (*index, right_sides, far, noise, near_parts, far_parts, blocks), True)
    summed, stat = call(sum_kernel, "sum_second", [vmem], [chunk, tile], [], (swapped(mirror, "row"),))
    other = transposed(summed, n)
    part, = call(functools.partial(combine_second_kernel, n), "combine_second",
                 [vmem] * 3, [loaded], [], (other, stat, swapped(direct, "col")))
    return tuple(call(functools.partial(last_kernel, per), "last", [vmem] * 5, [field, field], [],
                      (right_sides, left, noise, base, swapped(part, "col"))))


def solution(mesh):
    n = mesh.shape["row"]
    assert n == mesh.shape["col"] and n & (n - 1) == 0
    placed = (
        P(None, ("groups", "row")),
        P(("groups", "row")),
        P(("groups", "row"), "col", None, None, None),
        P(("groups", "row"), "col", None),
        P(("groups", "row"), "col", None),
        P(("groups", "row"), "col"),
    )
    return jax.shard_map(
        functools.partial(on_device, n),
        mesh=mesh,
        in_specs=placed,
        out_specs=(P(None, ("groups", "row")), P(None, ("groups", "row"))),
        check_vma=False,
    )
```

```python
import functools

import jax
import jax.numpy as jnp
from jax import lax
from jax.experimental import pallas as pl
from jax.experimental.pallas import tpu as pltpu
from jax.sharding import PartitionSpec as P

ITERS = 2
LANES = 128
GROUP = 8
BF16 = jnp.bfloat16
F32 = jnp.float32


def shifted(value, axis, d, n):
    return lax.ppermute(value, axis, [(i, i ^ d) for i in range(n)])


def distances(n):
    return [d for d in range(n) if d > 1] + [1]


def hop(value, n, moves):
    pairs = [((c ^ s) * n + c, (c ^ t) * n + c) for c in range(n) for s, t in moves]
    return lax.ppermute(value, ("row", "col"), pairs)


def bits(n):
    return [1 << i for i in range(n.bit_length() - 1)]


def load_pair(dst, tile, value):
    rhs = value.shape[0]
    high = value.astype(BF16)
    dst[tile, :rhs, :] = high
    dst[tile, rhs:, :] = (value - high.astype(F32)).astype(BF16)


def product(pair, block, contract):
    both = lax.dot_general(pair, block, (((1,), (contract,)), ((), ())), preferred_element_type=F32)
    rhs = both.shape[0] // 2
    return both[:rhs] + both[rhs:]


def pack_stats(columns, rhs):
    lane = lax.broadcasted_iota(jnp.int32, (8, LANES), 1)
    tile = jnp.zeros((8, LANES), F32)
    groups = rhs // 8
    for i, column in enumerate(columns):
        for g in range(groups):
            tile = jnp.where(lane == i * groups + g, column[g * 8:(g + 1) * 8], tile)
    return tile


def unpack_stat(tile, i, rhs):
    groups = rhs // 8
    return jnp.concatenate([tile[:, i * groups + g:i * groups + g + 1] for g in range(groups)], axis=0)


def accumulate(total, tile, value):
    width = value.shape[1] // LANES
    for part in range(width):
        total[tile * width + part] += value[:, part * LANES:(part + 1) * LANES]


def add_blocks(blocks, slot_rows, slot_cols, live, pairs, total, mirror, ready=None):
    read, write, contract = (slot_rows, slot_cols, 0) if mirror else (slot_cols, slot_rows, 1)

    def body(step, carry):
        if ready is not None:
            ready(step)
        values = []
        for g in range(GROUP):
            slot = step * GROUP + g
            value = product(pairs[read[0, 0, slot]], blocks[slot], contract)
            values.append((write[0, 0, slot], jnp.where(slot < live, value, 0.0)))
        for tile, value in values:
            accumulate(total, tile, value)
        return carry

    lax.fori_loop(0, (live + GROUP - 1) // GROUP, body, 0)


def image_part(parts, me, i, per, rhs):
    rows = slice((i % per) * rhs, (i % per + 1) * rhs)
    value = parts[0][rows, :]
    for d in range(1, len(parts)):
        value = jnp.where(me ^ d == i // per, parts[d][rows, :], value)
    return value


def row_sums(value):
    return jnp.sum(value, axis=1, keepdims=True)


def cross_sums(total, value):
    rhs = value.shape[0]
    cross = jnp.zeros((rhs, LANES), F32)
    for i in range(total.shape[0]):
        cross += total[i] * value[:, i * LANES:(i + 1) * LANES]
    return row_sums(cross)


def tree_sum(values):
    values = list(values)
    while len(values) > 1:
        values = [a + b for a, b in zip(values[::2], values[1::2])]
    return values[0]


def fetch_index(sources, targets, sems):
    copies = [pltpu.make_async_copy(s, t, sems.at[i]) for i, (s, t) in enumerate(zip(sources, targets))]
    for copy in copies:
        copy.start()
    return copies


def mirror_first_kernel(rows_hbm, cols_hbm, count, right_hbm, cov, total, blocks, mark, *scratch):
    slot_rows, slot_cols, right, pairs, index_sems, right_sem, block_sems = scratch
    slots, tile_size = blocks.shape[:2]

    def block_copy(i):
        part = pl.ds(i * GROUP, GROUP)
        return pltpu.make_async_copy(cov.at[0, 0, part], blocks.at[part], block_sems.at[i])

    copies = fetch_index((rows_hbm, cols_hbm), (slot_rows, slot_cols), index_sems)
    load = pltpu.make_async_copy(right_hbm, right, right_sem)
    load.start()
    live = count[0, 0]
    for i in range(slots // GROUP):
        @pl.when(i * GROUP < live)
        def _():
            block_copy(i).start()
    total[...] = jnp.zeros_like(total)
    mark[...] = jnp.zeros_like(mark)
    load.wait()
    for tile in range(right.shape[1] // tile_size):
        load_pair(pairs, tile, right[:, tile * tile_size:(tile + 1) * tile_size])
    for copy in copies:
        copy.wait()
    add_blocks(blocks, slot_rows, slot_cols, live, pairs, total, True, lambda i: block_copy(i).wait())


def mirror_second_kernel(rows_any, cols_any, count, near, blocks, total, mark, *scratch):
    slot_rows, slot_cols, pairs, index_sems = scratch
    tile_size = blocks.shape[1]
    copies = fetch_index((rows_any, cols_any), (slot_rows, slot_cols), index_sems)
    total[...] = jnp.zeros_like(total)
    mark[...] = jnp.zeros_like(mark)
    for tile in range(near.shape[1] // tile_size):
        load_pair(pairs, tile, near[:, tile * tile_size:(tile + 1) * tile_size])
    for copy in copies:
        copy.wait()
    add_blocks(blocks, slot_rows, slot_cols, count[0, 0], pairs, total, True)


def direct_kernel(n, *refs):
    rows_any, cols_any, count, noise, blocks = refs[:5]
    held, (total, stat), scratch = refs[5:5 + n], refs[5 + n:7 + n], refs[7 + n:]
    slot_rows, slot_cols, pairs, index_sems = scratch
    tile_size = blocks.shape[1]
    near = held[0]
    rhs, width = near.shape
    copies = fetch_index((rows_any, cols_any), (slot_rows, slot_cols), index_sems)
    offset = lax.axis_index("row") ^ lax.axis_index("col")
    for o in range(n):
        @pl.when(offset == o)
        def _():
            for tile in range(width // tile_size):
                load_pair(pairs, tile, held[o][:, tile * tile_size:(tile + 1) * tile_size])
    total[...] = jnp.zeros_like(total)
    for copy in copies:
        copy.wait()
    add_blocks(blocks, slot_rows, slot_cols, count[0, 0], pairs, total, False)
    value = near[...]
    square = value * value
    share = 1.0 / n
    bend = share * row_sums(square * noise[...]) + 2.0 * cross_sums(total, value)
    stat[...] = pack_stats([share * row_sums(square), bend], rhs)


def add_kernel(one, two, out):
    out[...] = one[...] + two[...]


def pass_kernel(value, mark, out):
    out[...] = value[...]


def merge_kernel(n, direct, stat, held, arrived, *outs):
    per = direct.shape[0] // n
    rhs = direct.shape[1]
    me = lax.axis_index("col")
    diagonal = lax.axis_index("row") == me
    for d, out in enumerate(outs):
        first = (me ^ d) * per
        out[per * rhs:, :] = stat[...]

        @pl.when(diagonal)
        def _():
            for i in range(per):
                out[i * rhs:(i + 1) * rhs, :] = direct[first + i] + held[first + i] + arrived[first + i]

        @pl.when(jnp.logical_not(diagonal))
        def _():
            for i in range(per):
                out[i * rhs:(i + 1) * rhs, :] = direct[first + i]


def combine_kernel(n, near, noise, *refs):
    parts, (chunk, stat) = refs[:n], refs[n:]
    rhs = near.shape[0]
    data = chunk.shape[0]
    per = data // rhs
    value = tree_sum(ref[...] for ref in parts)
    chunk[...] = value[:data]
    stat[...] = value[data:]
    me = lax.axis_index("col")
    for k in range(n):
        @pl.when(me == k)
        def _():
            for i in range(per):
                lanes = slice((k * per + i) * LANES, (k * per + i + 1) * LANES)
                chunk[i * rhs:(i + 1) * rhs, :] += near[:, lanes] * noise[:, lanes]


def left_kernel(right, stat, *refs):
    parts, left = refs[:-1], refs[-1]
    rhs, width = right.shape
    per = parts[0].shape[0] // rhs
    me = lax.axis_index("col")
    size_now = unpack_stat(stat[...], 0, rhs) / unpack_stat(stat[...], 1, rhs)
    for i in range(width // LANES):
        lanes = slice(i * LANES, (i + 1) * LANES)
        left[:, lanes] = right[:, lanes] - size_now * image_part(parts, me, i, per, rhs)


def last_kernel(right, left, stat_now, stat_next, *refs):
    parts, (solution, residual) = refs[:-2], refs[-2:]
    rhs, width = right.shape
    per = parts[0].shape[0] // rhs
    me = lax.axis_index("col")
    norm = unpack_stat(stat_now[...], 0, rhs)
    norm_next = unpack_stat(stat_next[...], 0, rhs)
    size_now = norm / unpack_stat(stat_now[...], 1, rhs)
    ratio = norm_next / norm
    size_next = norm_next / (unpack_stat(stat_next[...], 1, rhs) - ratio * norm_next / size_now)
    back = ratio / size_now
    for i in range(width // LANES):
        lanes = slice(i * LANES, (i + 1) * LANES)
        first = right[:, lanes]
        now = left[:, lanes]
        solution[:, lanes] = size_now * first + size_next * (now + ratio * first)
        image = image_part(parts, me, i, per, rhs) + back * (first - now)
        residual[:, lanes] = now - size_next * image


def shape_of(*shape):
    return jax.ShapeDtypeStruct(shape, F32)


def on_device(n, right_sides, nugget, cov_blocks, block_rows, block_cols, block_count):
    rhs, width = right_sides.shape
    slots, tile_size = cov_blocks.shape[2:4]
    per = width // n // LANES
    data = per * rhs
    size = data + 8
    noise = nugget.reshape(1, width)
    index = (block_rows, block_cols, block_count)
    pair = pltpu.VMEM((width // tile_size, 2 * rhs, tile_size), BF16)
    index_scratch = [pltpu.SMEM(item.shape, item.dtype) for item in index[:2]]
    index_sems = pltpu.SemaphoreType.DMA((2,))
    vmem = pl.BlockSpec(memory_space=pltpu.VMEM)
    any_spec = pl.BlockSpec(memory_space=pl.ANY)
    smem = pl.BlockSpec(memory_space=pltpu.SMEM)
    hbm = pl.BlockSpec(memory_space=pltpu.HBM)
    params = pltpu.CompilerParams(vmem_limit_bytes=16 * 1024 * 1024)
    cost = pl.CostEstimate(flops=4 * rhs * slots * tile_size * tile_size, transcendentals=0,
                           bytes_accessed=2 * slots * tile_size * tile_size)
    field = shape_of(rhs, width)
    total = shape_of(width // LANES, rhs, LANES)
    chunk = shape_of(data, LANES)
    tile = shape_of(8, LANES)
    loaded = shape_of(size, LANES)

    def call(kernel, name, specs, outs, scratch, args, heavy=False):
        return pl.pallas_call(
            kernel,
            in_specs=specs,
            out_specs=jax.tree.map(lambda _: vmem, outs),
            out_shape=outs,
            scratch_shapes=scratch,
            compiler_params=params,
            cost_estimate=cost if heavy else None,
            name=name,
        )(*args)

    in_hbm = functools.partial(pltpu.with_memory_space_constraint, memory_space=pltpu.HBM)

    def image_of(value, mirrored):
        held = [value] + [None] * (n - 1)
        for o in distances(n):
            if o & (o - 1) == 0:
                held[o] = hop(value, n, [(0, o)])
        mirror, blocks, mark = mirrored(value)
        for o in range(n):
            if held[o] is None:
                parent = held[o & (o - 1)]
                passed, = call(pass_kernel, "pass_on", [vmem] * 2, [field], [], (parent, mark))
                held[o] = hop(passed, n, [(o & (o - 1), o)])
        for b in bits(n):
            arrived = hop(mirror, n, [(o, o ^ b) for o in range(n) if o & -o == b])
            if 2 * b < n:
                mirror, = call(add_kernel, "add_mirror", [vmem] * 2, [total], [], (mirror, arrived))
        direct, stat = call(
            functools.partial(direct_kernel, n), "direct",
            [any_spec] * 2 + [smem] + [vmem] * (n + 2),
            [total, tile], index_scratch + [pair, index_sems],
            (*index, noise, blocks, *held), True)
        merged = call(functools.partial(merge_kernel, n), "merge", [vmem] * 4, [loaded] * n, [],
                      (direct, stat, mirror, arrived))
        parts = [merged[0]] + [None] * (n - 1)
        for d in distances(n):
            parts[d] = shifted(merged[d], "col", d, n)
        own, stat = call(functools.partial(combine_kernel, n), "combine", [vmem] * (n + 2), [chunk, tile], [],
                         (value, noise, *parts))
        parts = [own] + [None] * (n - 1)
        for d in distances(n):
            parts[d] = shifted(own, "col", d, n)
        for b in bits(n):
            stat, = call(add_kernel, "add_stat", [vmem] * 2, [tile], [], (stat, shifted(stat, "row", b, n)))
        return parts, stat, blocks

    def mirror_first(value):
        return call(
            mirror_first_kernel, "mirror_first", [hbm] * 2 + [smem] + [hbm] * 2,
            [total, jax.ShapeDtypeStruct(cov_blocks.shape[2:], cov_blocks.dtype), tile],
            index_scratch + [pltpu.VMEM((rhs, width), F32), pair, index_sems,
                             pltpu.SemaphoreType.DMA, pltpu.SemaphoreType.DMA((slots // GROUP,))],
            (*map(in_hbm, index[:2]), block_count, in_hbm(value), in_hbm(cov_blocks)), True)

    parts, stat_now, blocks = image_of(right_sides, mirror_first)
    left, = call(left_kernel, "left", [vmem] * (n + 2), [field], [], (right_sides, stat_now, *parts))

    def mirror_second(value):
        mirror, mark = call(
            mirror_second_kernel, "mirror_second", [any_spec] * 2 + [smem] + [vmem] * 2,
            [total, tile], index_scratch + [pair, index_sems], (*index, value, blocks), True)
        return mirror, blocks, mark

    parts, stat_next, _ = image_of(left, mirror_second)
    return tuple(call(last_kernel, "last", [vmem] * (n + 4), [field, field], [],
                      (right_sides, left, stat_now, stat_next, *parts)))


def solution(mesh):
    n = mesh.shape["row"]
    assert n == mesh.shape["col"] and n & (n - 1) == 0
    placed = (
        P(None, ("groups", "row")),
        P(("groups", "row")),
        P(("groups", "row"), "col", None, None, None),
        P(("groups", "row"), "col", None),
        P(("groups", "row"), "col", None),
        P(("groups", "row"), "col"),
    )
    return jax.shard_map(
        functools.partial(on_device, n),
        mesh=mesh,
        in_specs=placed,
        out_specs=(P(None, ("groups", "row")), P(None, ("groups", "row"))),
        check_vma=False,
    )
```

```python
import functools

import jax
import jax.numpy as jnp
from jax import lax
from jax.experimental import pallas as pl
from jax.experimental.pallas import tpu as pltpu
from jax.sharding import PartitionSpec as P

ITERS = 2
LANES = 128
GROUP = 8
BF16 = jnp.bfloat16
F32 = jnp.float32


def shifted(value, axis, d, n):
    return lax.ppermute(value, axis, [(i, i ^ d) for i in range(n)])


def distances(n):
    return [d for d in range(n) if d > 1] + [1]


def moved(value, n, target):
    pairs = [(r * n + c, target(r, c)) for r in range(n) for c in range(n)]
    return lax.ppermute(value, ("row", "col"), [(s, t[0] * n + t[1]) for s, t in pairs])


def far_target(j):
    def target(r, c):
        d = r ^ c
        return (c ^ 2 * j, r) if d ^ 2 * j >= 2 else (c ^ (d & 1), c)

    return target


def far_source(j, n):
    back = {far_target(j)(r, c): (r, c) for r in range(n) for c in range(n)}
    return lambda r, c: back[r, c]


def spread_target(b):
    return lambda r, c: (r ^ b, c) if (r ^ c) % b == 0 else (r, c)


def bits(n):
    return [1 << i for i in range(n.bit_length() - 1)]


def load_pair(dst, tile, value):
    rhs = value.shape[0]
    high = value.astype(BF16)
    dst[tile, :rhs, :] = high
    dst[tile, rhs:, :] = (value - high.astype(F32)).astype(BF16)


def product(pair, block, contract):
    both = lax.dot_general(pair, block, (((1,), (contract,)), ((), ())), preferred_element_type=F32)
    rhs = both.shape[0] // 2
    return both[:rhs] + both[rhs:]


def pack_stats(columns, rhs):
    lane = lax.broadcasted_iota(jnp.int32, (8, LANES), 1)
    tile = jnp.zeros((8, LANES), F32)
    groups = rhs // 8
    for i, column in enumerate(columns):
        for g in range(groups):
            tile = jnp.where(lane == i * groups + g, column[g * 8:(g + 1) * 8], tile)
    return tile


def unpack_stat(tile, i, rhs):
    groups = rhs // 8
    return jnp.concatenate([tile[:, i * groups + g:i * groups + g + 1] for g in range(groups)], axis=0)


def accumulate(total, tile, value):
    width = value.shape[1] // LANES
    for part in range(width):
        total[tile * width + part] += value[:, part * LANES:(part + 1) * LANES]


def add_blocks(blocks, slot_rows, slot_cols, live, pairs, total, mirror, ready=None):
    read, write, contract = (slot_rows, slot_cols, 0) if mirror else (slot_cols, slot_rows, 1)

    def body(step, carry):
        if ready is not None:
            ready(step)
        values = []
        for g in range(GROUP):
            slot = step * GROUP + g
            value = product(pairs[read[0, 0, slot]], blocks[slot], contract)
            values.append((write[0, 0, slot], jnp.where(slot < live, value, 0.0)))
        for tile, value in values:
            accumulate(total, tile, value)
        return carry

    lax.fori_loop(0, (live + GROUP - 1) // GROUP, body, 0)


def image_part(parts, me, i, per, rhs):
    rows = slice((i % per) * rhs, (i % per + 1) * rhs)
    value = parts[0][rows, :]
    for d, part in zip(distances(len(parts)), parts[1:]):
        value = jnp.where(me ^ d == i // per, part[rows, :], value)
    return value


def row_sums(value):
    return jnp.sum(value, axis=1, keepdims=True)


def cross_sums(total, value):
    rhs = value.shape[0]
    cross = jnp.zeros((rhs, LANES), F32)
    for i in range(total.shape[0]):
        cross += total[i] * value[:, i * LANES:(i + 1) * LANES]
    return row_sums(cross)


def tree_sum(values):
    values = list(values)
    while len(values) > 1:
        values = [a + b for a, b in zip(values[::2], values[1::2])]
    return values[0]


def fetch_index(sources, targets, sems):
    copies = [pltpu.make_async_copy(s, t, sems.at[i]) for i, (s, t) in enumerate(zip(sources, targets))]
    for copy in copies:
        copy.start()
    return copies


def mirror_first_kernel(rows_hbm, cols_hbm, count, right_hbm, cov, total, blocks, *scratch):
    slot_rows, slot_cols, right, pairs, index_sems, right_sem, block_sems = scratch
    slots, tile_size = blocks.shape[:2]

    def block_copy(i):
        part = pl.ds(i * GROUP, GROUP)
        return pltpu.make_async_copy(cov.at[0, 0, part], blocks.at[part], block_sems.at[i])

    copies = fetch_index((rows_hbm, cols_hbm), (slot_rows, slot_cols), index_sems)
    load = pltpu.make_async_copy(right_hbm, right, right_sem)
    load.start()
    live = count[0, 0]
    for i in range(slots // GROUP):
        @pl.when(i * GROUP < live)
        def _():
            block_copy(i).start()
    total[...] = jnp.zeros_like(total)
    load.wait()
    for tile in range(right.shape[1] // tile_size):
        load_pair(pairs, tile, right[:, tile * tile_size:(tile + 1) * tile_size])
    for copy in copies:
        copy.wait()
    add_blocks(blocks, slot_rows, slot_cols, live, pairs, total, True, lambda i: block_copy(i).wait())


def mirror_second_kernel(rows_any, cols_any, count, near, blocks, total, *scratch):
    slot_rows, slot_cols, pairs, index_sems = scratch
    tile_size = blocks.shape[1]
    copies = fetch_index((rows_any, cols_any), (slot_rows, slot_cols), index_sems)
    total[...] = jnp.zeros_like(total)
    for tile in range(near.shape[1] // tile_size):
        load_pair(pairs, tile, near[:, tile * tile_size:(tile + 1) * tile_size])
    for copy in copies:
        copy.wait()
    add_blocks(blocks, slot_rows, slot_cols, count[0, 0], pairs, total, True)


def finish_direct(total, near, noise, stat, n):
    value = near[...]
    rhs = value.shape[0]
    square = value * value
    share = 1.0 / n
    bend = share * row_sums(square * noise[...]) + 2.0 * cross_sums(total, value)
    stat[...] = pack_stats([share * row_sums(square), bend], rhs)


def direct_first_kernel(n, rows_any, cols_any, count, noise, blocks, near, current, twin, mark, total, stat, far, *scratch):
    slot_rows, slot_cols, pairs, index_sems = scratch
    tile_size = blocks.shape[1]
    pieces = tile_size // LANES
    copies = fetch_index((rows_any, cols_any), (slot_rows, slot_cols), index_sems)
    odd = (lax.axis_index("row") ^ lax.axis_index("col")) & 1
    for o, source in enumerate((current, twin)):
        @pl.when(odd == o)
        def _():
            for tile in range(near.shape[1] // tile_size):
                value = source[:, tile * tile_size:(tile + 1) * tile_size]
                load_pair(pairs, tile, value)
                for i in range(pieces):
                    far[tile * pieces + i] = value[:, i * LANES:(i + 1) * LANES]
    total[...] = jnp.zeros_like(total)
    for copy in copies:
        copy.wait()
    add_blocks(blocks, slot_rows, slot_cols, count[0, 0], pairs, total, False)
    finish_direct(total, near, noise, stat, n)


def direct_second_kernel(n, rows_any, cols_any, count, noise, blocks, near, held, twin, mark, total, stat, *scratch):
    slot_rows, slot_cols, pairs, index_sems = scratch
    tile_size = blocks.shape[1]
    pieces = tile_size // LANES
    per = held.shape[0] // n
    copies = fetch_index((rows_any, cols_any), (slot_rows, slot_cols), index_sems)
    row = lax.axis_index("row")
    offset = row ^ lax.axis_index("col")
    for tile in range(near.shape[1] // tile_size):
        value = []
        for i in range(tile * pieces, (tile + 1) * pieces):
            own = jnp.logical_or(offset == 0, jnp.logical_and(offset >= 2, ((i // per) ^ row) & 1 == 0))
            value.append(jnp.where(own, held[i], twin[i]))
        load_pair(pairs, tile, jnp.concatenate(value, axis=1))
    total[...] = jnp.zeros_like(total)
    for copy in copies:
        copy.wait()
    add_blocks(blocks, slot_rows, slot_cols, count[0, 0], pairs, total, False)
    finish_direct(total, near, noise, stat, n)


def add_kernel(one, two, *refs):
    refs[-1][...] = one[...] + two[...]


def pick_kernel(b, current, arrived, mark, out):
    there = (lax.axis_index("row") ^ lax.axis_index("col")) & b
    out[...] = jnp.where(there != 0, arrived[...], current[...])


def split_kernel(n, mirror, twin, *outs):
    per = mirror.shape[0] // n
    rhs = mirror.shape[1]
    row = lax.axis_index("row")
    for j, out in enumerate(outs):
        first = (row ^ 2 * j) * per
        for i in range(per):
            out[i * rhs:(i + 1) * rhs, :] = mirror[first + i] + twin[first + i]


def merge_kernel(n, direct, mirror, twin, stat, *outs):
    per = direct.shape[0] // n
    rhs = direct.shape[1]
    me = lax.axis_index("col")
    diagonal = lax.axis_index("row") == me
    outs[n][...] = stat[...]
    for d, out in zip([0] + distances(n), outs):
        first = (me ^ d) * per

        @pl.when(diagonal)
        def _():
            for i in range(per):
                out[i * rhs:(i + 1) * rhs, :] = direct[first + i] + (mirror[first + i] + twin[first + i])

        @pl.when(jnp.logical_not(diagonal))
        def _():
            for i in range(per):
                out[i * rhs:(i + 1) * rhs, :] = direct[first + i]


def combine_kernel(n, near, noise, stat, *refs):
    parts, others, chunk = refs[:n], refs[n:-1], refs[-1]
    rhs = near.shape[0]
    data = parts[0].shape[0]
    per = data // rhs
    me = lax.axis_index("col")
    group = (lax.axis_index("row") ^ me) // 2
    value = tree_sum(ref[...] for ref in parts)
    for j, other in enumerate(others):
        value += jnp.where(group == j, 0.0, other[...])
    chunk[:data, :] = value
    chunk[data:, :] = stat[...]
    for k in range(n):
        @pl.when(me == k)
        def _():
            for i in range(per):
                lanes = slice((k * per + i) * LANES, (k * per + i + 1) * LANES)
                chunk[i * rhs:(i + 1) * rhs, :] += near[:, lanes] * noise[:, lanes]


def left_kernel(right, *refs):
    parts, (left, stat) = refs[:-2], refs[-2:]
    rhs, width = right.shape
    data = parts[0].shape[0] - 8
    per = data // rhs
    me = lax.axis_index("col")
    both = tree_sum(part[data:, :] for part in parts)
    stat[...] = both
    size_now = unpack_stat(both, 0, rhs) / unpack_stat(both, 1, rhs)
    for i in range(width // LANES):
        lanes = slice(i * LANES, (i + 1) * LANES)
        left[:, lanes] = right[:, lanes] - size_now * image_part(parts, me, i, per, rhs)


def held_kernel(n, left, stat, far, mark, *refs):
    parts, held = refs[:-1], refs[-1]
    rhs = left.shape[0]
    per = held.shape[0] // n
    row = lax.axis_index("row")
    diagonal = (row ^ lax.axis_index("col")) < 2
    size_now = unpack_stat(stat[...], 0, rhs) / unpack_stat(stat[...], 1, rhs)

    @pl.when(diagonal)
    def _():
        for i in range(held.shape[0]):
            held[i] = left[:, i * LANES:(i + 1) * LANES]

    @pl.when(jnp.logical_not(diagonal))
    def _():
        for j, part in enumerate(parts):
            first = (row ^ 2 * j) * per
            for i in range(per):
                held[first + i] = far[first + i] - size_now * part[i * rhs:(i + 1) * rhs, :]


def last_kernel(right, left, stat_now, *refs):
    parts, (solution, residual) = refs[:-2], refs[-2:]
    rhs, width = right.shape
    data = parts[0].shape[0] - 8
    per = data // rhs
    me = lax.axis_index("col")
    both = tree_sum(part[data:, :] for part in parts)
    norm = unpack_stat(stat_now[...], 0, rhs)
    norm_next = unpack_stat(both, 0, rhs)
    size_now = norm / unpack_stat(stat_now[...], 1, rhs)
    ratio = norm_next / norm
    size_next = norm_next / (unpack_stat(both, 1, rhs) - ratio * norm_next / size_now)
    back = ratio / size_now
    for i in range(width // LANES):
        lanes = slice(i * LANES, (i + 1) * LANES)
        first = right[:, lanes]
        now = left[:, lanes]
        solution[:, lanes] = size_now * first + size_next * (now + ratio * first)
        image = image_part(parts, me, i, per, rhs) + back * (first - now)
        residual[:, lanes] = now - size_next * image


def shape_of(*shape):
    return jax.ShapeDtypeStruct(shape, F32)


def on_device(n, right_sides, nugget, cov_blocks, block_rows, block_cols, block_count):
    rhs, width = right_sides.shape
    slots, tile_size = cov_blocks.shape[2:4]
    per = width // n // LANES
    data = per * rhs
    size = data + 8
    noise = nugget.reshape(1, width)
    index = (block_rows, block_cols, block_count)
    pair = pltpu.VMEM((width // tile_size, 2 * rhs, tile_size), BF16)
    index_scratch = [pltpu.SMEM(item.shape, item.dtype) for item in index[:2]]
    index_sems = pltpu.SemaphoreType.DMA((2,))
    vmem = pl.BlockSpec(memory_space=pltpu.VMEM)
    any_spec = pl.BlockSpec(memory_space=pl.ANY)
    smem = pl.BlockSpec(memory_space=pltpu.SMEM)
    hbm = pl.BlockSpec(memory_space=pltpu.HBM)
    params = pltpu.CompilerParams(vmem_limit_bytes=16 * 1024 * 1024)
    cost = pl.CostEstimate(flops=4 * rhs * slots * tile_size * tile_size, transcendentals=0,
                           bytes_accessed=2 * slots * tile_size * tile_size)
    field = shape_of(rhs, width)
    total = shape_of(width // LANES, rhs, LANES)
    chunk = shape_of(data, LANES)
    tile = shape_of(8, LANES)
    loaded = shape_of(size, LANES)

    def call(kernel, name, specs, outs, scratch, args, heavy=False):
        return pl.pallas_call(
            kernel,
            in_specs=specs,
            out_specs=jax.tree.map(lambda _: vmem, outs),
            out_shape=outs,
            scratch_shapes=scratch,
            compiler_params=params,
            cost_estimate=cost if heavy else None,
            name=name,
        )(*args)

    in_hbm = functools.partial(pltpu.with_memory_space_constraint, memory_space=pltpu.HBM)
    kernel_index = index_scratch + [pair, index_sems]

    def to_owners(mirror, twin):
        sent = call(functools.partial(split_kernel, n), "split", [vmem] * 2, [chunk] * (n // 2), [], (mirror, twin))
        return [moved(value, n, far_source(j, n)) for j, value in enumerate(sent)], sent[0]

    def gathered(near, mirror, twin, others, direct, stat):
        merged = call(functools.partial(merge_kernel, n), "merge", [vmem] * 4, [chunk] * n + [tile], [],
                      (direct, mirror, twin, stat))
        parts = [merged[0]] + [shifted(value, "col", d, n) for d, value in zip(distances(n), merged[1:n])]
        stat = merged[n]
        for b in bits(n):
            stat, = call(add_kernel, "add_stat", [vmem] * (2 + n // 2), [tile], [],
                         (stat, shifted(stat, "row", b, n), *others))
        own, = call(functools.partial(combine_kernel, n), "combine", [vmem] * (3 + n + n // 2), [loaded], [],
                    (near, noise, stat, *parts, *others))
        return [own] + [shifted(own, "col", d, n) for d in distances(n)]

    current = right_sides
    for b in bits(n)[:0:-1]:
        arrived = moved(current, n, spread_target(b))
        if b == n // 2:
            mirror, blocks = call(
                mirror_first_kernel, "mirror_first", [hbm] * 2 + [smem] + [hbm] * 2,
                [total, jax.ShapeDtypeStruct(cov_blocks.shape[2:], cov_blocks.dtype)],
                index_scratch + [pltpu.VMEM((rhs, width), F32), pair, index_sems,
                                 pltpu.SemaphoreType.DMA, pltpu.SemaphoreType.DMA((slots // GROUP,))],
                (*map(in_hbm, index[:2]), block_count, in_hbm(right_sides), in_hbm(cov_blocks)), True)
            twin_mirror = shifted(mirror, "row", 1, n)
        current, = call(functools.partial(pick_kernel, b), "pick", [vmem] * 3, [field], [], (current, arrived, mirror))
    twin = shifted(current, "row", 1, n)
    others, mark = to_owners(mirror, twin_mirror)
    direct, stat, far = call(
        functools.partial(direct_first_kernel, n), "direct_first", [any_spec] * 2 + [smem] + [vmem] * 6,
        [total, tile, total], kernel_index, (*index, noise, blocks, right_sides, current, twin, mark), True)
    parts = gathered(right_sides, mirror, twin_mirror, others, direct, stat)
    far_parts = [moved(parts[0], n, far_target(j)) for j in range(n // 2)]

    left, stat_now = call(left_kernel, "left", [vmem] * (n + 1), [field, tile], [], (right_sides, *parts))
    mirror, = call(mirror_second_kernel, "mirror_second", [any_spec] * 2 + [smem] + [vmem] * 2,
                   [total], kernel_index, (*index, left, blocks), True)
    twin_mirror = shifted(mirror, "row", 1, n)
    held, = call(functools.partial(held_kernel, n), "held", [vmem] * (4 + n // 2), [total], [],
                 (left, stat_now, far, mirror, *far_parts))
    twin = shifted(held, "row", 1, n)
    others, mark = to_owners(mirror, twin_mirror)
    direct, stat = call(
        functools.partial(direct_second_kernel, n), "direct_second", [any_spec] * 2 + [smem] + [vmem] * 6,
        [total, tile], kernel_index, (*index, noise, blocks, left, held, twin, mark), True)
    parts = gathered(left, mirror, twin_mirror, others, direct, stat)
    return tuple(call(last_kernel, "last", [vmem] * (n + 3), [field, field], [],
                      (right_sides, left, stat_now, *parts)))


def solution(mesh):
    n = mesh.shape["row"]
    assert n == mesh.shape["col"] and n & (n - 1) == 0 and n >= 4
    placed = (
        P(None, ("groups", "row")),
        P(("groups", "row")),
        P(("groups", "row"), "col", None, None, None),
        P(("groups", "row"), "col", None),
        P(("groups", "row"), "col", None),
        P(("groups", "row"), "col"),
    )
    return jax.shard_map(
        functools.partial(on_device, n),
        mesh=mesh,
        in_specs=placed,
        out_specs=(P(None, ("groups", "row")), P(None, ("groups", "row"))),
        check_vma=False,
    )
```

```python
import functools

import jax
import jax.numpy as jnp
from jax import lax
from jax.experimental import pallas as pl
from jax.experimental.pallas import tpu as pltpu
from jax.sharding import PartitionSpec as P

ITERS = 2
LANES = 128
GROUP = 8
BF16 = jnp.bfloat16
F32 = jnp.float32


def shifted(value, axis, d, n):
    return lax.ppermute(value, axis, [(i, i ^ d) for i in range(n)])


def distances(n):
    return [d for d in range(n) if d > 1] + [1]


def moved(value, n, target):
    pairs = [(r * n + c, target(r, c)) for r in range(n) for c in range(n)]
    return lax.ppermute(value, ("row", "col"), [(s, t[0] * n + t[1]) for s, t in pairs])


def far_target(j):
    def target(r, c):
        d = r ^ c
        if d ^ 2 * j >= 2:
            return c ^ 2 * j, r
        return c ^ (d & 1) ^ (j == 0), c

    return target


def far_source(j, n):
    back = {far_target(j)(r, c): (r, c) for r in range(n) for c in range(n)}
    return lambda r, c: back[r, c]


def spread_target(b):
    def target(r, c):
        o = r ^ c
        move = {0: b, b: 1, b + 1: b, 1: 1}.get(o % (2 * b), 1)
        return r ^ move, c

    return target


def bits(n):
    return [1 << i for i in range(n.bit_length() - 1)]


def load_pair(dst, tile, value):
    rhs = value.shape[0]
    high = value.astype(BF16)
    dst[tile, :rhs, :] = high
    dst[tile, rhs:, :] = (value - high.astype(F32)).astype(BF16)


def product(pair, block, contract):
    both = lax.dot_general(pair, block, (((1,), (contract,)), ((), ())), preferred_element_type=F32)
    rhs = both.shape[0] // 2
    return both[:rhs] + both[rhs:]


def pack_stats(columns, rhs):
    lane = lax.broadcasted_iota(jnp.int32, (8, LANES), 1)
    tile = jnp.zeros((8, LANES), F32)
    groups = rhs // 8
    for i, column in enumerate(columns):
        for g in range(groups):
            tile = jnp.where(lane == i * groups + g, column[g * 8:(g + 1) * 8], tile)
    return tile


def unpack_stat(tile, i, rhs):
    groups = rhs // 8
    return jnp.concatenate([tile[:, i * groups + g:i * groups + g + 1] for g in range(groups)], axis=0)


def accumulate(total, tile, value):
    width = value.shape[1] // LANES
    for part in range(width):
        total[tile * width + part] += value[:, part * LANES:(part + 1) * LANES]


def add_blocks(blocks, slot_rows, slot_cols, live, pairs, total, mirror, ready=None):
    read, write, contract = (slot_rows, slot_cols, 0) if mirror else (slot_cols, slot_rows, 1)

    def body(step, carry):
        if ready is not None:
            ready(step)
        values = []
        for g in range(GROUP):
            slot = step * GROUP + g
            value = product(pairs[read[0, 0, slot]], blocks[slot], contract)
            values.append((write[0, 0, slot], jnp.where(slot < live, value, 0.0)))
        for tile, value in values:
            accumulate(total, tile, value)
        return carry

    lax.fori_loop(0, (live + GROUP - 1) // GROUP, body, 0)


def image_part(parts, me, i, per, rhs):
    rows = slice((i % per) * rhs, (i % per + 1) * rhs)
    value = parts[0][rows, :]
    for d, part in zip(distances(len(parts))[::-1], parts[1:]):
        value = jnp.where(me ^ d == i // per, part[rows, :], value)
    return value


def row_sums(value):
    return jnp.sum(value, axis=1, keepdims=True)


def cross_sums(total, value):
    rhs = value.shape[0]
    cross = jnp.zeros((rhs, LANES), F32)
    for i in range(total.shape[0]):
        cross += total[i] * value[:, i * LANES:(i + 1) * LANES]
    return row_sums(cross)


def tree_sum(values):
    values = list(values)
    while len(values) > 1:
        values = [a + b for a, b in zip(values[::2], values[1::2])]
    return values[0]


def stat_sum(parts, data):
    order = [0] + distances(len(parts))[::-1]
    return tree_sum(parts[order.index(d)][data:, :] for d in range(len(parts)))


def fetch_index(sources, targets, sems):
    copies = [pltpu.make_async_copy(s, t, sems.at[i]) for i, (s, t) in enumerate(zip(sources, targets))]
    for copy in copies:
        copy.start()
    return copies


def mirror_first_kernel(rows_hbm, cols_hbm, count, right_hbm, cov, total, blocks, *scratch):
    slot_rows, slot_cols, right, pairs, index_sems, right_sem, block_sems = scratch
    slots, tile_size = blocks.shape[:2]

    def block_copy(i):
        part = pl.ds(i * GROUP, GROUP)
        return pltpu.make_async_copy(cov.at[0, 0, part], blocks.at[part], block_sems.at[i])

    copies = fetch_index((rows_hbm, cols_hbm), (slot_rows, slot_cols), index_sems)
    load = pltpu.make_async_copy(right_hbm, right, right_sem)
    load.start()
    live = count[0, 0]
    for i in range(slots // GROUP):
        @pl.when(i * GROUP < live)
        def _():
            block_copy(i).start()
    total[...] = jnp.zeros_like(total)
    load.wait()
    for tile in range(right.shape[1] // tile_size):
        load_pair(pairs, tile, right[:, tile * tile_size:(tile + 1) * tile_size])
    for copy in copies:
        copy.wait()
    add_blocks(blocks, slot_rows, slot_cols, live, pairs, total, True, lambda i: block_copy(i).wait())


def mirror_second_kernel(rows_any, cols_any, count, near, blocks, total, *scratch):
    slot_rows, slot_cols, pairs, index_sems = scratch
    tile_size = blocks.shape[1]
    copies = fetch_index((rows_any, cols_any), (slot_rows, slot_cols), index_sems)
    total[...] = jnp.zeros_like(total)
    for tile in range(near.shape[1] // tile_size):
        load_pair(pairs, tile, near[:, tile * tile_size:(tile + 1) * tile_size])
    for copy in copies:
        copy.wait()
    add_blocks(blocks, slot_rows, slot_cols, count[0, 0], pairs, total, True)


def finish_direct(total, near, noise, stat, n):
    value = near[...]
    rhs = value.shape[0]
    square = value * value
    share = 1.0 / n
    bend = share * row_sums(square * noise[...]) + 2.0 * cross_sums(total, value)
    stat[...] = pack_stats([share * row_sums(square), bend], rhs)


def direct_first_kernel(n, rows_any, cols_any, count, noise, blocks, near, current, twin, mark, total, stat, far, *scratch):
    slot_rows, slot_cols, pairs, index_sems = scratch
    tile_size = blocks.shape[1]
    pieces = tile_size // LANES
    copies = fetch_index((rows_any, cols_any), (slot_rows, slot_cols), index_sems)
    odd = (lax.axis_index("row") ^ lax.axis_index("col")) & 1
    for o, source in enumerate((current, twin)):
        @pl.when(odd == o)
        def _():
            for tile in range(near.shape[1] // tile_size):
                value = source[:, tile * tile_size:(tile + 1) * tile_size]
                load_pair(pairs, tile, value)
                for i in range(pieces):
                    far[tile * pieces + i] = value[:, i * LANES:(i + 1) * LANES]
    total[...] = jnp.zeros_like(total)
    for copy in copies:
        copy.wait()
    add_blocks(blocks, slot_rows, slot_cols, count[0, 0], pairs, total, False)
    finish_direct(total, near, noise, stat, n)


def direct_second_kernel(n, rows_any, cols_any, count, noise, blocks, near, held, twin, mark, total, stat, *scratch):
    slot_rows, slot_cols, pairs, index_sems = scratch
    tile_size = blocks.shape[1]
    pieces = tile_size // LANES
    per = held.shape[0] // n
    copies = fetch_index((rows_any, cols_any), (slot_rows, slot_cols), index_sems)
    row = lax.axis_index("row")
    offset = row ^ lax.axis_index("col")
    for tile in range(near.shape[1] // tile_size):
        value = []
        for i in range(tile * pieces, (tile + 1) * pieces):
            own = jnp.logical_or(offset == 0, jnp.logical_and(offset >= 2, ((i // per) ^ row) & 1 == 0))
            value.append(jnp.where(own, held[i], twin[i]))
        load_pair(pairs, tile, jnp.concatenate(value, axis=1))
    total[...] = jnp.zeros_like(total)
    for copy in copies:
        copy.wait()
    add_blocks(blocks, slot_rows, slot_cols, count[0, 0], pairs, total, False)
    finish_direct(total, near, noise, stat, n)


def add_kernel(one, two, *refs):
    refs[-1][...] = one[...] + two[...]


def pick_kernel(b, current, arrived, mark, out):
    there = (lax.axis_index("row") ^ lax.axis_index("col")) & b
    out[...] = jnp.where(there != 0, arrived[...], current[...])


def split_kernel(n, mirror, twin, *outs):
    per = mirror.shape[0] // n
    rhs = mirror.shape[1]
    row = lax.axis_index("row")
    for j, out in enumerate(outs):
        first = (row ^ 2 * j) * per
        for i in range(per):
            out[i * rhs:(i + 1) * rhs, :] = mirror[first + i] + twin[first + i]


def merge_kernel(n, direct, mirror, twin, stat, *outs):
    per = direct.shape[0] // n
    rhs = direct.shape[1]
    me = lax.axis_index("col")
    diagonal = lax.axis_index("row") == me
    outs[n][...] = stat[...]
    for d, out in zip([0] + distances(n), outs):
        first = (me ^ d) * per

        @pl.when(diagonal)
        def _():
            for i in range(per):
                out[i * rhs:(i + 1) * rhs, :] = direct[first + i] + (mirror[first + i] + twin[first + i])

        @pl.when(jnp.logical_not(diagonal))
        def _():
            for i in range(per):
                out[i * rhs:(i + 1) * rhs, :] = direct[first + i]


def combine_kernel(n, near, noise, stat, *refs):
    parts, others, chunk = refs[:n], refs[n:-1], refs[-1]
    rhs = near.shape[0]
    data = parts[0].shape[0]
    per = data // rhs
    me = lax.axis_index("col")
    group = (lax.axis_index("row") ^ me) // 2
    value = tree_sum(ref[...] for ref in parts)
    for j, other in enumerate(others):
        value += jnp.where(group == j, 0.0, other[...])
    chunk[:data, :] = value
    chunk[data:, :] = stat[...]
    for k in range(n):
        @pl.when(me == k)
        def _():
            for i in range(per):
                lanes = slice((k * per + i) * LANES, (k * per + i + 1) * LANES)
                chunk[i * rhs:(i + 1) * rhs, :] += near[:, lanes] * noise[:, lanes]


def left_kernel(right, *refs):
    parts, (left, stat) = refs[:-2], refs[-2:]
    rhs, width = right.shape
    data = parts[0].shape[0] - 8
    per = data // rhs
    me = lax.axis_index("col")
    both = stat_sum(parts, data)
    stat[...] = both
    size_now = unpack_stat(both, 0, rhs) / unpack_stat(both, 1, rhs)
    for i in range(width // LANES):
        lanes = slice(i * LANES, (i + 1) * LANES)
        left[:, lanes] = right[:, lanes] - size_now * image_part(parts, me, i, per, rhs)


def held_kernel(n, left, stat, far, mark, *refs):
    parts, held = refs[:-1], refs[-1]
    rhs = left.shape[0]
    per = held.shape[0] // n
    row = lax.axis_index("row")
    diagonal = (row ^ lax.axis_index("col")) < 2
    size_now = unpack_stat(stat[...], 0, rhs) / unpack_stat(stat[...], 1, rhs)

    @pl.when(diagonal)
    def _():
        for i in range(held.shape[0]):
            held[i] = left[:, i * LANES:(i + 1) * LANES]

    @pl.when(jnp.logical_not(diagonal))
    def _():
        for j, part in enumerate(parts):
            first = (row ^ 2 * j) * per
            for i in range(per):
                held[first + i] = far[first + i] - size_now * part[i * rhs:(i + 1) * rhs, :]


def last_kernel(right, left, stat_now, *refs):
    parts, (solution, residual) = refs[:-2], refs[-2:]
    rhs, width = right.shape
    data = parts[0].shape[0] - 8
    per = data // rhs
    me = lax.axis_index("col")
    both = stat_sum(parts, data)
    norm = unpack_stat(stat_now[...], 0, rhs)
    norm_next = unpack_stat(both, 0, rhs)
    size_now = norm / unpack_stat(stat_now[...], 1, rhs)
    ratio = norm_next / norm
    size_next = norm_next / (unpack_stat(both, 1, rhs) - ratio * norm_next / size_now)
    back = ratio / size_now
    for i in range(width // LANES):
        lanes = slice(i * LANES, (i + 1) * LANES)
        first = right[:, lanes]
        now = left[:, lanes]
        solution[:, lanes] = size_now * first + size_next * (now + ratio * first)
        image = image_part(parts, me, i, per, rhs) + back * (first - now)
        residual[:, lanes] = now - size_next * image


def shape_of(*shape):
    return jax.ShapeDtypeStruct(shape, F32)


def on_device(n, right_sides, nugget, cov_blocks, block_rows, block_cols, block_count):
    rhs, width = right_sides.shape
    slots, tile_size = cov_blocks.shape[2:4]
    per = width // n // LANES
    data = per * rhs
    size = data + 8
    noise = nugget.reshape(1, width)
    index = (block_rows, block_cols, block_count)
    pair = pltpu.VMEM((width // tile_size, 2 * rhs, tile_size), BF16)
    index_scratch = [pltpu.SMEM(item.shape, item.dtype) for item in index[:2]]
    index_sems = pltpu.SemaphoreType.DMA((2,))
    vmem = pl.BlockSpec(memory_space=pltpu.VMEM)
    any_spec = pl.BlockSpec(memory_space=pl.ANY)
    smem = pl.BlockSpec(memory_space=pltpu.SMEM)
    hbm = pl.BlockSpec(memory_space=pltpu.HBM)
    params = pltpu.CompilerParams(vmem_limit_bytes=16 * 1024 * 1024)
    cost = pl.CostEstimate(flops=4 * rhs * slots * tile_size * tile_size, transcendentals=0,
                           bytes_accessed=2 * slots * tile_size * tile_size)
    field = shape_of(rhs, width)
    total = shape_of(width // LANES, rhs, LANES)
    chunk = shape_of(data, LANES)
    tile = shape_of(8, LANES)
    loaded = shape_of(size, LANES)

    def call(kernel, name, specs, outs, scratch, args, heavy=False):
        return pl.pallas_call(
            kernel,
            in_specs=specs,
            out_specs=jax.tree.map(lambda _: vmem, outs),
            out_shape=outs,
            scratch_shapes=scratch,
            compiler_params=params,
            cost_estimate=cost if heavy else None,
            name=name,
        )(*args)

    in_hbm = functools.partial(pltpu.with_memory_space_constraint, memory_space=pltpu.HBM)
    kernel_index = index_scratch + [pair, index_sems]

    def to_owners(mirror, twin):
        sent = call(functools.partial(split_kernel, n), "split", [vmem] * 2, [chunk] * (n // 2), [], (mirror, twin))
        return [moved(value, n, far_source(j, n)) for j, value in enumerate(sent)], sent[0]

    def gathered(near, mirror, twin, others, direct, stat):
        merged = call(functools.partial(merge_kernel, n), "merge", [vmem] * 4, [chunk] * n + [tile], [],
                      (direct, mirror, twin, stat))
        parts = [merged[0]] + [shifted(value, "col", d, n) for d, value in zip(distances(n), merged[1:n])]
        stat = merged[n]
        for b in bits(n):
            stat, = call(add_kernel, "add_stat", [vmem] * (2 + n // 2), [tile], [],
                         (stat, shifted(stat, "row", b, n), *others))
        own, = call(functools.partial(combine_kernel, n), "combine", [vmem] * (3 + n + n // 2), [loaded], [],
                    (near, noise, stat, *parts, *others))
        return [own] + [shifted(own, "col", d, n) for d in distances(n)[::-1]]

    current = right_sides
    for b in bits(n)[:0:-1]:
        arrived = moved(current, n, spread_target(b))
        if b == n // 2:
            mirror, blocks = call(
                mirror_first_kernel, "mirror_first", [hbm] * 2 + [smem] + [hbm] * 2,
                [total, jax.ShapeDtypeStruct(cov_blocks.shape[2:], cov_blocks.dtype)],
                index_scratch + [pltpu.VMEM((rhs, width), F32), pair, index_sems,
                                 pltpu.SemaphoreType.DMA, pltpu.SemaphoreType.DMA((slots // GROUP,))],
                (*map(in_hbm, index[:2]), block_count, in_hbm(right_sides), in_hbm(cov_blocks)), True)
            twin_mirror = shifted(mirror, "row", 1, n)
        current, = call(functools.partial(pick_kernel, b), "pick", [vmem] * 3, [field], [], (current, arrived, mirror))
    twin = shifted(current, "row", 1, n)
    others, mark = to_owners(mirror, twin_mirror)
    direct, stat, far = call(
        functools.partial(direct_first_kernel, n), "direct_first", [any_spec] * 2 + [smem] + [vmem] * 6,
        [total, tile, total], kernel_index, (*index, noise, blocks, right_sides, current, twin, mark), True)
    parts = gathered(right_sides, mirror, twin_mirror, others, direct, stat)
    far_parts = [moved(parts[0], n, far_target(j)) for j in range(n // 2)]

    left, stat_now = call(left_kernel, "left", [vmem] * (n + 1), [field, tile], [], (right_sides, *parts))
    mirror, = call(mirror_second_kernel, "mirror_second", [any_spec] * 2 + [smem] + [vmem] * 2,
                   [total], kernel_index, (*index, left, blocks), True)
    twin_mirror = shifted(mirror, "row", 1, n)
    held, = call(functools.partial(held_kernel, n), "held", [vmem] * (4 + n // 2), [total], [],
                 (left, stat_now, far, mirror, *far_parts))
    twin = shifted(held, "row", 1, n)
    others, mark = to_owners(mirror, twin_mirror)
    direct, stat = call(
        functools.partial(direct_second_kernel, n), "direct_second", [any_spec] * 2 + [smem] + [vmem] * 6,
        [total, tile], kernel_index, (*index, noise, blocks, left, held, twin, mark), True)
    parts = gathered(left, mirror, twin_mirror, others, direct, stat)
    return tuple(call(last_kernel, "last", [vmem] * (n + 3), [field, field], [],
                      (right_sides, left, stat_now, *parts)))


def solution(mesh):
    n = mesh.shape["row"]
    assert n == mesh.shape["col"] and n & (n - 1) == 0 and n >= 4
    placed = (
        P(None, ("groups", "row")),
        P(("groups", "row")),
        P(("groups", "row"), "col", None, None, None),
        P(("groups", "row"), "col", None),
        P(("groups", "row"), "col", None),
        P(("groups", "row"), "col"),
    )
    return jax.shard_map(
        functools.partial(on_device, n),
        mesh=mesh,
        in_specs=placed,
        out_specs=(P(None, ("groups", "row")), P(None, ("groups", "row"))),
        check_vma=False,
    )
```

```python
import functools

import jax
import jax.numpy as jnp
from jax import lax
from jax.experimental import pallas as pl
from jax.experimental.pallas import tpu as pltpu
from jax.sharding import PartitionSpec as P

ITERS = 2
LANES = 128
GROUP = 8
BF16 = jnp.bfloat16
F32 = jnp.float32


def shifted(value, axis, d, n):
    return lax.ppermute(value, axis, [(i, i ^ d) for i in range(n)])


def distances(n):
    return [d for d in range(n) if d > 1] + [1]


def moved(value, n, target):
    pairs = [(r * n + c, target(r, c)) for r in range(n) for c in range(n)]
    return lax.ppermute(value, ("row", "col"), [(s, t[0] * n + t[1]) for s, t in pairs])


def far_target(j):
    def target(r, c):
        d = r ^ c
        if d ^ 2 * j >= 2:
            return c ^ 2 * j, r
        return c ^ (d & 1) ^ (j == 0), c

    return target


def far_source(j, n):
    back = {far_target(j)(r, c): (r, c) for r in range(n) for c in range(n)}
    return lambda r, c: back[r, c]


def spread_target(b):
    def target(r, c):
        o = r ^ c
        move = {0: b, b: 1, b + 1: b, 1: 1}.get(o % (2 * b), 1)
        return r ^ move, c

    return target


def bits(n):
    return [1 << i for i in range(n.bit_length() - 1)]


def load_pair(dst, tile, value):
    rhs = value.shape[0]
    high = value.astype(BF16)
    dst[tile, :rhs, :] = high
    dst[tile, rhs:, :] = (value - high.astype(F32)).astype(BF16)


def product(pair, block, contract):
    both = lax.dot_general(pair, block, (((1,), (contract,)), ((), ())), preferred_element_type=F32)
    rhs = both.shape[0] // 2
    return both[:rhs] + both[rhs:]


def pack_stats(columns, rhs):
    lane = lax.broadcasted_iota(jnp.int32, (8, LANES), 1)
    tile = jnp.zeros((8, LANES), F32)
    groups = rhs // 8
    for i, column in enumerate(columns):
        for g in range(groups):
            tile = jnp.where(lane == i * groups + g, column[g * 8:(g + 1) * 8], tile)
    return tile


def unpack_stat(tile, i, rhs):
    groups = rhs // 8
    return jnp.concatenate([tile[:, i * groups + g:i * groups + g + 1] for g in range(groups)], axis=0)


def accumulate(total, tile, value):
    width = value.shape[1] // LANES
    for part in range(width):
        total[tile * width + part] += value[:, part * LANES:(part + 1) * LANES]


def add_blocks(blocks, slot_rows, slot_cols, live, pairs, total, mirror, ready=None):
    read, write, contract = (slot_rows, slot_cols, 0) if mirror else (slot_cols, slot_rows, 1)

    def body(step, carry):
        if ready is not None:
            ready(step)
        values = []
        for g in range(GROUP):
            slot = step * GROUP + g
            value = product(pairs[read[0, 0, slot]], blocks[slot], contract)
            values.append((write[0, 0, slot], jnp.where(slot < live, value, 0.0)))
        for tile, value in values:
            accumulate(total, tile, value)
        return carry

    lax.fori_loop(0, (live + GROUP - 1) // GROUP, body, 0)


def image_part(parts, me, i, per, rhs):
    rows = slice((i % per) * rhs, (i % per + 1) * rhs)
    value = parts[0][rows, :]
    for d, part in zip(distances(len(parts))[::-1], parts[1:]):
        value = jnp.where(me ^ d == i // per, part[rows, :], value)
    return value


def row_sums(value):
    return jnp.sum(value, axis=1, keepdims=True)


def cross_sums(total, value):
    rhs = value.shape[0]
    cross = jnp.zeros((rhs, LANES), F32)
    for i in range(total.shape[0]):
        cross += total[i] * value[:, i * LANES:(i + 1) * LANES]
    return row_sums(cross)


def tree_sum(values):
    values = list(values)
    while len(values) > 1:
        values = [a + b for a, b in zip(values[::2], values[1::2])]
    return values[0]


def stat_sum(parts, data):
    order = [0] + distances(len(parts))[::-1]
    return tree_sum(parts[order.index(d)][data:, :] for d in range(len(parts)))


def fetch_index(sources, targets, sems):
    copies = [pltpu.make_async_copy(s, t, sems.at[i]) for i, (s, t) in enumerate(zip(sources, targets))]
    for copy in copies:
        copy.start()
    return copies


def mirror_first_kernel(rows_hbm, cols_hbm, count, right_hbm, cov, total, blocks, *scratch):
    slot_rows, slot_cols, right, pairs, index_sems, right_sem, block_sems = scratch
    slots, tile_size = blocks.shape[:2]

    def block_copy(i):
        part = pl.ds(i * GROUP, GROUP)
        return pltpu.make_async_copy(cov.at[0, 0, part], blocks.at[part], block_sems.at[i])

    copies = fetch_index((rows_hbm, cols_hbm), (slot_rows, slot_cols), index_sems)
    load = pltpu.make_async_copy(right_hbm, right, right_sem)
    load.start()
    live = count[0, 0]
    for i in range(slots // GROUP):
        @pl.when(i * GROUP < live)
        def _():
            block_copy(i).start()
    total[...] = jnp.zeros_like(total)
    load.wait()
    for tile in range(right.shape[1] // tile_size):
        load_pair(pairs, tile, right[:, tile * tile_size:(tile + 1) * tile_size])
    for copy in copies:
        copy.wait()
    add_blocks(blocks, slot_rows, slot_cols, live, pairs, total, True, lambda i: block_copy(i).wait())


def mirror_second_kernel(rows_any, cols_any, count, near, blocks, total, *scratch):
    slot_rows, slot_cols, pairs, index_sems = scratch
    tile_size = blocks.shape[1]
    copies = fetch_index((rows_any, cols_any), (slot_rows, slot_cols), index_sems)
    total[...] = jnp.zeros_like(total)
    for tile in range(near.shape[1] // tile_size):
        load_pair(pairs, tile, near[:, tile * tile_size:(tile + 1) * tile_size])
    for copy in copies:
        copy.wait()
    add_blocks(blocks, slot_rows, slot_cols, count[0, 0], pairs, total, True)


def finish_direct(total, near, noise, stat, n):
    value = near[...]
    rhs = value.shape[0]
    square = value * value
    share = 1.0 / n
    bend = share * row_sums(square * noise[...]) + 2.0 * cross_sums(total, value)
    stat[...] = pack_stats([share * row_sums(square), bend], rhs)


def direct_first_kernel(n, rows_any, cols_any, count, noise, blocks, near, current, twin, total, stat, far, *scratch):
    slot_rows, slot_cols, pairs, index_sems = scratch
    tile_size = blocks.shape[1]
    pieces = tile_size // LANES
    copies = fetch_index((rows_any, cols_any), (slot_rows, slot_cols), index_sems)
    odd = (lax.axis_index("row") ^ lax.axis_index("col")) & 1
    for o, source in enumerate((current, twin)):
        @pl.when(odd == o)
        def _():
            for tile in range(near.shape[1] // tile_size):
                value = source[:, tile * tile_size:(tile + 1) * tile_size]
                load_pair(pairs, tile, value)
                for i in range(pieces):
                    far[tile * pieces + i] = value[:, i * LANES:(i + 1) * LANES]
    total[...] = jnp.zeros_like(total)
    for copy in copies:
        copy.wait()
    add_blocks(blocks, slot_rows, slot_cols, count[0, 0], pairs, total, False)
    finish_direct(total, near, noise, stat, n)


def direct_second_kernel(n, rows_any, cols_any, count, noise, blocks, near, held, twin, total, stat, *scratch):
    slot_rows, slot_cols, pairs, index_sems = scratch
    tile_size = blocks.shape[1]
    pieces = tile_size // LANES
    per = held.shape[0] // n
    copies = fetch_index((rows_any, cols_any), (slot_rows, slot_cols), index_sems)
    row = lax.axis_index("row")
    offset = row ^ lax.axis_index("col")
    for tile in range(near.shape[1] // tile_size):
        value = []
        for i in range(tile * pieces, (tile + 1) * pieces):
            own = jnp.logical_or(offset == 0, jnp.logical_and(offset >= 2, ((i // per) ^ row) & 1 == 0))
            value.append(jnp.where(own, held[i], twin[i]))
        load_pair(pairs, tile, jnp.concatenate(value, axis=1))
    total[...] = jnp.zeros_like(total)
    for copy in copies:
        copy.wait()
    add_blocks(blocks, slot_rows, slot_cols, count[0, 0], pairs, total, False)
    finish_direct(total, near, noise, stat, n)


def add_kernel(one, two, mark, out):
    out[...] = one[...] + two[...]


def pick_kernel(b, current, arrived, mark, out):
    there = (lax.axis_index("row") ^ lax.axis_index("col")) & b
    out[...] = jnp.where(there != 0, arrived[...], current[...])


def split_kernel(n, mirror, twin, mark, *outs):
    per = mirror.shape[0] // n
    rhs = mirror.shape[1]
    row = lax.axis_index("row")
    for j, out in enumerate(outs):
        first = (row ^ 2 * j) * per
        for i in range(per):
            out[i * rhs:(i + 1) * rhs, :] = mirror[first + i] + twin[first + i]


def merge_kernel(n, direct, mirror, twin, stat, *outs):
    per = direct.shape[0] // n
    rhs = direct.shape[1]
    me = lax.axis_index("col")
    diagonal = lax.axis_index("row") == me
    outs[n][...] = stat[...]
    for d, out in zip([0] + distances(n), outs):
        first = (me ^ d) * per

        @pl.when(diagonal)
        def _():
            for i in range(per):
                out[i * rhs:(i + 1) * rhs, :] = direct[first + i] + (mirror[first + i] + twin[first + i])

        @pl.when(jnp.logical_not(diagonal))
        def _():
            for i in range(per):
                out[i * rhs:(i + 1) * rhs, :] = direct[first + i]


def combine_kernel(n, near, noise, stat, *refs):
    parts, others, chunk = refs[:n], refs[n:-1], refs[-1]
    rhs = near.shape[0]
    data = parts[0].shape[0]
    per = data // rhs
    me = lax.axis_index("col")
    group = (lax.axis_index("row") ^ me) // 2
    value = tree_sum(ref[...] for ref in parts)
    for j, other in enumerate(others):
        value += jnp.where(group == j, 0.0, other[...])
    chunk[:data, :] = value
    chunk[data:, :] = stat[...]
    for k in range(n):
        @pl.when(me == k)
        def _():
            for i in range(per):
                lanes = slice((k * per + i) * LANES, (k * per + i + 1) * LANES)
                chunk[i * rhs:(i + 1) * rhs, :] += near[:, lanes] * noise[:, lanes]


def left_kernel(right, *refs):
    parts, (left, stat) = refs[:-2], refs[-2:]
    rhs, width = right.shape
    data = parts[0].shape[0] - 8
    per = data // rhs
    me = lax.axis_index("col")
    both = stat_sum(parts, data)
    stat[...] = both
    size_now = unpack_stat(both, 0, rhs) / unpack_stat(both, 1, rhs)
    for i in range(width // LANES):
        lanes = slice(i * LANES, (i + 1) * LANES)
        left[:, lanes] = right[:, lanes] - size_now * image_part(parts, me, i, per, rhs)


def held_kernel(n, left, stat, far, mark, *refs):
    parts, held = refs[:-1], refs[-1]
    rhs = left.shape[0]
    per = held.shape[0] // n
    row = lax.axis_index("row")
    diagonal = (row ^ lax.axis_index("col")) < 2
    size_now = unpack_stat(stat[...], 0, rhs) / unpack_stat(stat[...], 1, rhs)

    @pl.when(diagonal)
    def _():
        for i in range(held.shape[0]):
            held[i] = left[:, i * LANES:(i + 1) * LANES]

    @pl.when(jnp.logical_not(diagonal))
    def _():
        for j, part in enumerate(parts):
            first = (row ^ 2 * j) * per
            for i in range(per):
                held[first + i] = far[first + i] - size_now * part[i * rhs:(i + 1) * rhs, :]


def last_kernel(right, left, stat_now, *refs):
    parts, (solution, residual) = refs[:-2], refs[-2:]
    rhs, width = right.shape
    data = parts[0].shape[0] - 8
    per = data // rhs
    me = lax.axis_index("col")
    both = stat_sum(parts, data)
    norm = unpack_stat(stat_now[...], 0, rhs)
    norm_next = unpack_stat(both, 0, rhs)
    size_now = norm / unpack_stat(stat_now[...], 1, rhs)
    ratio = norm_next / norm
    size_next = norm_next / (unpack_stat(both, 1, rhs) - ratio * norm_next / size_now)
    back = ratio / size_now
    for i in range(width // LANES):
        lanes = slice(i * LANES, (i + 1) * LANES)
        first = right[:, lanes]
        now = left[:, lanes]
        solution[:, lanes] = size_now * first + size_next * (now + ratio * first)
        image = image_part(parts, me, i, per, rhs) + back * (first - now)
        residual[:, lanes] = now - size_next * image


def shape_of(*shape):
    return jax.ShapeDtypeStruct(shape, F32)


def on_device(n, right_sides, nugget, cov_blocks, block_rows, block_cols, block_count):
    rhs, width = right_sides.shape
    slots, tile_size = cov_blocks.shape[2:4]
    per = width // n // LANES
    data = per * rhs
    size = data + 8
    noise = nugget.reshape(1, width)
    index = (block_rows, block_cols, block_count)
    pair = pltpu.VMEM((width // tile_size, 2 * rhs, tile_size), BF16)
    index_scratch = [pltpu.SMEM(item.shape, item.dtype) for item in index[:2]]
    index_sems = pltpu.SemaphoreType.DMA((2,))
    vmem = pl.BlockSpec(memory_space=pltpu.VMEM)
    any_spec = pl.BlockSpec(memory_space=pl.ANY)
    smem = pl.BlockSpec(memory_space=pltpu.SMEM)
    hbm = pl.BlockSpec(memory_space=pltpu.HBM)
    params = pltpu.CompilerParams(vmem_limit_bytes=16 * 1024 * 1024)
    cost = pl.CostEstimate(flops=4 * rhs * slots * tile_size * tile_size, transcendentals=0,
                           bytes_accessed=2 * slots * tile_size * tile_size)
    field = shape_of(rhs, width)
    total = shape_of(width // LANES, rhs, LANES)
    chunk = shape_of(data, LANES)
    tile = shape_of(8, LANES)
    loaded = shape_of(size, LANES)

    def call(kernel, name, specs, outs, scratch, args, heavy=False):
        return pl.pallas_call(
            kernel,
            in_specs=specs,
            out_specs=jax.tree.map(lambda _: vmem, outs),
            out_shape=outs,
            scratch_shapes=scratch,
            compiler_params=params,
            cost_estimate=cost if heavy else None,
            name=name,
        )(*args)

    in_hbm = functools.partial(pltpu.with_memory_space_constraint, memory_space=pltpu.HBM)
    kernel_index = index_scratch + [pair, index_sems]

    def gathered(near, mirror, twin, direct, stat):
        merged = call(functools.partial(merge_kernel, n), "merge", [vmem] * 4, [chunk] * n + [tile], [],
                      (direct, mirror, twin, stat))
        parts = [merged[0]] + [shifted(value, "col", d, n) for d, value in zip(distances(n), merged[1:n])]
        sent = call(functools.partial(split_kernel, n), "split", [vmem] * 3, [chunk] * (n // 2), [],
                    (mirror, twin, merged[n]))
        others = [moved(value, n, far_source(j, n)) for j, value in enumerate(sent)]
        stat = merged[n]
        for b in bits(n):
            stat, = call(add_kernel, "add_stat", [vmem] * 3, [tile], [], (stat, shifted(stat, "row", b, n), parts[1]))
        own, = call(functools.partial(combine_kernel, n), "combine", [vmem] * (3 + n + n // 2), [loaded], [],
                    (near, noise, stat, *parts, *others))
        return [own] + [shifted(own, "col", d, n) for d in distances(n)[::-1]]

    current = right_sides
    for b in bits(n)[:0:-1]:
        arrived = moved(current, n, spread_target(b))
        if b == n // 2:
            mirror, blocks = call(
                mirror_first_kernel, "mirror_first", [hbm] * 2 + [smem] + [hbm] * 2,
                [total, jax.ShapeDtypeStruct(cov_blocks.shape[2:], cov_blocks.dtype)],
                index_scratch + [pltpu.VMEM((rhs, width), F32), pair, index_sems,
                                 pltpu.SemaphoreType.DMA, pltpu.SemaphoreType.DMA((slots // GROUP,))],
                (*map(in_hbm, index[:2]), block_count, in_hbm(right_sides), in_hbm(cov_blocks)), True)
            twin_mirror = shifted(mirror, "row", 1, n)
        current, = call(functools.partial(pick_kernel, b), "pick", [vmem] * 3, [field], [], (current, arrived, mirror))
    twin = shifted(current, "row", 1, n)
    direct, stat, far = call(
        functools.partial(direct_first_kernel, n), "direct_first", [any_spec] * 2 + [smem] + [vmem] * 5,
        [total, tile, total], kernel_index, (*index, noise, blocks, right_sides, current, twin), True)
    parts = gathered(right_sides, mirror, twin_mirror, direct, stat)
    far_parts = [moved(parts[0], n, far_target(j)) for j in range(n // 2)]

    left, stat_now = call(left_kernel, "left", [vmem] * (n + 1), [field, tile], [], (right_sides, *parts))
    mirror, = call(mirror_second_kernel, "mirror_second", [any_spec] * 2 + [smem] + [vmem] * 2,
                   [total], kernel_index, (*index, left, blocks), True)
    twin_mirror = shifted(mirror, "row", 1, n)
    held, = call(functools.partial(held_kernel, n), "held", [vmem] * (4 + n // 2), [total], [],
                 (left, stat_now, far, mirror, *far_parts))
    twin = shifted(held, "row", 1, n)
    direct, stat = call(
        functools.partial(direct_second_kernel, n), "direct_second", [any_spec] * 2 + [smem] + [vmem] * 5,
        [total, tile], kernel_index, (*index, noise, blocks, left, held, twin), True)
    parts = gathered(left, mirror, twin_mirror, direct, stat)
    return tuple(call(last_kernel, "last", [vmem] * (n + 3), [field, field], [],
                      (right_sides, left, stat_now, *parts)))


def solution(mesh):
    n = mesh.shape["row"]
    assert n == mesh.shape["col"] and n & (n - 1) == 0 and n >= 4
    placed = (
        P(None, ("groups", "row")),
        P(("groups", "row")),
        P(("groups", "row"), "col", None, None, None),
        P(("groups", "row"), "col", None),
        P(("groups", "row"), "col", None),
        P(("groups", "row"), "col"),
    )
    return jax.shard_map(
        functools.partial(on_device, n),
        mesh=mesh,
        in_specs=placed,
        out_specs=(P(None, ("groups", "row")), P(None, ("groups", "row"))),
        check_vma=False,
    )
```

```python
import functools

import jax
import jax.numpy as jnp
from jax import lax
from jax.experimental import pallas as pl
from jax.experimental.pallas import tpu as pltpu
from jax.sharding import PartitionSpec as P

ITERS = 2
LANES = 128
GROUP = 8
BF16 = jnp.bfloat16
F32 = jnp.float32


def shifted(value, axis, d, n):
    return lax.ppermute(value, axis, [(i, i ^ d) for i in range(n)])


def distances(n):
    return [d for d in range(n) if d > 1] + [1]


def moved(value, n, target):
    pairs = [(r * n + c, target(r, c)) for r in range(n) for c in range(n)]
    return lax.ppermute(value, ("row", "col"), [(s, t[0] * n + t[1]) for s, t in pairs])


def far_target(j):
    def target(r, c):
        d = r ^ c
        if d ^ 2 * j >= 2:
            return c ^ 2 * j, r
        return c ^ (d & 1) ^ (j == 0), c

    return target


def far_source(j, n):
    back = {far_target(j)(r, c): (r, c) for r in range(n) for c in range(n)}
    return lambda r, c: back[r, c]


def spread_target(b):
    def target(r, c):
        o = r ^ c
        move = {0: b, b: 1, b + 1: b, 1: 1}.get(o % (2 * b), 1)
        return r ^ move, c

    return target


def bits(n):
    return [1 << i for i in range(n.bit_length() - 1)]


def load_pair(dst, tile, value):
    rhs = value.shape[0]
    high = value.astype(BF16)
    dst[tile, :rhs, :] = high
    dst[tile, rhs:, :] = (value - high.astype(F32)).astype(BF16)


def product(pair, block, contract):
    both = lax.dot_general(pair, block, (((1,), (contract,)), ((), ())), preferred_element_type=F32)
    rhs = both.shape[0] // 2
    return both[:rhs] + both[rhs:]


def pack_stats(columns, rhs):
    lane = lax.broadcasted_iota(jnp.int32, (8, LANES), 1)
    tile = jnp.zeros((8, LANES), F32)
    groups = rhs // 8
    for i, column in enumerate(columns):
        for g in range(groups):
            tile = jnp.where(lane == i * groups + g, column[g * 8:(g + 1) * 8], tile)
    return tile


def unpack_stat(tile, i, rhs):
    groups = rhs // 8
    return jnp.concatenate([tile[:, i * groups + g:i * groups + g + 1] for g in range(groups)], axis=0)


def accumulate(total, tile, value):
    width = value.shape[1] // LANES
    for part in range(width):
        total[tile * width + part] += value[:, part * LANES:(part + 1) * LANES]


def add_blocks(blocks, slot_rows, slot_cols, live, pairs, total, mirror, ready=None):
    read, write, contract = (slot_rows, slot_cols, 0) if mirror else (slot_cols, slot_rows, 1)

    def body(step, carry):
        if ready is not None:
            ready(step)
        values = []
        for g in range(GROUP):
            slot = step * GROUP + g
            value = product(pairs[read[0, 0, slot]], blocks[slot], contract)
            values.append((write[0, 0, slot], jnp.where(slot < live, value, 0.0)))
        for tile, value in values:
            accumulate(total, tile, value)
        return carry

    lax.fori_loop(0, (live + GROUP - 1) // GROUP, body, 0)


def image_part(parts, me, i, per, rhs):
    rows = slice((i % per) * rhs, (i % per + 1) * rhs)
    value = parts[0][rows, :]
    for d, part in zip(distances(len(parts)), parts[1:]):
        value = jnp.where(me ^ d == i // per, part[rows, :], value)
    return value


def row_sums(value):
    return jnp.sum(value, axis=1, keepdims=True)


def cross_sums(total, value):
    rhs = value.shape[0]
    cross = jnp.zeros((rhs, LANES), F32)
    for i in range(total.shape[0]):
        cross += total[i] * value[:, i * LANES:(i + 1) * LANES]
    return row_sums(cross)


def tree_sum(values):
    values = list(values)
    while len(values) > 1:
        values = [a + b for a, b in zip(values[::2], values[1::2])]
    return values[0]


def stat_sum(parts, data):
    order = [0] + distances(len(parts))
    return tree_sum(parts[order.index(d)][data:, :] for d in range(len(parts)))


def fetch_index(sources, targets, sems):
    copies = [pltpu.make_async_copy(s, t, sems.at[i]) for i, (s, t) in enumerate(zip(sources, targets))]
    for copy in copies:
        copy.start()
    return copies


def mirror_first_kernel(rows_hbm, cols_hbm, count, right_hbm, cov, total, blocks, *scratch):
    slot_rows, slot_cols, right, pairs, index_sems, right_sem, block_sems = scratch
    slots, tile_size = blocks.shape[:2]

    def block_copy(i):
        part = pl.ds(i * GROUP, GROUP)
        return pltpu.make_async_copy(cov.at[0, 0, part], blocks.at[part], block_sems.at[i])

    copies = fetch_index((rows_hbm, cols_hbm), (slot_rows, slot_cols), index_sems)
    load = pltpu.make_async_copy(right_hbm, right, right_sem)
    load.start()
    live = count[0, 0]
    for i in range(slots // GROUP):
        @pl.when(i * GROUP < live)
        def _():
            block_copy(i).start()
    total[...] = jnp.zeros_like(total)
    load.wait()
    for tile in range(right.shape[1] // tile_size):
        load_pair(pairs, tile, right[:, tile * tile_size:(tile + 1) * tile_size])
    for copy in copies:
        copy.wait()
    add_blocks(blocks, slot_rows, slot_cols, live, pairs, total, True, lambda i: block_copy(i).wait())


def mirror_second_kernel(rows_any, cols_any, count, near, blocks, total, *scratch):
    slot_rows, slot_cols, pairs, index_sems = scratch
    tile_size = blocks.shape[1]
    copies = fetch_index((rows_any, cols_any), (slot_rows, slot_cols), index_sems)
    total[...] = jnp.zeros_like(total)
    for tile in range(near.shape[1] // tile_size):
        load_pair(pairs, tile, near[:, tile * tile_size:(tile + 1) * tile_size])
    for copy in copies:
        copy.wait()
    add_blocks(blocks, slot_rows, slot_cols, count[0, 0], pairs, total, True)


def finish_direct(total, near, noise, stat, n):
    value = near[...]
    rhs = value.shape[0]
    square = value * value
    share = 1.0 / n
    bend = share * row_sums(square * noise[...]) + 2.0 * cross_sums(total, value)
    stat[...] = pack_stats([share * row_sums(square), bend], rhs)


def direct_first_kernel(n, rows_any, cols_any, count, noise, blocks, near, current, twin, total, stat, far, *scratch):
    slot_rows, slot_cols, pairs, index_sems = scratch
    tile_size = blocks.shape[1]
    pieces = tile_size // LANES
    copies = fetch_index((rows_any, cols_any), (slot_rows, slot_cols), index_sems)
    odd = (lax.axis_index("row") ^ lax.axis_index("col")) & 1
    for o, source in enumerate((current, twin)):
        @pl.when(odd == o)
        def _():
            for tile in range(near.shape[1] // tile_size):
                value = source[:, tile * tile_size:(tile + 1) * tile_size]
                load_pair(pairs, tile, value)
                for i in range(pieces):
                    far[tile * pieces + i] = value[:, i * LANES:(i + 1) * LANES]
    total[...] = jnp.zeros_like(total)
    for copy in copies:
        copy.wait()
    add_blocks(blocks, slot_rows, slot_cols, count[0, 0], pairs, total, False)
    finish_direct(total, near, noise, stat, n)


def direct_second_kernel(n, rows_any, cols_any, count, noise, blocks, near, held, twin, total, stat, *scratch):
    slot_rows, slot_cols, pairs, index_sems = scratch
    tile_size = blocks.shape[1]
    pieces = tile_size // LANES
    per = held.shape[0] // n
    copies = fetch_index((rows_any, cols_any), (slot_rows, slot_cols), index_sems)
    row = lax.axis_index("row")
    offset = row ^ lax.axis_index("col")
    for tile in range(near.shape[1] // tile_size):
        value = []
        for i in range(tile * pieces, (tile + 1) * pieces):
            own = jnp.logical_or(offset == 0, jnp.logical_and(offset >= 2, ((i // per) ^ row) & 1 == 0))
            value.append(jnp.where(own, held[i], twin[i]))
        load_pair(pairs, tile, jnp.concatenate(value, axis=1))
    total[...] = jnp.zeros_like(total)
    for copy in copies:
        copy.wait()
    add_blocks(blocks, slot_rows, slot_cols, count[0, 0], pairs, total, False)
    finish_direct(total, near, noise, stat, n)


def add_kernel(one, two, *refs):
    refs[-1][...] = one[...] + two[...]


def pick_kernel(b, current, arrived, mark, out):
    there = (lax.axis_index("row") ^ lax.axis_index("col")) & b
    out[...] = jnp.where(there != 0, arrived[...], current[...])


def split_kernel(n, mirror, twin, mark, *outs):
    per = mirror.shape[0] // n
    rhs = mirror.shape[1]
    row = lax.axis_index("row")
    for j, out in enumerate(outs):
        first = (row ^ 2 * j) * per
        for i in range(per):
            out[i * rhs:(i + 1) * rhs, :] = mirror[first + i] + twin[first + i]


def merge_kernel(n, direct, mirror, twin, stat, *outs):
    per = direct.shape[0] // n
    rhs = direct.shape[1]
    me = lax.axis_index("col")
    diagonal = lax.axis_index("row") == me
    outs[n][...] = stat[...]
    for d, out in zip([0] + distances(n), outs):
        first = (me ^ d) * per

        @pl.when(diagonal)
        def _():
            for i in range(per):
                out[i * rhs:(i + 1) * rhs, :] = direct[first + i] + (mirror[first + i] + twin[first + i])

        @pl.when(jnp.logical_not(diagonal))
        def _():
            for i in range(per):
                out[i * rhs:(i + 1) * rhs, :] = direct[first + i]


def combine_kernel(n, near, noise, stat, *refs):
    parts, others, chunk = refs[:n], refs[n:-1], refs[-1]
    rhs = near.shape[0]
    data = parts[0].shape[0]
    per = data // rhs
    me = lax.axis_index("col")
    group = (lax.axis_index("row") ^ me) // 2
    value = tree_sum(ref[...] for ref in parts)
    for j, other in enumerate(others):
        value += jnp.where(group == j, 0.0, other[...])
    chunk[:data, :] = value
    chunk[data:, :] = stat[...]
    for k in range(n):
        @pl.when(me == k)
        def _():
            for i in range(per):
                lanes = slice((k * per + i) * LANES, (k * per + i + 1) * LANES)
                chunk[i * rhs:(i + 1) * rhs, :] += near[:, lanes] * noise[:, lanes]


def left_kernel(n, right, far, *refs):
    parts, others, (left, stat, held) = refs[:n], refs[n:-3], refs[-3:]
    rhs, width = right.shape
    data = parts[0].shape[0] - 8
    per = data // rhs
    row, me = lax.axis_index("row"), lax.axis_index("col")
    diagonal = (row ^ me) < 2
    both = stat_sum(parts, data)
    stat[...] = both
    size_now = unpack_stat(both, 0, rhs) / unpack_stat(both, 1, rhs)
    for i in range(width // LANES):
        lanes = slice(i * LANES, (i + 1) * LANES)
        value = right[:, lanes] - size_now * image_part(parts, me, i, per, rhs)
        left[:, lanes] = value
        held[i] = value

    @pl.when(jnp.logical_not(diagonal))
    def _():
        for j, other in enumerate(others):
            first = (row ^ 2 * j) * per
            for i in range(per):
                held[first + i] = far[first + i] - size_now * other[i * rhs:(i + 1) * rhs, :]


def last_kernel(right, left, stat_now, *refs):
    parts, (solution, residual) = refs[:-2], refs[-2:]
    rhs, width = right.shape
    data = parts[0].shape[0] - 8
    per = data // rhs
    me = lax.axis_index("col")
    both = stat_sum(parts, data)
    norm = unpack_stat(stat_now[...], 0, rhs)
    norm_next = unpack_stat(both, 0, rhs)
    size_now = norm / unpack_stat(stat_now[...], 1, rhs)
    ratio = norm_next / norm
    size_next = norm_next / (unpack_stat(both, 1, rhs) - ratio * norm_next / size_now)
    back = ratio / size_now
    for i in range(width // LANES):
        lanes = slice(i * LANES, (i + 1) * LANES)
        first = right[:, lanes]
        now = left[:, lanes]
        solution[:, lanes] = size_now * first + size_next * (now + ratio * first)
        image = image_part(parts, me, i, per, rhs) + back * (first - now)
        residual[:, lanes] = now - size_next * image


def shape_of(*shape):
    return jax.ShapeDtypeStruct(shape, F32)


def on_device(n, right_sides, nugget, cov_blocks, block_rows, block_cols, block_count):
    rhs, width = right_sides.shape
    slots, tile_size = cov_blocks.shape[2:4]
    per = width // n // LANES
    data = per * rhs
    size = data + 8
    noise = nugget.reshape(1, width)
    index = (block_rows, block_cols, block_count)
    pair = pltpu.VMEM((width // tile_size, 2 * rhs, tile_size), BF16)
    index_scratch = [pltpu.SMEM(item.shape, item.dtype) for item in index[:2]]
    index_sems = pltpu.SemaphoreType.DMA((2,))
    vmem = pl.BlockSpec(memory_space=pltpu.VMEM)
    any_spec = pl.BlockSpec(memory_space=pl.ANY)
    smem = pl.BlockSpec(memory_space=pltpu.SMEM)
    hbm = pl.BlockSpec(memory_space=pltpu.HBM)
    params = pltpu.CompilerParams(vmem_limit_bytes=16 * 1024 * 1024)
    cost = pl.CostEstimate(flops=4 * rhs * slots * tile_size * tile_size, transcendentals=0,
                           bytes_accessed=2 * slots * tile_size * tile_size)
    field = shape_of(rhs, width)
    total = shape_of(width // LANES, rhs, LANES)
    chunk = shape_of(data, LANES)
    tile = shape_of(8, LANES)
    loaded = shape_of(size, LANES)

    def call(kernel, name, specs, outs, scratch, args, heavy=False):
        return pl.pallas_call(
            kernel,
            in_specs=specs,
            out_specs=jax.tree.map(lambda _: vmem, outs),
            out_shape=outs,
            scratch_shapes=scratch,
            compiler_params=params,
            cost_estimate=cost if heavy else None,
            name=name,
        )(*args)

    in_hbm = functools.partial(pltpu.with_memory_space_constraint, memory_space=pltpu.HBM)
    kernel_index = index_scratch + [pair, index_sems]

    def gathered(near, mirror, twin, direct, stat):
        sent = call(functools.partial(split_kernel, n), "split", [vmem] * 3, [chunk] * (n // 2), [],
                    (mirror, twin, stat))
        others = [moved(value, n, far_source(j, n)) for j, value in enumerate(sent)]
        merged = call(functools.partial(merge_kernel, n), "merge", [vmem] * 4, [chunk] * n + [tile], [],
                      (direct, mirror, twin, stat))
        parts = [merged[0]] + [shifted(value, "col", d, n) for d, value in zip(distances(n), merged[1:n])]
        stat = merged[n]
        for b in bits(n):
            stat, = call(add_kernel, "add_stat", [vmem] * (2 + n // 2), [tile], [],
                         (stat, shifted(stat, "row", b, n), *others))
        own, = call(functools.partial(combine_kernel, n), "combine", [vmem] * (3 + n + n // 2), [loaded], [],
                    (near, noise, stat, *parts, *others))
        return [own] + [shifted(own, "col", d, n) for d in distances(n)]

    current = right_sides
    for b in bits(n)[:0:-1]:
        arrived = moved(current, n, spread_target(b))
        if b == n // 2:
            mirror, blocks = call(
                mirror_first_kernel, "mirror_first", [hbm] * 2 + [smem] + [hbm] * 2,
                [total, jax.ShapeDtypeStruct(cov_blocks.shape[2:], cov_blocks.dtype)],
                index_scratch + [pltpu.VMEM((rhs, width), F32), pair, index_sems,
                                 pltpu.SemaphoreType.DMA, pltpu.SemaphoreType.DMA((slots // GROUP,))],
                (*map(in_hbm, index[:2]), block_count, in_hbm(right_sides), in_hbm(cov_blocks)), True)
            twin_mirror = shifted(mirror, "row", 1, n)
        current, = call(functools.partial(pick_kernel, b), "pick", [vmem] * 3, [field], [], (current, arrived, mirror))
    twin = shifted(current, "row", 1, n)
    direct, stat, far = call(
        functools.partial(direct_first_kernel, n), "direct_first", [any_spec] * 2 + [smem] + [vmem] * 5,
        [total, tile, total], kernel_index, (*index, noise, blocks, right_sides, current, twin), True)
    parts = gathered(right_sides, mirror, twin_mirror, direct, stat)
    far_parts = [moved(parts[0], n, far_target(j)) for j in range(n // 2)]

    left, stat_now, held = call(
        functools.partial(left_kernel, n), "left", [vmem] * (2 + n + n // 2), [field, tile, total], [],
        (right_sides, far, *parts, *far_parts))
    twin = shifted(held, "row", 1, n)
    mirror, = call(mirror_second_kernel, "mirror_second", [any_spec] * 2 + [smem] + [vmem] * 2,
                   [total], kernel_index, (*index, left, blocks), True)
    twin_mirror = shifted(mirror, "row", 1, n)
    direct, stat = call(
        functools.partial(direct_second_kernel, n), "direct_second", [any_spec] * 2 + [smem] + [vmem] * 5,
        [total, tile], kernel_index, (*index, noise, blocks, left, held, twin), True)
    parts = gathered(left, mirror, twin_mirror, direct, stat)
    return tuple(call(last_kernel, "last", [vmem] * (n + 3), [field, field], [],
                      (right_sides, left, stat_now, *parts)))


def solution(mesh):
    n = mesh.shape["row"]
    assert n == mesh.shape["col"] and n & (n - 1) == 0 and n >= 4
    placed = (
        P(None, ("groups", "row")),
        P(("groups", "row")),
        P(("groups", "row"), "col", None, None, None),
        P(("groups", "row"), "col", None),
        P(("groups", "row"), "col", None),
        P(("groups", "row"), "col"),
    )
    return jax.shard_map(
        functools.partial(on_device, n),
        mesh=mesh,
        in_specs=placed,
        out_specs=(P(None, ("groups", "row")), P(None, ("groups", "row"))),
        check_vma=False,
    )
```

```python
import functools

import jax
import jax.numpy as jnp
from jax import lax
from jax.experimental import pallas as pl
from jax.experimental.pallas import tpu as pltpu
from jax.sharding import PartitionSpec as P

ITERS = 2
LANES = 128
GROUP = 8
BF16 = jnp.bfloat16
F32 = jnp.float32


def shifted(value, axis, d, n):
    return lax.ppermute(value, axis, [(i, i ^ d) for i in range(n)])


def distances(n):
    return [d for d in range(n) if d > 1] + [1]


def moved(value, n, target):
    pairs = [(r * n + c, target(r, c)) for r in range(n) for c in range(n)]
    return lax.ppermute(value, ("row", "col"), [(s, t[0] * n + t[1]) for s, t in pairs])


def far_target(j):
    def target(r, c):
        d = r ^ c
        if d ^ 2 * j >= 2:
            return c ^ 2 * j, r
        return c ^ (d & 1) ^ (j == 0), c

    return target


def far_source(j, n):
    back = {far_target(j)(r, c): (r, c) for r in range(n) for c in range(n)}
    return lambda r, c: back[r, c]


def spread_target(b):
    def target(r, c):
        o = r ^ c
        move = {0: b, b: 1, b + 1: b, 1: 1}.get(o % (2 * b), 1)
        return r ^ move, c

    return target


def bits(n):
    return [1 << i for i in range(n.bit_length() - 1)]


def load_pair(dst, tile, value):
    rhs = value.shape[0]
    high = value.astype(BF16)
    dst[tile, :rhs, :] = high
    dst[tile, rhs:, :] = (value - high.astype(F32)).astype(BF16)


def product(pair, block, contract):
    both = lax.dot_general(pair, block, (((1,), (contract,)), ((), ())), preferred_element_type=F32)
    rhs = both.shape[0] // 2
    return both[:rhs] + both[rhs:]


def pack_stats(columns, rhs):
    lane = lax.broadcasted_iota(jnp.int32, (8, LANES), 1)
    tile = jnp.zeros((8, LANES), F32)
    groups = rhs // 8
    for i, column in enumerate(columns):
        for g in range(groups):
            tile = jnp.where(lane == i * groups + g, column[g * 8:(g + 1) * 8], tile)
    return tile


def unpack_stat(tile, i, rhs):
    groups = rhs // 8
    return jnp.concatenate([tile[:, i * groups + g:i * groups + g + 1] for g in range(groups)], axis=0)


def accumulate(total, tile, value):
    width = value.shape[1] // LANES
    for part in range(width):
        total[tile * width + part] += value[:, part * LANES:(part + 1) * LANES]


def wide_group(blocks):
    return 2 * GROUP if blocks.shape[0] % (2 * GROUP) == 0 else GROUP


def add_blocks(blocks, slot_rows, slot_cols, live, pairs, total, mirror, group, ready=None):
    read, write, contract = (slot_rows, slot_cols, 0) if mirror else (slot_cols, slot_rows, 1)

    def body(step, carry):
        if ready is not None:
            ready(step)
        for g in range(group):
            slot = step * group + g
            value = product(pairs[read[0, 0, slot]], blocks[slot], contract)
            accumulate(total, write[0, 0, slot], jnp.where(slot < live, value, 0.0))
        return carry

    lax.fori_loop(0, (live + group - 1) // group, body, 0)


def image_part(parts, me, i, per, rhs):
    rows = slice((i % per) * rhs, (i % per + 1) * rhs)
    value = parts[0][rows, :]
    for d, part in zip(distances(len(parts))[::-1], parts[1:]):
        value = jnp.where(me ^ d == i // per, part[rows, :], value)
    return value


def row_sums(value):
    return jnp.sum(value, axis=1, keepdims=True)


def cross_sums(total, value):
    rhs = value.shape[0]
    cross = jnp.zeros((rhs, LANES), F32)
    for i in range(total.shape[0]):
        cross += total[i] * value[:, i * LANES:(i + 1) * LANES]
    return row_sums(cross)


def tree_sum(values):
    values = list(values)
    while len(values) > 1:
        values = [a + b for a, b in zip(values[::2], values[1::2])]
    return values[0]


def stat_sum(parts, data):
    order = [0] + distances(len(parts))[::-1]
    return tree_sum(parts[order.index(d)][data:, :] for d in range(len(parts)))


def fetch_index(sources, targets, sems):
    copies = [pltpu.make_async_copy(s, t, sems.at[i]) for i, (s, t) in enumerate(zip(sources, targets))]
    for copy in copies:
        copy.start()
    return copies


def mirror_first_kernel(rows_hbm, cols_hbm, count, right_hbm, cov, total, blocks, *scratch):
    slot_rows, slot_cols, right, pairs, index_sems, right_sem, block_sems = scratch
    slots, tile_size = blocks.shape[:2]

    def block_copy(i):
        part = pl.ds(i * GROUP, GROUP)
        return pltpu.make_async_copy(cov.at[0, 0, part], blocks.at[part], block_sems.at[i])

    copies = fetch_index((rows_hbm, cols_hbm), (slot_rows, slot_cols), index_sems)
    load = pltpu.make_async_copy(right_hbm, right, right_sem)
    load.start()
    live = count[0, 0]
    for i in range(slots // GROUP):
        @pl.when(i * GROUP < live)
        def _():
            block_copy(i).start()
    total[...] = jnp.zeros_like(total)
    load.wait()
    for tile in range(right.shape[1] // tile_size):
        load_pair(pairs, tile, right[:, tile * tile_size:(tile + 1) * tile_size])
    for copy in copies:
        copy.wait()
    add_blocks(blocks, slot_rows, slot_cols, live, pairs, total, True, GROUP, lambda i: block_copy(i).wait())


def mirror_second_kernel(rows_any, cols_any, count, near, blocks, total, *scratch):
    slot_rows, slot_cols, pairs, index_sems = scratch
    tile_size = blocks.shape[1]
    copies = fetch_index((rows_any, cols_any), (slot_rows, slot_cols), index_sems)
    total[...] = jnp.zeros_like(total)
    for tile in range(near.shape[1] // tile_size):
        load_pair(pairs, tile, near[:, tile * tile_size:(tile + 1) * tile_size])
    for copy in copies:
        copy.wait()
    add_blocks(blocks, slot_rows, slot_cols, count[0, 0], pairs, total, True, wide_group(blocks))


def finish_direct(total, near, noise, stat, n):
    value = near[...]
    rhs = value.shape[0]
    square = value * value
    share = 1.0 / n
    bend = share * row_sums(square * noise[...]) + 2.0 * cross_sums(total, value)
    stat[...] = pack_stats([share * row_sums(square), bend], rhs)


def direct_first_kernel(n, rows_any, cols_any, count, noise, blocks, near, current, twin, mark, total, stat, far, *scratch):
    slot_rows, slot_cols, pairs, index_sems = scratch
    tile_size = blocks.shape[1]
    pieces = tile_size // LANES
    copies = fetch_index((rows_any, cols_any), (slot_rows, slot_cols), index_sems)
    odd = (lax.axis_index("row") ^ lax.axis_index("col")) & 1
    for o, source in enumerate((current, twin)):
        @pl.when(odd == o)
        def _():
            for tile in range(near.shape[1] // tile_size):
                value = source[:, tile * tile_size:(tile + 1) * tile_size]
                load_pair(pairs, tile, value)
                for i in range(pieces):
                    far[tile * pieces + i] = value[:, i * LANES:(i + 1) * LANES]
    total[...] = jnp.zeros_like(total)
    for copy in copies:
        copy.wait()
    add_blocks(blocks, slot_rows, slot_cols, count[0, 0], pairs, total, False, wide_group(blocks))
    finish_direct(total, near, noise, stat, n)


def direct_second_kernel(n, rows_any, cols_any, count, noise, blocks, near, held, twin, mark, total, stat, *scratch):
    slot_rows, slot_cols, pairs, index_sems = scratch
    tile_size = blocks.shape[1]
    pieces = tile_size // LANES
    per = held.shape[0] // n
    copies = fetch_index((rows_any, cols_any), (slot_rows, slot_cols), index_sems)
    row = lax.axis_index("row")
    offset = row ^ lax.axis_index("col")
    for tile in range(near.shape[1] // tile_size):
        value = []
        for i in range(tile * pieces, (tile + 1) * pieces):
            own = jnp.logical_or(offset == 0, jnp.logical_and(offset >= 2, ((i // per) ^ row) & 1 == 0))
            value.append(jnp.where(own, held[i], twin[i]))
        load_pair(pairs, tile, jnp.concatenate(value, axis=1))
    total[...] = jnp.zeros_like(total)
    for copy in copies:
        copy.wait()
    add_blocks(blocks, slot_rows, slot_cols, count[0, 0], pairs, total, False, wide_group(blocks))
    finish_direct(total, near, noise, stat, n)


def add_kernel(one, two, *refs):
    refs[-1][...] = one[...] + two[...]


def pick_kernel(b, current, arrived, mark, out):
    there = (lax.axis_index("row") ^ lax.axis_index("col")) & b
    out[...] = jnp.where(there != 0, arrived[...], current[...])


def split_kernel(n, mirror, twin, *outs):
    per = mirror.shape[0] // n
    rhs = mirror.shape[1]
    row = lax.axis_index("row")
    for j, out in enumerate(outs):
        first = (row ^ 2 * j) * per
        for i in range(per):
            out[i * rhs:(i + 1) * rhs, :] = mirror[first + i] + twin[first + i]


def merge_kernel(n, direct, mirror, twin, stat, *outs):
    per = direct.shape[0] // n
    rhs = direct.shape[1]
    me = lax.axis_index("col")
    diagonal = lax.axis_index("row") == me
    outs[n][...] = stat[...]
    for d, out in zip([0] + distances(n), outs):
        first = (me ^ d) * per

        @pl.when(diagonal)
        def _():
            for i in range(per):
                out[i * rhs:(i + 1) * rhs, :] = direct[first + i] + (mirror[first + i] + twin[first + i])

        @pl.when(jnp.logical_not(diagonal))
        def _():
            for i in range(per):
                out[i * rhs:(i + 1) * rhs, :] = direct[first + i]


def combine_kernel(n, near, noise, stat, *refs):
    parts, others, chunk = refs[:n], refs[n:-1], refs[-1]
    rhs = near.shape[0]
    data = parts[0].shape[0]
    per = data // rhs
    me = lax.axis_index("col")
    group = (lax.axis_index("row") ^ me) // 2
    value = tree_sum(ref[...] for ref in parts)
    for j, other in enumerate(others):
        value += jnp.where(group == j, 0.0, other[...])
    chunk[:data, :] = value
    chunk[data:, :] = stat[...]
    for k in range(n):
        @pl.when(me == k)
        def _():
            for i in range(per):
                lanes = slice((k * per + i) * LANES, (k * per + i + 1) * LANES)
                chunk[i * rhs:(i + 1) * rhs, :] += near[:, lanes] * noise[:, lanes]


def left_kernel(right, *refs):
    parts, (left, stat) = refs[:-2], refs[-2:]
    rhs, width = right.shape
    data = parts[0].shape[0] - 8
    per = data // rhs
    me = lax.axis_index("col")
    both = stat_sum(parts, data)
    stat[...] = both
    size_now = unpack_stat(both, 0, rhs) / unpack_stat(both, 1, rhs)
    for i in range(width // LANES):
        lanes = slice(i * LANES, (i + 1) * LANES)
        left[:, lanes] = right[:, lanes] - size_now * image_part(parts, me, i, per, rhs)


def held_kernel(n, left, stat, far, mark, *refs):
    parts, held = refs[:-1], refs[-1]
    rhs = left.shape[0]
    per = held.shape[0] // n
    row = lax.axis_index("row")
    diagonal = (row ^ lax.axis_index("col")) < 2
    size_now = unpack_stat(stat[...], 0, rhs) / unpack_stat(stat[...], 1, rhs)

    @pl.when(diagonal)
    def _():
        for i in range(held.shape[0]):
            held[i] = left[:, i * LANES:(i + 1) * LANES]

    @pl.when(jnp.logical_not(diagonal))
    def _():
        for j, part in zip(range(n // 2)[::-1], parts):
            first = (row ^ 2 * j) * per
            for i in range(per):
                held[first + i] = far[first + i] - size_now * part[i * rhs:(i + 1) * rhs, :]


def last_kernel(n, right, left, stat_now, *refs):
    parts, (solution_out, residual_out, solution, residual, sems) = refs[:n], refs[n:]
    rhs, width = right.shape
    data = parts[0].shape[0] - 8
    per = data // rhs
    me = lax.axis_index("col")
    both = stat_sum(parts, data)
    norm = unpack_stat(stat_now[...], 0, rhs)
    norm_next = unpack_stat(both, 0, rhs)
    size_now = norm / unpack_stat(stat_now[...], 1, rhs)
    ratio = norm_next / norm
    size_next = norm_next / (unpack_stat(both, 1, rhs) - ratio * norm_next / size_now)
    back = ratio / size_now
    copies = []
    groups = 4
    count = width // LANES // groups
    for group in range(groups):
        for i in range(group * count, (group + 1) * count):
            lanes = slice(i * LANES, (i + 1) * LANES)
            first = right[:, lanes]
            now = left[:, lanes]
            solution[:, lanes] = size_now * first + size_next * (now + ratio * first)
            image = image_part(parts, me, i, per, rhs) + back * (first - now)
            residual[:, lanes] = now - size_next * image
        lanes = pl.ds(group * count * LANES, count * LANES)
        for k, (source, target) in enumerate(((solution, solution_out), (residual, residual_out))):
            copies.append(pltpu.make_async_copy(source.at[:, lanes], target.at[:, lanes], sems.at[k, group]))
            copies[-1].start()
    for copy in copies:
        copy.wait()


def shape_of(*shape):
    return jax.ShapeDtypeStruct(shape, F32)


def on_device(n, right_sides, nugget, cov_blocks, block_rows, block_cols, block_count):
    rhs, width = right_sides.shape
    slots, tile_size = cov_blocks.shape[2:4]
    per = width // n // LANES
    data = per * rhs
    size = data + 8
    noise = nugget.reshape(1, width)
    index = (block_rows, block_cols, block_count)
    pair = pltpu.VMEM((width // tile_size, 2 * rhs, tile_size), BF16)
    index_scratch = [pltpu.SMEM(item.shape, item.dtype) for item in index[:2]]
    index_sems = pltpu.SemaphoreType.DMA((2,))
    vmem = pl.BlockSpec(memory_space=pltpu.VMEM)
    any_spec = pl.BlockSpec(memory_space=pl.ANY)
    smem = pl.BlockSpec(memory_space=pltpu.SMEM)
    hbm = pl.BlockSpec(memory_space=pltpu.HBM)
    params = pltpu.CompilerParams(vmem_limit_bytes=16 * 1024 * 1024)
    cost = pl.CostEstimate(flops=4 * rhs * slots * tile_size * tile_size, transcendentals=0,
                           bytes_accessed=2 * slots * tile_size * tile_size)
    field = shape_of(rhs, width)
    total = shape_of(width // LANES, rhs, LANES)
    chunk = shape_of(data, LANES)
    tile = shape_of(8, LANES)
    loaded = shape_of(size, LANES)

    def call(kernel, name, specs, outs, scratch, args, heavy=False):
        return pl.pallas_call(
            kernel,
            in_specs=specs,
            out_specs=jax.tree.map(lambda _: vmem, outs),
            out_shape=outs,
            scratch_shapes=scratch,
            compiler_params=params,
            cost_estimate=cost if heavy else None,
            name=name,
        )(*args)

    in_hbm = functools.partial(pltpu.with_memory_space_constraint, memory_space=pltpu.HBM)
    kernel_index = index_scratch + [pair, index_sems]

    def to_owners(mirror, twin):
        sent = call(functools.partial(split_kernel, n), "split", [vmem] * 2, [chunk] * (n // 2), [], (mirror, twin))
        return [moved(value, n, far_source(j, n)) for j, value in enumerate(sent)], sent[0]

    def gathered(near, mirror, twin, others, direct, stat):
        merged = call(functools.partial(merge_kernel, n), "merge", [vmem] * 4, [chunk] * n + [tile], [],
                      (direct, mirror, twin, stat))
        parts = [merged[0]] + [shifted(value, "col", d, n) for d, value in zip(distances(n), merged[1:n])]
        stat = merged[n]
        for b in bits(n):
            stat, = call(add_kernel, "add_stat", [vmem] * (2 + n // 2), [tile], [],
                         (stat, shifted(stat, "row", b, n), *others))
        own, = call(functools.partial(combine_kernel, n), "combine", [vmem] * (3 + n + n // 2), [loaded], [],
                    (near, noise, stat, *parts, *others))
        return [own] + [shifted(own, "col", d, n) for d in distances(n)[::-1]]

    current = right_sides
    for b in bits(n)[:0:-1]:
        arrived = moved(current, n, spread_target(b))
        if b == n // 2:
            mirror, blocks = call(
                mirror_first_kernel, "mirror_first", [hbm] * 2 + [smem] + [hbm] * 2,
                [total, jax.ShapeDtypeStruct(cov_blocks.shape[2:], cov_blocks.dtype)],
                index_scratch + [pltpu.VMEM((rhs, width), F32), pair, index_sems,
                                 pltpu.SemaphoreType.DMA, pltpu.SemaphoreType.DMA((slots // GROUP,))],
                (*map(in_hbm, index[:2]), block_count, in_hbm(right_sides), in_hbm(cov_blocks)), True)
            twin_mirror = shifted(mirror, "row", 1, n)
        current, = call(functools.partial(pick_kernel, b), "pick", [vmem] * 3, [field], [], (current, arrived, mirror))
    twin = shifted(current, "row", 1, n)
    others, mark = to_owners(mirror, twin_mirror)
    direct, stat, far = call(
        functools.partial(direct_first_kernel, n), "direct_first", [any_spec] * 2 + [smem] + [vmem] * 6,
        [total, tile, total], kernel_index, (*index, noise, blocks, right_sides, current, twin, mark), True)
    parts = gathered(right_sides, mirror, twin_mirror, others, direct, stat)
    far_parts = [moved(parts[0], n, far_target(j)) for j in range(n // 2)[::-1]]

    left, stat_now = call(left_kernel, "left", [vmem] * (n + 1), [field, tile], [], (right_sides, *parts))
    mirror, = call(mirror_second_kernel, "mirror_second", [any_spec] * 2 + [smem] + [vmem] * 2,
                   [total], kernel_index, (*index, left, blocks), True)
    twin_mirror = shifted(mirror, "row", 1, n)
    held, = call(functools.partial(held_kernel, n), "held", [vmem] * (4 + n // 2), [total], [],
                 (left, stat_now, far, mirror, *far_parts))
    twin = shifted(held, "row", 1, n)
    others, mark = to_owners(mirror, twin_mirror)
    direct, stat = call(
        functools.partial(direct_second_kernel, n), "direct_second", [any_spec] * 2 + [smem] + [vmem] * 6,
        [total, tile], kernel_index, (*index, noise, blocks, left, held, twin, mark), True)
    parts = gathered(left, mirror, twin_mirror, others, direct, stat)
    return tuple(pl.pallas_call(
        functools.partial(last_kernel, n),
        in_specs=[vmem] * (n + 3),
        out_specs=[any_spec] * 2,
        out_shape=[field, field],
        scratch_shapes=[pltpu.VMEM((rhs, width), F32), pltpu.VMEM((rhs, width), F32), pltpu.SemaphoreType.DMA((2, 4))],
        compiler_params=params,
        name="last",
    )(right_sides, left, stat_now, *parts))


def solution(mesh):
    n = mesh.shape["row"]
    assert n == mesh.shape["col"] and n & (n - 1) == 0 and n >= 4
    placed = (
        P(None, ("groups", "row")),
        P(("groups", "row")),
        P(("groups", "row"), "col", None, None, None),
        P(("groups", "row"), "col", None),
        P(("groups", "row"), "col", None),
        P(("groups", "row"), "col"),
    )
    return jax.shard_map(
        functools.partial(on_device, n),
        mesh=mesh,
        in_specs=placed,
        out_specs=(P(None, ("groups", "row")), P(None, ("groups", "row"))),
        check_vma=False,
    )
```

```python
import functools

import jax
import jax.numpy as jnp
from jax import lax
from jax.experimental import pallas as pl
from jax.experimental.pallas import tpu as pltpu
from jax.sharding import PartitionSpec as P

ITERS = 2
LANES = 128
GROUP = 8
BF16 = jnp.bfloat16
F32 = jnp.float32


def shifted(value, axis, d, n):
    return lax.ppermute(value, axis, [(i, i ^ d) for i in range(n)])


def distances(row, n):
    even = [d for d in range(n) if d > 1] + [1]
    odd = [1] + [d for d in range(n) if d > 1]
    return [e + (o - e) * (row & 1) for e, o in zip(even, odd)]


def along_line(values, n):
    return [moved(value, n, lambda r, c: (r, c ^ distances(r, n)[i])) for i, value in enumerate(values)]


def moved(value, n, target):
    pairs = [(r * n + c, target(r, c)) for r in range(n) for c in range(n)]
    return lax.ppermute(value, ("row", "col"), [(s, t[0] * n + t[1]) for s, t in pairs])


def far_target(j):
    def target(r, c):
        d = r ^ c
        if d ^ 2 * j >= 2:
            return c ^ 2 * j, r
        return c ^ (d & 1) ^ (j == 0), c

    return target


def far_source(j, n):
    back = {far_target(j)(r, c): (r, c) for r in range(n) for c in range(n)}
    return lambda r, c: back[r, c]


def spread_target(b):
    def target(r, c):
        o = r ^ c
        move = {0: b, b: 1, b + 1: b, 1: 1}.get(o % (2 * b), 1)
        return r ^ move, c

    return target


def bits(n):
    return [1 << i for i in range(n.bit_length() - 1)]


def load_pair(dst, tile, value):
    rhs = value.shape[0]
    high = value.astype(BF16)
    dst[tile, :rhs, :] = high
    dst[tile, rhs:, :] = (value - high.astype(F32)).astype(BF16)


def product(pair, block, contract):
    both = lax.dot_general(pair, block, (((1,), (contract,)), ((), ())), preferred_element_type=F32)
    rhs = both.shape[0] // 2
    return both[:rhs] + both[rhs:]


def pack_stats(columns, rhs):
    lane = lax.broadcasted_iota(jnp.int32, (8, LANES), 1)
    tile = jnp.zeros((8, LANES), F32)
    groups = rhs // 8
    for i, column in enumerate(columns):
        for g in range(groups):
            tile = jnp.where(lane == i * groups + g, column[g * 8:(g + 1) * 8], tile)
    return tile


def unpack_stat(tile, i, rhs):
    groups = rhs // 8
    return jnp.concatenate([tile[:, i * groups + g:i * groups + g + 1] for g in range(groups)], axis=0)


def accumulate(total, tile, value):
    width = value.shape[1] // LANES
    for part in range(width):
        total[tile * width + part] += value[:, part * LANES:(part + 1) * LANES]


def wide_group(blocks):
    return 2 * GROUP if blocks.shape[0] % (2 * GROUP) == 0 else GROUP


def add_blocks(blocks, slot_rows, slot_cols, live, pairs, total, mirror, group, ready=None):
    read, write, contract = (slot_rows, slot_cols, 0) if mirror else (slot_cols, slot_rows, 1)

    def body(step, carry):
        if ready is not None:
            ready(step)
        for g in range(group):
            slot = step * group + g
            value = product(pairs[read[0, 0, slot]], blocks[slot], contract)
            accumulate(total, write[0, 0, slot], jnp.where(slot < live, value, 0.0))
        return carry

    lax.fori_loop(0, (live + group - 1) // group, body, 0)


def image_part(parts, i, per, rhs):
    row, me = lax.axis_index("row"), lax.axis_index("col")
    rows = slice((i % per) * rhs, (i % per + 1) * rhs)
    value = parts[0][rows, :]
    for d, part in zip(distances(row, len(parts))[::-1], parts[1:]):
        value = jnp.where(me ^ d == i // per, part[rows, :], value)
    return value


def row_sums(value):
    return jnp.sum(value, axis=1, keepdims=True)


def cross_sums(total, value):
    rhs = value.shape[0]
    cross = jnp.zeros((rhs, LANES), F32)
    for i in range(total.shape[0]):
        cross += total[i] * value[:, i * LANES:(i + 1) * LANES]
    return row_sums(cross)


def tree_sum(values):
    values = list(values)
    while len(values) > 1:
        values = [a + b for a, b in zip(values[::2], values[1::2])]
    return values[0]


def stat_sum(parts, data):
    odd = (lax.axis_index("row") & 1) == 1
    tiles = [part[data:, :] for part in parts]
    even_order = [tiles[0]] + tiles[:0:-1][-1:] + tiles[:0:-1][:-1]
    odd_order = [tiles[0]] + tiles[:0:-1]
    return jnp.where(odd, tree_sum(odd_order), tree_sum(even_order))


def fetch_index(sources, targets, sems):
    copies = [pltpu.make_async_copy(s, t, sems.at[i]) for i, (s, t) in enumerate(zip(sources, targets))]
    for copy in copies:
        copy.start()
    return copies


def mirror_first_kernel(rows_hbm, cols_hbm, count, right_hbm, cov, total, blocks, *scratch):
    slot_rows, slot_cols, right, pairs, index_sems, right_sem, block_sems = scratch
    slots, tile_size = blocks.shape[:2]

    def block_copy(i):
        part = pl.ds(i * GROUP, GROUP)
        return pltpu.make_async_copy(cov.at[0, 0, part], blocks.at[part], block_sems.at[i])

    copies = fetch_index((rows_hbm, cols_hbm), (slot_rows, slot_cols), index_sems)
    load = pltpu.make_async_copy(right_hbm, right, right_sem)
    load.start()
    live = count[0, 0]
    for i in range(slots // GROUP):
        @pl.when(i * GROUP < live)
        def _():
            block_copy(i).start()
    total[...] = jnp.zeros_like(total)
    load.wait()
    for tile in range(right.shape[1] // tile_size):
        load_pair(pairs, tile, right[:, tile * tile_size:(tile + 1) * tile_size])
    for copy in copies:
        copy.wait()
    add_blocks(blocks, slot_rows, slot_cols, live, pairs, total, True, GROUP, lambda i: block_copy(i).wait())


def mirror_second_kernel(rows_any, cols_any, count, near, blocks, total, *scratch):
    slot_rows, slot_cols, pairs, index_sems = scratch
    tile_size = blocks.shape[1]
    copies = fetch_index((rows_any, cols_any), (slot_rows, slot_cols), index_sems)
    total[...] = jnp.zeros_like(total)
    for tile in range(near.shape[1] // tile_size):
        load_pair(pairs, tile, near[:, tile * tile_size:(tile + 1) * tile_size])
    for copy in copies:
        copy.wait()
    add_blocks(blocks, slot_rows, slot_cols, count[0, 0], pairs, total, True, wide_group(blocks))


def finish_direct(total, near, noise, stat, n):
    value = near[...]
    rhs = value.shape[0]
    square = value * value
    share = 1.0 / n
    bend = share * row_sums(square * noise[...]) + 2.0 * cross_sums(total, value)
    stat[...] = pack_stats([share * row_sums(square), bend], rhs)


def direct_first_kernel(n, rows_any, cols_any, count, noise, blocks, near, current, twin, mark, total, stat, far, *scratch):
    slot_rows, slot_cols, pairs, index_sems = scratch
    tile_size = blocks.shape[1]
    pieces = tile_size // LANES
    copies = fetch_index((rows_any, cols_any), (slot_rows, slot_cols), index_sems)
    odd = (lax.axis_index("row") ^ lax.axis_index("col")) & 1
    for o, source in enumerate((current, twin)):
        @pl.when(odd == o)
        def _():
            for tile in range(near.shape[1] // tile_size):
                value = source[:, tile * tile_size:(tile + 1) * tile_size]
                load_pair(pairs, tile, value)
                for i in range(pieces):
                    far[tile * pieces + i] = value[:, i * LANES:(i + 1) * LANES]
    total[...] = jnp.zeros_like(total)
    for copy in copies:
        copy.wait()
    add_blocks(blocks, slot_rows, slot_cols, count[0, 0], pairs, total, False, wide_group(blocks))
    finish_direct(total, near, noise, stat, n)


def direct_second_kernel(n, rows_any, cols_any, count, noise, blocks, near, held, twin, mark, total, stat, *scratch):
    slot_rows, slot_cols, pairs, index_sems = scratch
    tile_size = blocks.shape[1]
    pieces = tile_size // LANES
    per = held.shape[0] // n
    copies = fetch_index((rows_any, cols_any), (slot_rows, slot_cols), index_sems)
    row = lax.axis_index("row")
    offset = row ^ lax.axis_index("col")
    for tile in range(near.shape[1] // tile_size):
        value = []
        for i in range(tile * pieces, (tile + 1) * pieces):
            own = jnp.logical_or(offset == 0, jnp.logical_and(offset >= 2, ((i // per) ^ row) & 1 == 0))
            value.append(jnp.where(own, held[i], twin[i]))
        load_pair(pairs, tile, jnp.concatenate(value, axis=1))
    total[...] = jnp.zeros_like(total)
    for copy in copies:
        copy.wait()
    add_blocks(blocks, slot_rows, slot_cols, count[0, 0], pairs, total, False, wide_group(blocks))
    finish_direct(total, near, noise, stat, n)


def add_kernel(one, two, *refs):
    refs[-1][...] = one[...] + two[...]


def pick_kernel(b, current, arrived, mark, out):
    there = (lax.axis_index("row") ^ lax.axis_index("col")) & b
    out[...] = jnp.where(there != 0, arrived[...], current[...])


def split_kernel(n, mirror, twin, *outs):
    per = mirror.shape[0] // n
    rhs = mirror.shape[1]
    row = lax.axis_index("row")
    for j, out in enumerate(outs):
        first = (row ^ 2 * j) * per
        for i in range(per):
            out[i * rhs:(i + 1) * rhs, :] = mirror[first + i] + twin[first + i]


def merge_kernel(n, direct, mirror, twin, stat, *outs):
    per = direct.shape[0] // n
    rhs = direct.shape[1]
    me = lax.axis_index("col")
    diagonal = lax.axis_index("row") == me
    if outs[n] is not None:
        outs[n][...] = stat[...]
    for d, out in zip([0] + distances(lax.axis_index("row"), n), outs):
        first = (me ^ d) * per

        @pl.when(diagonal)
        def _():
            for i in range(per):
                out[i * rhs:(i + 1) * rhs, :] = direct[first + i] + (mirror[first + i] + twin[first + i])

        @pl.when(jnp.logical_not(diagonal))
        def _():
            for i in range(per):
                out[i * rhs:(i + 1) * rhs, :] = direct[first + i]


def merge_last_kernel(n, direct, mirror, twin, stat, *outs):
    data = direct.shape[0] // n * direct.shape[1]
    merge_kernel(n, direct, mirror, twin, stat, *[out.at[:data] for out in outs], None)
    for out in outs:
        out[data:, :] = stat[...]


def pass_kernel(value, *refs):
    refs[-1][...] = value[...]


def combine_last_kernel(n, near, noise, *refs):
    parts, others, (chunk, stat) = refs[:n], refs[n:-2], refs[-2:]
    data = chunk.shape[0]
    stat[...] = tree_sum(ref[data:, :] for ref in parts)
    sum_chunk(near, noise, [ref.at[:data] for ref in parts], others, chunk)


def sum_chunk(near, noise, parts, others, chunk):
    rhs = near.shape[0]
    n = len(parts)
    data = parts[0].shape[0]
    per = data // rhs
    me = lax.axis_index("col")
    group = (lax.axis_index("row") ^ me) // 2
    value = tree_sum(ref[...] for ref in parts)
    for j, other in enumerate(others):
        value += jnp.where(group == j, 0.0, other[...])
    chunk[:data, :] = value
    for k in range(n):
        @pl.when(me == k)
        def _():
            for i in range(per):
                lanes = slice((k * per + i) * LANES, (k * per + i + 1) * LANES)
                chunk[i * rhs:(i + 1) * rhs, :] += near[:, lanes] * noise[:, lanes]


def combine_kernel(n, near, noise, stat, *refs):
    parts, others, chunk = refs[:n], refs[n:-1], refs[-1]
    data = parts[0].shape[0]
    sum_chunk(near, noise, parts, others, chunk)
    chunk[data:, :] = stat[...]


def left_kernel(right, *refs):
    parts, (left, stat) = refs[:-2], refs[-2:]
    rhs, width = right.shape
    data = parts[0].shape[0] - 8
    per = data // rhs
    both = stat_sum(parts, data)
    stat[...] = both
    size_now = unpack_stat(both, 0, rhs) / unpack_stat(both, 1, rhs)
    for i in range(width // LANES):
        lanes = slice(i * LANES, (i + 1) * LANES)
        left[:, lanes] = right[:, lanes] - size_now * image_part(parts, i, per, rhs)


def held_kernel(n, left, stat, far, mark, *refs):
    parts, held = refs[:-1], refs[-1]
    rhs = left.shape[0]
    per = held.shape[0] // n
    row = lax.axis_index("row")
    diagonal = (row ^ lax.axis_index("col")) < 2
    size_now = unpack_stat(stat[...], 0, rhs) / unpack_stat(stat[...], 1, rhs)

    @pl.when(diagonal)
    def _():
        for i in range(held.shape[0]):
            held[i] = left[:, i * LANES:(i + 1) * LANES]

    @pl.when(jnp.logical_not(diagonal))
    def _():
        for j, part in enumerate(parts):
            first = (row ^ 2 * j) * per
            for i in range(per):
                held[first + i] = far[first + i] - size_now * part[i * rhs:(i + 1) * rhs, :]


def last_kernel(right, left, stat_now, stat_next, *refs):
    parts, (solution, residual) = refs[:-2], refs[-2:]
    rhs, width = right.shape
    per = parts[0].shape[0] // rhs
    both = stat_next[...]
    norm = unpack_stat(stat_now[...], 0, rhs)
    norm_next = unpack_stat(both, 0, rhs)
    size_now = norm / unpack_stat(stat_now[...], 1, rhs)
    ratio = norm_next / norm
    size_next = norm_next / (unpack_stat(both, 1, rhs) - ratio * norm_next / size_now)
    back = ratio / size_now
    for i in range(width // LANES):
        lanes = slice(i * LANES, (i + 1) * LANES)
        first = right[:, lanes]
        now = left[:, lanes]
        solution[:, lanes] = size_now * first + size_next * (now + ratio * first)
        image = image_part(parts, i, per, rhs) + back * (first - now)
        residual[:, lanes] = now - size_next * image


def shape_of(*shape):
    return jax.ShapeDtypeStruct(shape, F32)


def on_device(n, right_sides, nugget, cov_blocks, block_rows, block_cols, block_count):
    rhs, width = right_sides.shape
    slots, tile_size = cov_blocks.shape[2:4]
    per = width // n // LANES
    data = per * rhs
    size = data + 8
    noise = nugget.reshape(1, width)
    index = (block_rows, block_cols, block_count)
    pair = pltpu.VMEM((width // tile_size, 2 * rhs, tile_size), BF16)
    index_scratch = [pltpu.SMEM(item.shape, item.dtype) for item in index[:2]]
    index_sems = pltpu.SemaphoreType.DMA((2,))
    vmem = pl.BlockSpec(memory_space=pltpu.VMEM)
    any_spec = pl.BlockSpec(memory_space=pl.ANY)
    smem = pl.BlockSpec(memory_space=pltpu.SMEM)
    hbm = pl.BlockSpec(memory_space=pltpu.HBM)
    params = pltpu.CompilerParams(vmem_limit_bytes=16 * 1024 * 1024)
    cost = pl.CostEstimate(flops=4 * rhs * slots * tile_size * tile_size, transcendentals=0,
                           bytes_accessed=2 * slots * tile_size * tile_size)
    field = shape_of(rhs, width)
    total = shape_of(width // LANES, rhs, LANES)
    chunk = shape_of(data, LANES)
    tile = shape_of(8, LANES)
    loaded = shape_of(size, LANES)

    def call(kernel, name, specs, outs, scratch, args, heavy=False):
        return pl.pallas_call(
            kernel,
            in_specs=specs,
            out_specs=jax.tree.map(lambda _: vmem, outs),
            out_shape=outs,
            scratch_shapes=scratch,
            compiler_params=params,
            cost_estimate=cost if heavy else None,
            name=name,
        )(*args)

    in_hbm = functools.partial(pltpu.with_memory_space_constraint, memory_space=pltpu.HBM)
    kernel_index = index_scratch + [pair, index_sems]

    def to_owners(mirror, twin):
        sent = call(functools.partial(split_kernel, n), "split", [vmem] * 2, [chunk] * (n // 2), [], (mirror, twin))
        return [moved(value, n, far_source(j, n)) for j, value in enumerate(sent)], sent[0]

    def gathered(near, mirror, twin, others, direct, stat):
        merged = call(functools.partial(merge_kernel, n), "merge", [vmem] * 4, [chunk] * n + [tile], [],
                      (direct, mirror, twin, stat))
        parts = [merged[0]] + along_line(merged[1:n], n)
        stat = merged[n]
        for b in bits(n):
            stat, = call(add_kernel, "add_stat", [vmem] * (2 + n // 2), [tile], [],
                         (stat, shifted(stat, "row", b, n), *others))
        own, = call(functools.partial(combine_kernel, n), "combine", [vmem] * (3 + n + n // 2), [loaded], [],
                    (near, noise, stat, *parts, *others))
        return [own] + along_line([own] * (n - 1), n)[::-1]

    def gathered_last(near, mirror, twin, others, direct, stat):
        merged = call(functools.partial(merge_last_kernel, n), "merge_last", [vmem] * 4, [loaded] * n, [],
                      (direct, mirror, twin, stat))
        final, = call(pass_kernel, "pass_on", [vmem] * (1 + n // 2), [loaded], [], (merged[n - 1], *others))
        parts = [merged[0]] + along_line([*merged[1:n - 1], final], n)
        own, stat = call(functools.partial(combine_last_kernel, n), "combine_last", [vmem] * (2 + n + n // 2),
                         [chunk, tile], [], (near, noise, *parts, *others))
        parts = [own] + along_line([own] * (n - 1), n)[::-1]
        for b in bits(n):
            stat, = call(add_kernel, "add_stat", [vmem] * 2, [tile], [], (stat, shifted(stat, "row", b, n)))
        return parts, stat

    current = right_sides
    for b in bits(n)[:0:-1]:
        arrived = moved(current, n, spread_target(b))
        if b == n // 2:
            mirror, blocks = call(
                mirror_first_kernel, "mirror_first", [hbm] * 2 + [smem] + [hbm] * 2,
                [total, jax.ShapeDtypeStruct(cov_blocks.shape[2:], cov_blocks.dtype)],
                index_scratch + [pltpu.VMEM((rhs, width), F32), pair, index_sems,
                                 pltpu.SemaphoreType.DMA, pltpu.SemaphoreType.DMA((slots // GROUP,))],
                (*map(in_hbm, index[:2]), block_count, in_hbm(right_sides), in_hbm(cov_blocks)), True)
            twin_mirror = shifted(mirror, "row", 1, n)
        current, = call(functools.partial(pick_kernel, b), "pick", [vmem] * 3, [field], [], (current, arrived, mirror))
    twin = shifted(current, "row", 1, n)
    others, mark = to_owners(mirror, twin_mirror)
    direct, stat, far = call(
        functools.partial(direct_first_kernel, n), "direct_first", [any_spec] * 2 + [smem] + [vmem] * 6,
        [total, tile, total], kernel_index, (*index, noise, blocks, right_sides, current, twin, mark), True)
    parts = gathered(right_sides, mirror, twin_mirror, others, direct, stat)
    far_parts = [moved(parts[0], n, far_target(j)) for j in range(n // 2)]

    left, stat_now = call(left_kernel, "left", [vmem] * (n + 1), [field, tile], [], (right_sides, *parts))
    mirror, = call(mirror_second_kernel, "mirror_second", [any_spec] * 2 + [smem] + [vmem] * 2,
                   [total], kernel_index, (*index, left, blocks), True)
    twin_mirror = shifted(mirror, "row", 1, n)
    held, = call(functools.partial(held_kernel, n), "held", [vmem] * (4 + n // 2), [total], [],
                 (left, stat_now, far, mirror, *far_parts))
    twin = shifted(held, "row", 1, n)
    others, mark = to_owners(mirror, twin_mirror)
    direct, stat = call(
        functools.partial(direct_second_kernel, n), "direct_second", [any_spec] * 2 + [smem] + [vmem] * 6,
        [total, tile], kernel_index, (*index, noise, blocks, left, held, twin, mark), True)
    parts, stat_next = gathered_last(left, mirror, twin_mirror, others, direct, stat)
    return tuple(call(last_kernel, "last", [vmem] * (n + 4), [field, field], [],
                      (right_sides, left, stat_now, stat_next, *parts)))


def solution(mesh):
    n = mesh.shape["row"]
    assert n == mesh.shape["col"] and n & (n - 1) == 0 and n >= 4
    placed = (
        P(None, ("groups", "row")),
        P(("groups", "row")),
        P(("groups", "row"), "col", None, None, None),
        P(("groups", "row"), "col", None),
        P(("groups", "row"), "col", None),
        P(("groups", "row"), "col"),
    )
    return jax.shard_map(
        functools.partial(on_device, n),
        mesh=mesh,
        in_specs=placed,
        out_specs=(P(None, ("groups", "row")), P(None, ("groups", "row"))),
        check_vma=False,
    )
```

```python
import functools

import jax
import jax.numpy as jnp
from jax import lax
from jax.experimental import pallas as pl
from jax.experimental.pallas import tpu as pltpu
from jax.sharding import PartitionSpec as P

ITERS = 2
LANES = 128
GROUP = 8
BF16 = jnp.bfloat16
F32 = jnp.float32


def shifted(value, axis, d, n):
    return lax.ppermute(value, axis, [(i, i ^ d) for i in range(n)])


def distances(n):
    return [d for d in range(n) if d > 1] + [1]


def moved(value, n, target):
    pairs = [(r * n + c, target(r, c)) for r in range(n) for c in range(n)]
    return lax.ppermute(value, ("row", "col"), [(s, t[0] * n + t[1]) for s, t in pairs])


def far_target(j):
    def target(r, c):
        d = r ^ c
        if d ^ 2 * j >= 2:
            return c ^ 2 * j, r
        return c ^ (d & 1) ^ (j == 0), c

    return target


def spread_target(b):
    def target(r, c):
        o = r ^ c
        move = {0: b, b: 1, b + 1: b, 1: 1}.get(o % (2 * b), 1)
        return r ^ move, c

    return target


def collect_target(b, n):
    back = {spread_target(b)(r, c): (r, c) for r in range(n) for c in range(n)}
    return lambda r, c: back[r, c]


def bits(n):
    return [1 << i for i in range(n.bit_length() - 1)]


def load_pair(dst, tile, value):
    rhs = value.shape[0]
    high = value.astype(BF16)
    dst[tile, :rhs, :] = high
    dst[tile, rhs:, :] = (value - high.astype(F32)).astype(BF16)


def product(pair, block, contract):
    both = lax.dot_general(pair, block, (((1,), (contract,)), ((), ())), preferred_element_type=F32)
    rhs = both.shape[0] // 2
    return both[:rhs] + both[rhs:]


def pack_stats(columns, rhs):
    lane = lax.broadcasted_iota(jnp.int32, (8, LANES), 1)
    tile = jnp.zeros((8, LANES), F32)
    groups = rhs // 8
    for i, column in enumerate(columns):
        for g in range(groups):
            tile = jnp.where(lane == i * groups + g, column[g * 8:(g + 1) * 8], tile)
    return tile


def unpack_stat(tile, i, rhs):
    groups = rhs // 8
    return jnp.concatenate([tile[:, i * groups + g:i * groups + g + 1] for g in range(groups)], axis=0)


def accumulate(total, tile, value):
    width = value.shape[1] // LANES
    for part in range(width):
        total[tile * width + part] += value[:, part * LANES:(part + 1) * LANES]


def wide_group(blocks):
    return 2 * GROUP if blocks.shape[0] % (2 * GROUP) == 0 else GROUP


def add_blocks(blocks, slot_rows, slot_cols, live, pairs, total, mirror, group, ready=None):
    read, write, contract = (slot_rows, slot_cols, 0) if mirror else (slot_cols, slot_rows, 1)

    def body(step, carry):
        if ready is not None:
            ready(step)
        for g in range(group):
            slot = step * group + g
            value = product(pairs[read[0, 0, slot]], blocks[slot], contract)
            accumulate(total, write[0, 0, slot], jnp.where(slot < live, value, 0.0))
        return carry

    lax.fori_loop(0, (live + group - 1) // group, body, 0)


def image_part(parts, me, i, per, rhs):
    rows = slice((i % per) * rhs, (i % per + 1) * rhs)
    value = parts[0][rows, :]
    for d, part in zip(distances(len(parts)), parts[1:]):
        value = jnp.where(me ^ d == i // per, part[rows, :], value)
    return value


def row_sums(value):
    return jnp.sum(value, axis=1, keepdims=True)


def cross_sums(total, value):
    rhs = value.shape[0]
    cross = jnp.zeros((rhs, LANES), F32)
    for i in range(total.shape[0]):
        cross += total[i] * value[:, i * LANES:(i + 1) * LANES]
    return row_sums(cross)


def tree_sum(values):
    values = list(values)
    while len(values) > 1:
        values = [a + b for a, b in zip(values[::2], values[1::2])]
    return values[0]


def stat_sum(parts, data):
    order = [0] + distances(len(parts))
    return tree_sum(parts[order.index(d)][data:, :] for d in range(len(parts)))


def fetch_index(sources, targets, sems):
    copies = [pltpu.make_async_copy(s, t, sems.at[i]) for i, (s, t) in enumerate(zip(sources, targets))]
    for copy in copies:
        copy.start()
    return copies


def mirror_first_kernel(rows_hbm, cols_hbm, count, right_hbm, cov, total, blocks, *scratch):
    slot_rows, slot_cols, right, pairs, index_sems, right_sem, block_sems = scratch
    slots, tile_size = blocks.shape[:2]

    def block_copy(i):
        part = pl.ds(i * GROUP, GROUP)
        return pltpu.make_async_copy(cov.at[0, 0, part], blocks.at[part], block_sems.at[i])

    copies = fetch_index((rows_hbm, cols_hbm), (slot_rows, slot_cols), index_sems)
    load = pltpu.make_async_copy(right_hbm, right, right_sem)
    load.start()
    live = count[0, 0]
    for i in range(slots // GROUP):
        @pl.when(i * GROUP < live)
        def _():
            block_copy(i).start()
    total[...] = jnp.zeros_like(total)
    load.wait()
    for tile in range(right.shape[1] // tile_size):
        load_pair(pairs, tile, right[:, tile * tile_size:(tile + 1) * tile_size])
    for copy in copies:
        copy.wait()
    add_blocks(blocks, slot_rows, slot_cols, live, pairs, total, True, GROUP, lambda i: block_copy(i).wait())


def mirror_second_kernel(rows_any, cols_any, count, near, blocks, total, *scratch):
    slot_rows, slot_cols, pairs, index_sems = scratch
    tile_size = blocks.shape[1]
    copies = fetch_index((rows_any, cols_any), (slot_rows, slot_cols), index_sems)
    total[...] = jnp.zeros_like(total)
    for tile in range(near.shape[1] // tile_size):
        load_pair(pairs, tile, near[:, tile * tile_size:(tile + 1) * tile_size])
    for copy in copies:
        copy.wait()
    add_blocks(blocks, slot_rows, slot_cols, count[0, 0], pairs, total, True, wide_group(blocks))


def finish_direct(total, near, noise, stat, n):
    value = near[...]
    rhs = value.shape[0]
    square = value * value
    share = 1.0 / n
    bend = share * row_sums(square * noise[...]) + 2.0 * cross_sums(total, value)
    stat[...] = pack_stats([share * row_sums(square), bend], rhs)


def direct_first_kernel(n, rows_any, cols_any, count, noise, blocks, near, current, twin, total, stat, far, *scratch):
    slot_rows, slot_cols, pairs, index_sems = scratch
    tile_size = blocks.shape[1]
    pieces = tile_size // LANES
    copies = fetch_index((rows_any, cols_any), (slot_rows, slot_cols), index_sems)
    odd = (lax.axis_index("row") ^ lax.axis_index("col")) & 1
    for o, source in enumerate((current, twin)):
        @pl.when(odd == o)
        def _():
            for tile in range(near.shape[1] // tile_size):
                value = source[:, tile * tile_size:(tile + 1) * tile_size]
                load_pair(pairs, tile, value)
                for i in range(pieces):
                    far[tile * pieces + i] = value[:, i * LANES:(i + 1) * LANES]
    total[...] = jnp.zeros_like(total)
    for copy in copies:
        copy.wait()
    add_blocks(blocks, slot_rows, slot_cols, count[0, 0], pairs, total, False, wide_group(blocks))
    finish_direct(total, near, noise, stat, n)


def direct_second_kernel(n, rows_any, cols_any, count, noise, blocks, near, held, twin, total, stat, *scratch):
    slot_rows, slot_cols, pairs, index_sems = scratch
    tile_size = blocks.shape[1]
    pieces = tile_size // LANES
    per = held.shape[0] // n
    copies = fetch_index((rows_any, cols_any), (slot_rows, slot_cols), index_sems)
    row = lax.axis_index("row")
    offset = row ^ lax.axis_index("col")
    for tile in range(near.shape[1] // tile_size):
        value = []
        for i in range(tile * pieces, (tile + 1) * pieces):
            own = jnp.logical_or(offset == 0, jnp.logical_and(offset >= 2, ((i // per) ^ row) & 1 == 0))
            value.append(jnp.where(own, held[i], twin[i]))
        load_pair(pairs, tile, jnp.concatenate(value, axis=1))
    total[...] = jnp.zeros_like(total)
    for copy in copies:
        copy.wait()
    add_blocks(blocks, slot_rows, slot_cols, count[0, 0], pairs, total, False, wide_group(blocks))
    finish_direct(total, near, noise, stat, n)


def add_kernel(one, two, *refs):
    refs[-1][...] = one[...] + two[...]


def pick_kernel(b, current, arrived, mark, out):
    there = (lax.axis_index("row") ^ lax.axis_index("col")) & b
    out[...] = jnp.where(there != 0, arrived[...], current[...])


def split_kernel(n, mirror, twin, far, near):
    per = mirror.shape[0] // n
    me = lax.axis_index("col")
    for d in range(n):
        first = (me ^ d) * per
        out, start = (near, d * per) if d < 2 else (far, (d - 2) * per)
        for i in range(per):
            out[start + i] = mirror[first + i] + twin[first + i]


def merge_kernel(n, ways, direct, mirror, twin, arrived, mark, *outs):
    per = direct.shape[0] // n
    rhs = direct.shape[1]
    me = lax.axis_index("col")
    diagonal = lax.axis_index("row") == me
    for d, out in zip(ways, outs):
        first = (me ^ d) * per
        start = (d if d < 2 else d - 2) * per

        @pl.when(diagonal)
        def _():
            for i in range(per):
                both = mirror[first + i] + twin[first + i]
                out[i * rhs:(i + 1) * rhs, :] = direct[first + i] + (both + arrived[start + i])

        @pl.when(jnp.logical_not(diagonal))
        def _():
            for i in range(per):
                out[i * rhs:(i + 1) * rhs, :] = direct[first + i]


def combine_kernel(n, near, noise, stat, *refs):
    parts, chunk = refs[:n], refs[n]
    rhs = near.shape[0]
    data = parts[0].shape[0]
    per = data // rhs
    me = lax.axis_index("col")
    chunk[:data, :] = tree_sum(ref[...] for ref in parts)
    chunk[data:, :] = stat[...]
    for k in range(n):
        @pl.when(me == k)
        def _():
            for i in range(per):
                lanes = slice((k * per + i) * LANES, (k * per + i + 1) * LANES)
                chunk[i * rhs:(i + 1) * rhs, :] += near[:, lanes] * noise[:, lanes]


def left_kernel(n, right, far, *refs):
    others, parts, (left, stat, held) = refs[:n // 2], refs[n // 2:-3], refs[-3:]
    rhs, width = right.shape
    data = parts[0].shape[0] - 8
    per = data // rhs
    row, me = lax.axis_index("row"), lax.axis_index("col")
    diagonal = (row ^ me) < 2
    both = stat_sum(parts, data)
    stat[...] = both
    size_now = unpack_stat(both, 0, rhs) / unpack_stat(both, 1, rhs)
    for i in range(width // LANES):
        lanes = slice(i * LANES, (i + 1) * LANES)
        value = right[:, lanes] - size_now * image_part(parts, me, i, per, rhs)
        left[:, lanes] = value
        held[i] = value

    @pl.when(jnp.logical_not(diagonal))
    def _():
        for j, other in enumerate(others):
            first = (row ^ 2 * j) * per
            for i in range(per):
                held[first + i] = far[first + i] - size_now * other[i * rhs:(i + 1) * rhs, :]


def last_kernel(right, left, stat_now, *refs):
    parts, (solution, residual) = refs[:-2], refs[-2:]
    rhs, width = right.shape
    data = parts[0].shape[0] - 8
    per = data // rhs
    me = lax.axis_index("col")
    both = stat_sum(parts, data)
    norm = unpack_stat(stat_now[...], 0, rhs)
    norm_next = unpack_stat(both, 0, rhs)
    size_now = norm / unpack_stat(stat_now[...], 1, rhs)
    ratio = norm_next / norm
    size_next = norm_next / (unpack_stat(both, 1, rhs) - ratio * norm_next / size_now)
    back = ratio / size_now
    for i in range(width // LANES):
        lanes = slice(i * LANES, (i + 1) * LANES)
        first = right[:, lanes]
        now = left[:, lanes]
        solution[:, lanes] = size_now * first + size_next * (now + ratio * first)
        image = image_part(parts, me, i, per, rhs) + back * (first - now)
        residual[:, lanes] = now - size_next * image


def shape_of(*shape):
    return jax.ShapeDtypeStruct(shape, F32)


def on_device(n, right_sides, nugget, cov_blocks, block_rows, block_cols, block_count):
    rhs, width = right_sides.shape
    slots, tile_size = cov_blocks.shape[2:4]
    per = width // n // LANES
    data = per * rhs
    size = data + 8
    noise = nugget.reshape(1, width)
    index = (block_rows, block_cols, block_count)
    pair = pltpu.VMEM((width // tile_size, 2 * rhs, tile_size), BF16)
    index_scratch = [pltpu.SMEM(item.shape, item.dtype) for item in index[:2]]
    index_sems = pltpu.SemaphoreType.DMA((2,))
    vmem = pl.BlockSpec(memory_space=pltpu.VMEM)
    any_spec = pl.BlockSpec(memory_space=pl.ANY)
    smem = pl.BlockSpec(memory_space=pltpu.SMEM)
    hbm = pl.BlockSpec(memory_space=pltpu.HBM)
    params = pltpu.CompilerParams(vmem_limit_bytes=16 * 1024 * 1024)
    cost = pl.CostEstimate(flops=4 * rhs * slots * tile_size * tile_size, transcendentals=0,
                           bytes_accessed=2 * slots * tile_size * tile_size)
    field = shape_of(rhs, width)
    total = shape_of(width // LANES, rhs, LANES)
    chunk = shape_of(data, LANES)
    far_chunks = shape_of((n - 2) * per, rhs, LANES)
    near_chunks = shape_of(2 * per, rhs, LANES)
    tile = shape_of(8, LANES)
    loaded = shape_of(size, LANES)

    def call(kernel, name, specs, outs, scratch, args, heavy=False):
        return pl.pallas_call(
            kernel,
            in_specs=specs,
            out_specs=jax.tree.map(lambda _: vmem, outs),
            out_shape=outs,
            scratch_shapes=scratch,
            compiler_params=params,
            cost_estimate=cost if heavy else None,
            name=name,
        )(*args)

    in_hbm = functools.partial(pltpu.with_memory_space_constraint, memory_space=pltpu.HBM)
    kernel_index = index_scratch + [pair, index_sems]

    def collected(mirror, twin):
        far, near = call(functools.partial(split_kernel, n), "split", [vmem] * 2, [far_chunks, near_chunks], [],
                         (mirror, twin))
        for b in bits(n)[1:]:
            arrived = [moved(value, n, collect_target(b, n)) for value in (far, near)]
            if 2 * b < n:
                far, near = [call(add_kernel, "add_sums", [vmem] * 2, [shape], [], (own, other))[0]
                             for shape, own, other in zip((far_chunks, near_chunks), (far, near), arrived)]
        return arrived

    def gathered(near, mirror, twin, others, direct, stat):
        ways = distances(n)[:-1]
        sent = call(functools.partial(merge_kernel, n, ways), "merge_far", [vmem] * 5, [chunk] * (n - 2), [],
                    (direct, mirror, twin, others[0], stat))
        own, last = call(functools.partial(merge_kernel, n, (0, 1)), "merge_near", [vmem] * 5, [chunk] * 2, [],
                         (direct, mirror, twin, others[1], stat))
        parts = [own] + [shifted(value, "col", d, n) for d, value in zip(distances(n), (*sent, last))]
        for b in bits(n):
            stat, = call(add_kernel, "add_stat", [vmem] * 3, [tile], [], (stat, shifted(stat, "row", b, n), sent[0]))
        own, = call(functools.partial(combine_kernel, n), "combine", [vmem] * (3 + n), [loaded], [],
                    (near, noise, stat, *parts))
        return [own] + [shifted(own, "col", d, n) for d in distances(n)]

    current = right_sides
    for b in bits(n)[:0:-1]:
        arrived = moved(current, n, spread_target(b))
        if b == n // 2:
            mirror, blocks = call(
                mirror_first_kernel, "mirror_first", [hbm] * 2 + [smem] + [hbm] * 2,
                [total, jax.ShapeDtypeStruct(cov_blocks.shape[2:], cov_blocks.dtype)],
                index_scratch + [pltpu.VMEM((rhs, width), F32), pair, index_sems,
                                 pltpu.SemaphoreType.DMA, pltpu.SemaphoreType.DMA((slots // GROUP,))],
                (*map(in_hbm, index[:2]), block_count, in_hbm(right_sides), in_hbm(cov_blocks)), True)
            twin_mirror = shifted(mirror, "row", 1, n)
        current, = call(functools.partial(pick_kernel, b), "pick", [vmem] * 3, [field], [], (current, arrived, mirror))
    twin = shifted(current, "row", 1, n)
    others = collected(mirror, twin_mirror)
    direct, stat, far = call(
        functools.partial(direct_first_kernel, n), "direct_first", [any_spec] * 2 + [smem] + [vmem] * 5,
        [total, tile, total], kernel_index, (*index, noise, blocks, right_sides, current, twin), True)
    parts = gathered(right_sides, mirror, twin_mirror, others, direct, stat)
    far_parts = [moved(parts[0], n, far_target(j)) for j in range(n // 2)]

    left, stat_now, held = call(
        functools.partial(left_kernel, n), "left", [vmem] * (2 + n + n // 2), [field, tile, total], [],
        (right_sides, far, *far_parts, *parts))
    twin = shifted(held, "row", 1, n)
    mirror, = call(mirror_second_kernel, "mirror_second", [any_spec] * 2 + [smem] + [vmem] * 2,
                   [total], kernel_index, (*index, left, blocks), True)
    twin_mirror = shifted(mirror, "row", 1, n)
    others = collected(mirror, twin_mirror)
    direct, stat = call(
        functools.partial(direct_second_kernel, n), "direct_second", [any_spec] * 2 + [smem] + [vmem] * 5,
        [total, tile], kernel_index, (*index, noise, blocks, left, held, twin), True)
    parts = gathered(left, mirror, twin_mirror, others, direct, stat)
    return tuple(call(last_kernel, "last", [vmem] * (n + 3), [field, field], [],
                      (right_sides, left, stat_now, *parts)))


def solution(mesh):
    n = mesh.shape["row"]
    assert n == mesh.shape["col"] and n & (n - 1) == 0 and n >= 4
    placed = (
        P(None, ("groups", "row")),
        P(("groups", "row")),
        P(("groups", "row"), "col", None, None, None),
        P(("groups", "row"), "col", None),
        P(("groups", "row"), "col", None),
        P(("groups", "row"), "col"),
    )
    return jax.shard_map(
        functools.partial(on_device, n),
        mesh=mesh,
        in_specs=placed,
        out_specs=(P(None, ("groups", "row")), P(None, ("groups", "row"))),
        check_vma=False,
    )
```

```python
import functools

import jax
import jax.numpy as jnp
from jax import lax
from jax.experimental import pallas as pl
from jax.experimental.pallas import tpu as pltpu
from jax.sharding import PartitionSpec as P

ITERS = 2
LANES = 128
GROUP = 8
BF16 = jnp.bfloat16
F32 = jnp.float32


def shifted(value, axis, d, n):
    return lax.ppermute(value, axis, [(i, i ^ d) for i in range(n)])


def distances(n):
    return [d for d in range(n) if d > 1] + [1]


def moved(value, n, target):
    pairs = [(r * n + c, target(r, c)) for r in range(n) for c in range(n)]
    return lax.ppermute(value, ("row", "col"), [(s, t[0] * n + t[1]) for s, t in pairs])


def far_target(j):
    def target(r, c):
        d = r ^ c
        if d ^ 2 * j >= 2:
            return c ^ 2 * j, r
        return c ^ (d & 1) ^ (j == 0), c

    return target


def far_source(j, n):
    back = {far_target(j)(r, c): (r, c) for r in range(n) for c in range(n)}
    return lambda r, c: back[r, c]


def spread_target(b):
    def target(r, c):
        o = r ^ c
        move = {0: b, b: 1, b + 1: b, 1: 1}.get(o % (2 * b), 1)
        return r ^ move, c

    return target


def bits(n):
    return [1 << i for i in range(n.bit_length() - 1)]


def load_pair(dst, tile, value):
    rhs = value.shape[0]
    high = value.astype(BF16)
    dst[tile, :rhs, :] = high
    dst[tile, rhs:, :] = (value - high.astype(F32)).astype(BF16)


def product(pair, block, contract):
    both = lax.dot_general(pair, block, (((1,), (contract,)), ((), ())), preferred_element_type=F32)
    rhs = both.shape[0] // 2
    return both[:rhs] + both[rhs:]


def pack_stats(columns, rhs):
    lane = lax.broadcasted_iota(jnp.int32, (8, LANES), 1)
    tile = jnp.zeros((8, LANES), F32)
    groups = rhs // 8
    for i, column in enumerate(columns):
        for g in range(groups):
            tile = jnp.where(lane == i * groups + g, column[g * 8:(g + 1) * 8], tile)
    return tile


def unpack_stat(tile, i, rhs):
    groups = rhs // 8
    return jnp.concatenate([tile[:, i * groups + g:i * groups + g + 1] for g in range(groups)], axis=0)


def accumulate(total, tile, value):
    width = value.shape[1] // LANES
    for part in range(width):
        total[tile * width + part] += value[:, part * LANES:(part + 1) * LANES]


def add_blocks(blocks, slot_rows, slot_cols, live, pairs, total, mirror, wide, ready=None):
    read, write, contract = (slot_rows, slot_cols, 0) if mirror else (slot_cols, slot_rows, 1)

    def steps(group, base):
        def body(step, carry):
            if ready is not None:
                ready(step)
            for g in range(group):
                slot = base + step * group + g
                value = product(pairs[read[0, 0, slot]], blocks[slot], contract)
                accumulate(total, write[0, 0, slot], jnp.where(slot < live, value, 0.0))
            return carry

        return body

    done = 0
    if wide > GROUP:
        count = live // wide
        lax.fori_loop(0, count, steps(wide, 0), 0)
        done = count * wide
    lax.fori_loop(0, (live - done + GROUP - 1) // GROUP, steps(GROUP, done), 0)


def image_part(parts, me, i, per, rhs):
    rows = slice((i % per) * rhs, (i % per + 1) * rhs)
    value = parts[0][rows, :]
    for d, part in zip(distances(len(parts))[::-1], parts[1:]):
        value = jnp.where(me ^ d == i // per, part[rows, :], value)
    return value


def row_sums(value):
    return jnp.sum(value, axis=1, keepdims=True)


def cross_sums(total, value):
    rhs = value.shape[0]
    cross = jnp.zeros((rhs, LANES), F32)
    for i in range(total.shape[0]):
        cross += total[i] * value[:, i * LANES:(i + 1) * LANES]
    return row_sums(cross)


def tree_sum(values):
    values = list(values)
    while len(values) > 1:
        values = [a + b for a, b in zip(values[::2], values[1::2])]
    return values[0]


def stat_sum(parts, data):
    order = [0] + distances(len(parts))[::-1]
    return tree_sum(parts[order.index(d)][data:, :] for d in range(len(parts)))


def fetch_index(sources, targets, sems):
    copies = [pltpu.make_async_copy(s, t, sems.at[i]) for i, (s, t) in enumerate(zip(sources, targets))]
    for copy in copies:
        copy.start()
    return copies


def mirror_first_kernel(rows_hbm, cols_hbm, count, right_hbm, cov, total, blocks, *scratch):
    slot_rows, slot_cols, right, pairs, index_sems, right_sem, block_sems = scratch
    slots, tile_size = blocks.shape[:2]

    def block_copy(i):
        part = pl.ds(i * GROUP, GROUP)
        return pltpu.make_async_copy(cov.at[0, 0, part], blocks.at[part], block_sems.at[i])

    copies = fetch_index((rows_hbm, cols_hbm), (slot_rows, slot_cols), index_sems)
    load = pltpu.make_async_copy(right_hbm, right, right_sem)
    load.start()
    live = count[0, 0]
    for i in range(slots // GROUP):
        @pl.when(i * GROUP < live)
        def _():
            block_copy(i).start()
    total[...] = jnp.zeros_like(total)
    load.wait()
    for tile in range(right.shape[1] // tile_size):
        load_pair(pairs, tile, right[:, tile * tile_size:(tile + 1) * tile_size])
    for copy in copies:
        copy.wait()
    add_blocks(blocks, slot_rows, slot_cols, live, pairs, total, True, GROUP, lambda i: block_copy(i).wait())


def mirror_second_kernel(rows_any, cols_any, count, near, blocks, total, *scratch):
    slot_rows, slot_cols, pairs, index_sems = scratch
    tile_size = blocks.shape[1]
    copies = fetch_index((rows_any, cols_any), (slot_rows, slot_cols), index_sems)
    total[...] = jnp.zeros_like(total)
    for tile in range(near.shape[1] // tile_size):
        load_pair(pairs, tile, near[:, tile * tile_size:(tile + 1) * tile_size])
    for copy in copies:
        copy.wait()
    add_blocks(blocks, slot_rows, slot_cols, count[0, 0], pairs, total, True, 2 * GROUP)


def finish_direct(total, near, noise, stat, n):
    value = near[...]
    rhs = value.shape[0]
    square = value * value
    share = 1.0 / n
    bend = share * row_sums(square * noise[...]) + 2.0 * cross_sums(total, value)
    stat[...] = pack_stats([share * row_sums(square), bend], rhs)


def direct_first_kernel(n, rows_any, cols_any, count, noise, blocks, near, current, twin, mark, total, stat, far, *scratch):
    slot_rows, slot_cols, pairs, index_sems = scratch
    tile_size = blocks.shape[1]
    pieces = tile_size // LANES
    copies = fetch_index((rows_any, cols_any), (slot_rows, slot_cols), index_sems)
    odd = (lax.axis_index("row") ^ lax.axis_index("col")) & 1
    for o, source in enumerate((current, twin)):
        @pl.when(odd == o)
        def _():
            for tile in range(near.shape[1] // tile_size):
                value = source[:, tile * tile_size:(tile + 1) * tile_size]
                load_pair(pairs, tile, value)
                for i in range(pieces):
                    far[tile * pieces + i] = value[:, i * LANES:(i + 1) * LANES]
    total[...] = jnp.zeros_like(total)
    for copy in copies:
        copy.wait()
    add_blocks(blocks, slot_rows, slot_cols, count[0, 0], pairs, total, False, 2 * GROUP)
    finish_direct(total, near, noise, stat, n)


def direct_second_kernel(n, rows_any, cols_any, count, noise, blocks, near, held, twin, mark, total, stat, *scratch):
    slot_rows, slot_cols, pairs, index_sems = scratch
    tile_size = blocks.shape[1]
    pieces = tile_size // LANES
    per = held.shape[0] // n
    copies = fetch_index((rows_any, cols_any), (slot_rows, slot_cols), index_sems)
    row = lax.axis_index("row")
    offset = row ^ lax.axis_index("col")
    for tile in range(near.shape[1] // tile_size):
        value = []
        for i in range(tile * pieces, (tile + 1) * pieces):
            own = jnp.logical_or(offset == 0, jnp.logical_and(offset >= 2, ((i // per) ^ row) & 1 == 0))
            value.append(jnp.where(own, held[i], twin[i]))
        load_pair(pairs, tile, jnp.concatenate(value, axis=1))
    total[...] = jnp.zeros_like(total)
    for copy in copies:
        copy.wait()
    add_blocks(blocks, slot_rows, slot_cols, count[0, 0], pairs, total, False, 2 * GROUP)
    finish_direct(total, near, noise, stat, n)


def add_kernel(one, two, *refs):
    refs[-1][...] = one[...] + two[...]


def pick_kernel(b, current, arrived, mark, out):
    there = (lax.axis_index("row") ^ lax.axis_index("col")) & b
    out[...] = jnp.where(there != 0, arrived[...], current[...])


def split_kernel(n, mirror, twin, *outs):
    per = mirror.shape[0] // n
    rhs = mirror.shape[1]
    row = lax.axis_index("row")
    for j, out in enumerate(outs):
        first = (row ^ 2 * j) * per
        for i in range(per):
            out[i * rhs:(i + 1) * rhs, :] = mirror[first + i] + twin[first + i]


def merge_kernel(n, direct, mirror, twin, stat, *outs):
    per = direct.shape[0] // n
    rhs = direct.shape[1]
    me = lax.axis_index("col")
    diagonal = lax.axis_index("row") == me
    outs[n][...] = stat[...]
    for d, out in zip([0] + distances(n), outs):
        first = (me ^ d) * per

        @pl.when(diagonal)
        def _():
            for i in range(per):
                out[i * rhs:(i + 1) * rhs, :] = direct[first + i] + (mirror[first + i] + twin[first + i])

        @pl.when(jnp.logical_not(diagonal))
        def _():
            for i in range(per):
                out[i * rhs:(i + 1) * rhs, :] = direct[first + i]


def combine_kernel(n, near, noise, stat, *refs):
    parts, others, chunk = refs[:n], refs[n:-1], refs[-1]
    rhs = near.shape[0]
    data = parts[0].shape[0]
    per = data // rhs
    me = lax.axis_index("col")
    group = (lax.axis_index("row") ^ me) // 2
    value = tree_sum(ref[...] for ref in parts)
    for j, other in enumerate(others):
        value += jnp.where(group == j, 0.0, other[...])
    chunk[:data, :] = value
    chunk[data:, :] = stat[...]
    for k in range(n):
        @pl.when(me == k)
        def _():
            for i in range(per):
                lanes = slice((k * per + i) * LANES, (k * per + i + 1) * LANES)
                chunk[i * rhs:(i + 1) * rhs, :] += near[:, lanes] * noise[:, lanes]


def left_kernel(right, *refs):
    parts, (left, stat) = refs[:-2], refs[-2:]
    rhs, width = right.shape
    data = parts[0].shape[0] - 8
    per = data // rhs
    me = lax.axis_index("col")
    both = stat_sum(parts, data)
    stat[...] = both
    size_now = unpack_stat(both, 0, rhs) / unpack_stat(both, 1, rhs)
    for i in range(width // LANES):
        lanes = slice(i * LANES, (i + 1) * LANES)
        left[:, lanes] = right[:, lanes] - size_now * image_part(parts, me, i, per, rhs)


def held_kernel(n, left, stat, far, mark, *refs):
    parts, held = refs[:-1], refs[-1]
    rhs = left.shape[0]
    per = held.shape[0] // n
    row = lax.axis_index("row")
    diagonal = (row ^ lax.axis_index("col")) < 2
    size_now = unpack_stat(stat[...], 0, rhs) / unpack_stat(stat[...], 1, rhs)

    @pl.when(diagonal)
    def _():
        for i in range(held.shape[0]):
            held[i] = left[:, i * LANES:(i + 1) * LANES]

    @pl.when(jnp.logical_not(diagonal))
    def _():
        for j, part in enumerate(parts):
            first = (row ^ 2 * j) * per
            for i in range(per):
                held[first + i] = far[first + i] - size_now * part[i * rhs:(i + 1) * rhs, :]


def last_kernel(right, left, stat_now, *refs):
    parts, (solution, residual) = refs[:-2], refs[-2:]
    rhs, width = right.shape
    data = parts[0].shape[0] - 8
    per = data // rhs
    me = lax.axis_index("col")
    both = stat_sum(parts, data)
    norm = unpack_stat(stat_now[...], 0, rhs)
    norm_next = unpack_stat(both, 0, rhs)
    size_now = norm / unpack_stat(stat_now[...], 1, rhs)
    ratio = norm_next / norm
    size_next = norm_next / (unpack_stat(both, 1, rhs) - ratio * norm_next / size_now)
    back = ratio / size_now
    for i in range(width // LANES):
        lanes = slice(i * LANES, (i + 1) * LANES)
        first = right[:, lanes]
        now = left[:, lanes]
        solution[:, lanes] = size_now * first + size_next * (now + ratio * first)
        image = image_part(parts, me, i, per, rhs) + back * (first - now)
        residual[:, lanes] = now - size_next * image


def shape_of(*shape):
    return jax.ShapeDtypeStruct(shape, F32)


def on_device(n, right_sides, nugget, cov_blocks, block_rows, block_cols, block_count):
    rhs, width = right_sides.shape
    slots, tile_size = cov_blocks.shape[2:4]
    per = width // n // LANES
    data = per * rhs
    size = data + 8
    noise = nugget.reshape(1, width)
    index = (block_rows, block_cols, block_count)
    pair = pltpu.VMEM((width // tile_size, 2 * rhs, tile_size), BF16)
    index_scratch = [pltpu.SMEM(item.shape, item.dtype) for item in index[:2]]
    index_sems = pltpu.SemaphoreType.DMA((2,))
    vmem = pl.BlockSpec(memory_space=pltpu.VMEM)
    any_spec = pl.BlockSpec(memory_space=pl.ANY)
    smem = pl.BlockSpec(memory_space=pltpu.SMEM)
    hbm = pl.BlockSpec(memory_space=pltpu.HBM)
    params = pltpu.CompilerParams(vmem_limit_bytes=16 * 1024 * 1024)
    cost = pl.CostEstimate(flops=4 * rhs * slots * tile_size * tile_size, transcendentals=0,
                           bytes_accessed=2 * slots * tile_size * tile_size)
    field = shape_of(rhs, width)
    total = shape_of(width // LANES, rhs, LANES)
    chunk = shape_of(data, LANES)
    tile = shape_of(8, LANES)
    loaded = shape_of(size, LANES)

    def call(kernel, name, specs, outs, scratch, args, heavy=False):
        return pl.pallas_call(
            kernel,
            in_specs=specs,
            out_specs=jax.tree.map(lambda _: vmem, outs),
            out_shape=outs,
            scratch_shapes=scratch,
            compiler_params=params,
            cost_estimate=cost if heavy else None,
            name=name,
        )(*args)

    in_hbm = functools.partial(pltpu.with_memory_space_constraint, memory_space=pltpu.HBM)
    kernel_index = index_scratch + [pair, index_sems]

    def to_owners(mirror, twin):
        sent = call(functools.partial(split_kernel, n), "split", [vmem] * 2, [chunk] * (n // 2), [], (mirror, twin))
        return [moved(value, n, far_source(j, n)) for j, value in enumerate(sent)], sent[0]

    def gathered(near, mirror, twin, others, direct, stat):
        merged = call(functools.partial(merge_kernel, n), "merge", [vmem] * 4, [chunk] * n + [tile], [],
                      (direct, mirror, twin, stat))
        parts = [merged[0]] + [shifted(value, "col", d, n) for d, value in zip(distances(n), merged[1:n])]
        stat = merged[n]
        for b in bits(n):
            stat, = call(add_kernel, "add_stat", [vmem] * (2 + n // 2), [tile], [],
                         (stat, shifted(stat, "row", b, n), *others))
        own, = call(functools.partial(combine_kernel, n), "combine", [vmem] * (3 + n + n // 2), [loaded], [],
                    (near, noise, stat, *parts, *others))
        return [own] + [shifted(own, "col", d, n) for d in distances(n)[::-1]]

    current = right_sides
    for b in bits(n)[:0:-1]:
        arrived = moved(current, n, spread_target(b))
        if b == n // 2:
            mirror, blocks = call(
                mirror_first_kernel, "mirror_first", [hbm] * 2 + [smem] + [hbm] * 2,
                [total, jax.ShapeDtypeStruct(cov_blocks.shape[2:], cov_blocks.dtype)],
                index_scratch + [pltpu.VMEM((rhs, width), F32), pair, index_sems,
                                 pltpu.SemaphoreType.DMA, pltpu.SemaphoreType.DMA((slots // GROUP,))],
                (*map(in_hbm, index[:2]), block_count, in_hbm(right_sides), in_hbm(cov_blocks)), True)
            twin_mirror = shifted(mirror, "row", 1, n)
        current, = call(functools.partial(pick_kernel, b), "pick", [vmem] * 3, [field], [], (current, arrived, mirror))
    twin = shifted(current, "row", 1, n)
    others, mark = to_owners(mirror, twin_mirror)
    direct, stat, far = call(
        functools.partial(direct_first_kernel, n), "direct_first", [any_spec] * 2 + [smem] + [vmem] * 6,
        [total, tile, total], kernel_index, (*index, noise, blocks, right_sides, current, twin, mark), True)
    parts = gathered(right_sides, mirror, twin_mirror, others, direct, stat)
    far_parts = [moved(parts[0], n, far_target(j)) for j in range(n // 2)]

    left, stat_now = call(left_kernel, "left", [vmem] * (n + 1), [field, tile], [], (right_sides, *parts))
    mirror, = call(mirror_second_kernel, "mirror_second", [any_spec] * 2 + [smem] + [vmem] * 2,
                   [total], kernel_index, (*index, left, blocks), True)
    twin_mirror = shifted(mirror, "row", 1, n)
    held, = call(functools.partial(held_kernel, n), "held", [vmem] * (4 + n // 2), [total], [],
                 (left, stat_now, far, mirror, *far_parts))
    twin = shifted(held, "row", 1, n)
    others, mark = to_owners(mirror, twin_mirror)
    direct, stat = call(
        functools.partial(direct_second_kernel, n), "direct_second", [any_spec] * 2 + [smem] + [vmem] * 6,
        [total, tile], kernel_index, (*index, noise, blocks, left, held, twin, mark), True)
    parts = gathered(left, mirror, twin_mirror, others, direct, stat)
    return tuple(call(last_kernel, "last", [vmem] * (n + 3), [field, field], [],
                      (right_sides, left, stat_now, *parts)))


def solution(mesh):
    n = mesh.shape["row"]
    assert n == mesh.shape["col"] and n & (n - 1) == 0 and n >= 4
    placed = (
        P(None, ("groups", "row")),
        P(("groups", "row")),
        P(("groups", "row"), "col", None, None, None),
        P(("groups", "row"), "col", None),
        P(("groups", "row"), "col", None),
        P(("groups", "row"), "col"),
    )
    return jax.shard_map(
        functools.partial(on_device, n),
        mesh=mesh,
        in_specs=placed,
        out_specs=(P(None, ("groups", "row")), P(None, ("groups", "row"))),
        check_vma=False,
    )
```

```python
import functools

import jax
import jax.numpy as jnp
from jax import lax
from jax.experimental import pallas as pl
from jax.experimental.pallas import tpu as pltpu
from jax.sharding import PartitionSpec as P

ITERS = 2
LANES = 128
GROUP = 8
BF16 = jnp.bfloat16
F32 = jnp.float32


def shifted(value, axis, d, n):
    return lax.ppermute(value, axis, [(i, i ^ d) for i in range(n)])


def distances(n):
    return list(range(n - 1, 0, -1))


def moved(value, n, target):
    pairs = [(r * n + c, target(r, c)) for r in range(n) for c in range(n)]
    return lax.ppermute(value, ("row", "col"), [(s, t[0] * n + t[1]) for s, t in pairs])


def far_target(j):
    def target(r, c):
        d = r ^ c
        if d ^ 2 * j >= 2:
            return c ^ 2 * j, r
        return c ^ (d & 1) ^ (j == 0), c

    return target


def far_source(j, n):
    back = {far_target(j)(r, c): (r, c) for r in range(n) for c in range(n)}
    return lambda r, c: back[r, c]


def spread_target(b):
    def target(r, c):
        o = r ^ c
        move = {0: b, b: 1, b + 1: b, 1: 1}.get(o % (2 * b), 1)
        return r ^ move, c

    return target


def bits(n):
    return [1 << i for i in range(n.bit_length() - 1)]


def load_pair(dst, tile, value):
    rhs = value.shape[0]
    high = value.astype(BF16)
    dst[tile, :rhs, :] = high
    dst[tile, rhs:, :] = (value - high.astype(F32)).astype(BF16)


def product(pair, block, contract):
    both = lax.dot_general(pair, block, (((1,), (contract,)), ((), ())), preferred_element_type=F32)
    rhs = both.shape[0] // 2
    return both[:rhs] + both[rhs:]


def pack_stats(columns, rhs):
    lane = lax.broadcasted_iota(jnp.int32, (8, LANES), 1)
    tile = jnp.zeros((8, LANES), F32)
    groups = rhs // 8
    for i, column in enumerate(columns):
        for g in range(groups):
            tile = jnp.where(lane == i * groups + g, column[g * 8:(g + 1) * 8], tile)
    return tile


def unpack_stat(tile, i, rhs):
    groups = rhs // 8
    return jnp.concatenate([tile[:, i * groups + g:i * groups + g + 1] for g in range(groups)], axis=0)


def accumulate(total, tile, value):
    width = value.shape[1] // LANES
    for part in range(width):
        total[tile * width + part] += value[:, part * LANES:(part + 1) * LANES]


def add_blocks(blocks, slot_rows, slot_cols, live, pairs, total, mirror, wide, ready=None):
    read, write, contract = (slot_rows, slot_cols, 0) if mirror else (slot_cols, slot_rows, 1)

    def steps(group, base):
        def body(step, carry):
            if ready is not None:
                ready(step)
            for g in range(group):
                slot = base + step * group + g
                value = product(pairs[read[0, 0, slot]], blocks[slot], contract)
                accumulate(total, write[0, 0, slot], jnp.where(slot < live, value, 0.0))
            return carry

        return body

    done = 0
    if wide > GROUP:
        count = live // wide
        lax.fori_loop(0, count, steps(wide, 0), 0)
        done = count * wide
    lax.fori_loop(0, (live - done + GROUP - 1) // GROUP, steps(GROUP, done), 0)


def image_part(parts, me, i, per, rhs):
    rows = slice((i % per) * rhs, (i % per + 1) * rhs)
    value = parts[0][rows, :]
    for d, part in zip(distances(len(parts))[::-1], parts[1:]):
        value = jnp.where(me ^ d == i // per, part[rows, :], value)
    return value


def row_sums(value):
    return jnp.sum(value, axis=1, keepdims=True)


def cross_sums(total, value):
    rhs = value.shape[0]
    cross = jnp.zeros((rhs, LANES), F32)
    for i in range(total.shape[0]):
        cross += total[i] * value[:, i * LANES:(i + 1) * LANES]
    return row_sums(cross)


def tree_sum(values):
    values = list(values)
    while len(values) > 1:
        values = [a + b for a, b in zip(values[::2], values[1::2])]
    return values[0]


def stat_sum(parts, data):
    order = [0] + distances(len(parts))[::-1]
    return tree_sum(parts[order.index(d)][data:, :] for d in range(len(parts)))


def fetch_index(sources, targets, sems):
    copies = [pltpu.make_async_copy(s, t, sems.at[i]) for i, (s, t) in enumerate(zip(sources, targets))]
    for copy in copies:
        copy.start()
    return copies


def mirror_first_kernel(rows_hbm, cols_hbm, count, right_hbm, cov, total, blocks, *scratch):
    slot_rows, slot_cols, right, pairs, index_sems, right_sem, block_sems = scratch
    slots, tile_size = blocks.shape[:2]

    def block_copy(i):
        part = pl.ds(i * GROUP, GROUP)
        return pltpu.make_async_copy(cov.at[0, 0, part], blocks.at[part], block_sems.at[i])

    copies = fetch_index((rows_hbm, cols_hbm), (slot_rows, slot_cols), index_sems)
    load = pltpu.make_async_copy(right_hbm, right, right_sem)
    load.start()
    live = count[0, 0]
    for i in range(slots // GROUP):
        @pl.when(i * GROUP < live)
        def _():
            block_copy(i).start()
    total[...] = jnp.zeros_like(total)
    load.wait()
    for tile in range(right.shape[1] // tile_size):
        load_pair(pairs, tile, right[:, tile * tile_size:(tile + 1) * tile_size])
    for copy in copies:
        copy.wait()
    add_blocks(blocks, slot_rows, slot_cols, live, pairs, total, True, GROUP, lambda i: block_copy(i).wait())


def mirror_second_kernel(rows_any, cols_any, count, near, blocks, total, *scratch):
    slot_rows, slot_cols, pairs, index_sems = scratch
    tile_size = blocks.shape[1]
    copies = fetch_index((rows_any, cols_any), (slot_rows, slot_cols), index_sems)
    total[...] = jnp.zeros_like(total)
    for tile in range(near.shape[1] // tile_size):
        load_pair(pairs, tile, near[:, tile * tile_size:(tile + 1) * tile_size])
    for copy in copies:
        copy.wait()
    add_blocks(blocks, slot_rows, slot_cols, count[0, 0], pairs, total, True, 2 * GROUP)


def finish_direct(total, near, noise, stat, n):
    value = near[...]
    rhs = value.shape[0]
    square = value * value
    share = 1.0 / n
    bend = share * row_sums(square * noise[...]) + 2.0 * cross_sums(total, value)
    stat[...] = pack_stats([share * row_sums(square), bend], rhs)


def direct_first_kernel(n, rows_any, cols_any, count, noise, blocks, near, current, twin, mark, total, stat, far, *scratch):
    slot_rows, slot_cols, pairs, index_sems = scratch
    tile_size = blocks.shape[1]
    pieces = tile_size // LANES
    copies = fetch_index((rows_any, cols_any), (slot_rows, slot_cols), index_sems)
    odd = (lax.axis_index("row") ^ lax.axis_index("col")) & 1
    for o, source in enumerate((current, twin)):
        @pl.when(odd == o)
        def _():
            for tile in range(near.shape[1] // tile_size):
                value = source[:, tile * tile_size:(tile + 1) * tile_size]
                load_pair(pairs, tile, value)
                for i in range(pieces):
                    far[tile * pieces + i] = value[:, i * LANES:(i + 1) * LANES]
    total[...] = jnp.zeros_like(total)
    for copy in copies:
        copy.wait()
    add_blocks(blocks, slot_rows, slot_cols, count[0, 0], pairs, total, False, 2 * GROUP)
    finish_direct(total, near, noise, stat, n)


def direct_second_kernel(n, rows_any, cols_any, count, noise, blocks, near, held, twin, mark, total, stat, *scratch):
    slot_rows, slot_cols, pairs, index_sems = scratch
    tile_size = blocks.shape[1]
    pieces = tile_size // LANES
    per = held.shape[0] // n
    copies = fetch_index((rows_any, cols_any), (slot_rows, slot_cols), index_sems)
    row = lax.axis_index("row")
    offset = row ^ lax.axis_index("col")
    for tile in range(near.shape[1] // tile_size):
        value = []
        for i in range(tile * pieces, (tile + 1) * pieces):
            own = jnp.logical_or(offset == 0, jnp.logical_and(offset >= 2, ((i // per) ^ row) & 1 == 0))
            value.append(jnp.where(own, held[i], twin[i]))
        load_pair(pairs, tile, jnp.concatenate(value, axis=1))
    total[...] = jnp.zeros_like(total)
    for copy in copies:
        copy.wait()
    add_blocks(blocks, slot_rows, slot_cols, count[0, 0], pairs, total, False, 2 * GROUP)
    finish_direct(total, near, noise, stat, n)


def add_kernel(one, two, *refs):
    refs[-1][...] = one[...] + two[...]


def pick_kernel(b, current, arrived, mark, out):
    there = (lax.axis_index("row") ^ lax.axis_index("col")) & b
    out[...] = jnp.where(there != 0, arrived[...], current[...])


def split_kernel(n, mirror, twin, *outs):
    per = mirror.shape[0] // n
    rhs = mirror.shape[1]
    row = lax.axis_index("row")
    for j, out in enumerate(outs):
        first = (row ^ 2 * j) * per
        for i in range(per):
            out[i * rhs:(i + 1) * rhs, :] = mirror[first + i] + twin[first + i]


def merge_kernel(n, direct, mirror, twin, stat, *outs):
    per = direct.shape[0] // n
    rhs = direct.shape[1]
    me = lax.axis_index("col")
    diagonal = lax.axis_index("row") == me
    outs[n][...] = stat[...]
    for d, out in zip([0] + distances(n), outs):
        first = (me ^ d) * per

        @pl.when(diagonal)
        def _():
            for i in range(per):
                out[i * rhs:(i + 1) * rhs, :] = direct[first + i] + (mirror[first + i] + twin[first + i])

        @pl.when(jnp.logical_not(diagonal))
        def _():
            for i in range(per):
                out[i * rhs:(i + 1) * rhs, :] = direct[first + i]


def combine_kernel(n, near, noise, stat, *refs):
    parts, others, chunk = refs[:n], refs[n:-1], refs[-1]
    rhs = near.shape[0]
    data = parts[0].shape[0]
    per = data // rhs
    me = lax.axis_index("col")
    group = (lax.axis_index("row") ^ me) // 2
    value = tree_sum(ref[...] for ref in parts)
    for j, other in enumerate(others):
        value += jnp.where(group == j, 0.0, other[...])
    chunk[:data, :] = value
    chunk[data:, :] = stat[...]
    for k in range(n):
        @pl.when(me == k)
        def _():
            for i in range(per):
                lanes = slice((k * per + i) * LANES, (k * per + i + 1) * LANES)
                chunk[i * rhs:(i + 1) * rhs, :] += near[:, lanes] * noise[:, lanes]


def left_kernel(right, *refs):
    parts, (left, stat) = refs[:-2], refs[-2:]
    rhs, width = right.shape
    data = parts[0].shape[0] - 8
    per = data // rhs
    me = lax.axis_index("col")
    both = stat_sum(parts, data)
    stat[...] = both
    size_now = unpack_stat(both, 0, rhs) / unpack_stat(both, 1, rhs)
    for i in range(width // LANES):
        lanes = slice(i * LANES, (i + 1) * LANES)
        left[:, lanes] = right[:, lanes] - size_now * image_part(parts, me, i, per, rhs)


def held_kernel(n, left, stat, far, mark, *refs):
    parts, held = refs[:-1], refs[-1]
    rhs = left.shape[0]
    per = held.shape[0] // n
    row = lax.axis_index("row")
    diagonal = (row ^ lax.axis_index("col")) < 2
    size_now = unpack_stat(stat[...], 0, rhs) / unpack_stat(stat[...], 1, rhs)

    @pl.when(diagonal)
    def _():
        for i in range(held.shape[0]):
            held[i] = left[:, i * LANES:(i + 1) * LANES]

    @pl.when(jnp.logical_not(diagonal))
    def _():
        for j, part in enumerate(parts):
            first = (row ^ 2 * j) * per
            for i in range(per):
                held[first + i] = far[first + i] - size_now * part[i * rhs:(i + 1) * rhs, :]


def last_kernel(right, left, stat_now, *refs):
    parts, (solution, residual) = refs[:-2], refs[-2:]
    rhs, width = right.shape
    data = parts[0].shape[0] - 8
    per = data // rhs
    me = lax.axis_index("col")
    both = stat_sum(parts, data)
    norm = unpack_stat(stat_now[...], 0, rhs)
    norm_next = unpack_stat(both, 0, rhs)
    size_now = norm / unpack_stat(stat_now[...], 1, rhs)
    ratio = norm_next / norm
    size_next = norm_next / (unpack_stat(both, 1, rhs) - ratio * norm_next / size_now)
    back = ratio / size_now
    for i in range(width // LANES):
        lanes = slice(i * LANES, (i + 1) * LANES)
        first = right[:, lanes]
        now = left[:, lanes]
        solution[:, lanes] = size_now * first + size_next * (now + ratio * first)
        image = image_part(parts, me, i, per, rhs) + back * (first - now)
        residual[:, lanes] = now - size_next * image


def shape_of(*shape):
    return jax.ShapeDtypeStruct(shape, F32)


def on_device(n, right_sides, nugget, cov_blocks, block_rows, block_cols, block_count):
    rhs, width = right_sides.shape
    slots, tile_size = cov_blocks.shape[2:4]
    per = width // n // LANES
    data = per * rhs
    size = data + 8
    noise = nugget.reshape(1, width)
    index = (block_rows, block_cols, block_count)
    pair = pltpu.VMEM((width // tile_size, 2 * rhs, tile_size), BF16)
    index_scratch = [pltpu.SMEM(item.shape, item.dtype) for item in index[:2]]
    index_sems = pltpu.SemaphoreType.DMA((2,))
    vmem = pl.BlockSpec(memory_space=pltpu.VMEM)
    any_spec = pl.BlockSpec(memory_space=pl.ANY)
    smem = pl.BlockSpec(memory_space=pltpu.SMEM)
    hbm = pl.BlockSpec(memory_space=pltpu.HBM)
    params = pltpu.CompilerParams(vmem_limit_bytes=16 * 1024 * 1024)
    cost = pl.CostEstimate(flops=4 * rhs * slots * tile_size * tile_size, transcendentals=0,
                           bytes_accessed=2 * slots * tile_size * tile_size)
    field = shape_of(rhs, width)
    total = shape_of(width // LANES, rhs, LANES)
    chunk = shape_of(data, LANES)
    tile = shape_of(8, LANES)
    loaded = shape_of(size, LANES)

    def call(kernel, name, specs, outs, scratch, args, heavy=False):
        return pl.pallas_call(
            kernel,
            in_specs=specs,
            out_specs=jax.tree.map(lambda _: vmem, outs),
            out_shape=outs,
            scratch_shapes=scratch,
            compiler_params=params,
            cost_estimate=cost if heavy else None,
            name=name,
        )(*args)

    in_hbm = functools.partial(pltpu.with_memory_space_constraint, memory_space=pltpu.HBM)
    kernel_index = index_scratch + [pair, index_sems]

    def to_owners(mirror, twin):
        sent = call(functools.partial(split_kernel, n), "split", [vmem] * 2, [chunk] * (n // 2), [], (mirror, twin))
        return [moved(value, n, far_source(j, n)) for j, value in enumerate(sent)], sent[0]

    def gathered(near, mirror, twin, others, direct, stat):
        merged = call(functools.partial(merge_kernel, n), "merge", [vmem] * 4, [chunk] * n + [tile], [],
                      (direct, mirror, twin, stat))
        parts = [merged[0]] + [shifted(value, "col", d, n) for d, value in zip(distances(n), merged[1:n])]
        stat = merged[n]
        for b in bits(n):
            stat, = call(add_kernel, "add_stat", [vmem] * (2 + n // 2), [tile], [],
                         (stat, shifted(stat, "row", b, n), *others))
        own, = call(functools.partial(combine_kernel, n), "combine", [vmem] * (3 + n + n // 2), [loaded], [],
                    (near, noise, stat, *parts, *others))
        return [own] + [shifted(own, "col", d, n) for d in distances(n)[::-1]]

    current = right_sides
    for b in bits(n)[:0:-1]:
        arrived = moved(current, n, spread_target(b))
        if b == n // 2:
            mirror, blocks = call(
                mirror_first_kernel, "mirror_first", [hbm] * 2 + [smem] + [hbm] * 2,
                [total, jax.ShapeDtypeStruct(cov_blocks.shape[2:], cov_blocks.dtype)],
                index_scratch + [pltpu.VMEM((rhs, width), F32), pair, index_sems,
                                 pltpu.SemaphoreType.DMA, pltpu.SemaphoreType.DMA((slots // GROUP,))],
                (*map(in_hbm, index[:2]), block_count, in_hbm(right_sides), in_hbm(cov_blocks)), True)
            twin_mirror = shifted(mirror, "row", 1, n)
        current, = call(functools.partial(pick_kernel, b), "pick", [vmem] * 3, [field], [], (current, arrived, mirror))
    twin = shifted(current, "row", 1, n)
    others, mark = to_owners(mirror, twin_mirror)
    direct, stat, far = call(
        functools.partial(direct_first_kernel, n), "direct_first", [any_spec] * 2 + [smem] + [vmem] * 6,
        [total, tile, total], kernel_index, (*index, noise, blocks, right_sides, current, twin, mark), True)
    parts = gathered(right_sides, mirror, twin_mirror, others, direct, stat)
    far_parts = [moved(parts[0], n, far_target(j)) for j in range(n // 2)]

    left, stat_now = call(left_kernel, "left", [vmem] * (n + 1), [field, tile], [], (right_sides, *parts))
    mirror, = call(mirror_second_kernel, "mirror_second", [any_spec] * 2 + [smem] + [vmem] * 2,
                   [total], kernel_index, (*index, left, blocks), True)
    twin_mirror = shifted(mirror, "row", 1, n)
    held, = call(functools.partial(held_kernel, n), "held", [vmem] * (4 + n // 2), [total], [],
                 (left, stat_now, far, mirror, *far_parts))
    twin = shifted(held, "row", 1, n)
    others, mark = to_owners(mirror, twin_mirror)
    direct, stat = call(
        functools.partial(direct_second_kernel, n), "direct_second", [any_spec] * 2 + [smem] + [vmem] * 6,
        [total, tile], kernel_index, (*index, noise, blocks, left, held, twin, mark), True)
    parts = gathered(left, mirror, twin_mirror, others, direct, stat)
    return tuple(call(last_kernel, "last", [vmem] * (n + 3), [field, field], [],
                      (right_sides, left, stat_now, *parts)))


def solution(mesh):
    n = mesh.shape["row"]
    assert n == mesh.shape["col"] and n & (n - 1) == 0 and n >= 4
    placed = (
        P(None, ("groups", "row")),
        P(("groups", "row")),
        P(("groups", "row"), "col", None, None, None),
        P(("groups", "row"), "col", None),
        P(("groups", "row"), "col", None),
        P(("groups", "row"), "col"),
    )
    return jax.shard_map(
        functools.partial(on_device, n),
        mesh=mesh,
        in_specs=placed,
        out_specs=(P(None, ("groups", "row")), P(None, ("groups", "row"))),
        check_vma=False,
    )
```

```python
import functools

import jax
import jax.numpy as jnp
from jax import lax
from jax.experimental import pallas as pl
from jax.experimental.pallas import tpu as pltpu
from jax.sharding import PartitionSpec as P

ITERS = 2
LANES = 128
GROUP = 8
BF16 = jnp.bfloat16
F32 = jnp.float32


def shifted(value, axis, d, n):
    return lax.ppermute(value, axis, [(i, i ^ d) for i in range(n)])


def distances(n):
    return list(range(n - 1, 0, -1))


def moved(value, n, target):
    pairs = [(r * n + c, target(r, c)) for r in range(n) for c in range(n)]
    return lax.ppermute(value, ("row", "col"), [(s, t[0] * n + t[1]) for s, t in pairs])


def far_target(j):
    def target(r, c):
        d = r ^ c
        if d ^ 2 * j >= 2:
            return c ^ 2 * j, r
        return c ^ (d & 1) ^ (j == 0), c

    return target


def far_source(j, n):
    back = {far_target(j)(r, c): (r, c) for r in range(n) for c in range(n)}
    return lambda r, c: back[r, c]


def spread_target(b):
    def target(r, c):
        o = r ^ c
        move = {0: b, b: 1, b + 1: b, 1: 1}.get(o % (2 * b), 1)
        return r ^ move, c

    return target


def bits(n):
    return [1 << i for i in range(n.bit_length() - 1)]


def load_pair(dst, tile, value):
    rhs = value.shape[0]
    high = value.astype(BF16)
    dst[tile, :rhs, :] = high
    dst[tile, rhs:, :] = (value - high.astype(F32)).astype(BF16)


def product(pair, block, contract):
    both = lax.dot_general(pair, block, (((1,), (contract,)), ((), ())), preferred_element_type=F32)
    rhs = both.shape[0] // 2
    return both[:rhs] + both[rhs:]


def pack_stats(columns, rhs):
    lane = lax.broadcasted_iota(jnp.int32, (8, LANES), 1)
    tile = jnp.zeros((8, LANES), F32)
    groups = rhs // 8
    for i, column in enumerate(columns):
        for g in range(groups):
            tile = jnp.where(lane == i * groups + g, column[g * 8:(g + 1) * 8], tile)
    return tile


def unpack_stat(tile, i, rhs):
    groups = rhs // 8
    return jnp.concatenate([tile[:, i * groups + g:i * groups + g + 1] for g in range(groups)], axis=0)


def accumulate(total, tile, value):
    width = value.shape[1] // LANES
    for part in range(width):
        total[tile * width + part] += value[:, part * LANES:(part + 1) * LANES]


def add_blocks(blocks, slot_rows, slot_cols, live, pairs, total, mirror, wide, ready=None):
    read, write, contract = (slot_rows, slot_cols, 0) if mirror else (slot_cols, slot_rows, 1)

    def steps(group, base):
        def body(step, carry):
            if ready is not None:
                ready(step)
            for g in range(group):
                slot = base + step * group + g
                value = product(pairs[read[0, 0, slot]], blocks[slot], contract)
                accumulate(total, write[0, 0, slot], jnp.where(slot < live, value, 0.0))
            return carry

        return body

    done = 0
    if wide > GROUP:
        count = live // wide
        lax.fori_loop(0, count, steps(wide, 0), 0)
        done = count * wide
    lax.fori_loop(0, (live - done + GROUP - 1) // GROUP, steps(GROUP, done), 0)


def image_part(parts, me, i, per, rhs):
    rows = slice((i % per) * rhs, (i % per + 1) * rhs)
    value = parts[0][rows, :]
    for d, part in zip(distances(len(parts))[::-1], parts[1:]):
        value = jnp.where(me ^ d == i // per, part[rows, :], value)
    return value


def row_sums(value):
    return jnp.sum(value, axis=1, keepdims=True)


def cross_sums(total, value):
    rhs = value.shape[0]
    cross = jnp.zeros((rhs, LANES), F32)
    for i in range(total.shape[0]):
        cross += total[i] * value[:, i * LANES:(i + 1) * LANES]
    return row_sums(cross)


def tree_sum(values):
    values = list(values)
    while len(values) > 1:
        values = [a + b for a, b in zip(values[::2], values[1::2])]
    return values[0]


def stat_sum(parts, data):
    order = [0] + distances(len(parts))[::-1]
    return tree_sum(parts[order.index(d)][data:, :] for d in range(len(parts)))


def fetch_index(sources, targets, sems):
    copies = [pltpu.make_async_copy(s, t, sems.at[i]) for i, (s, t) in enumerate(zip(sources, targets))]
    for copy in copies:
        copy.start()
    return copies


def mirror_first_kernel(rows_hbm, cols_hbm, count, right_hbm, cov, total, blocks, *scratch):
    slot_rows, slot_cols, right, pairs, index_sems, right_sem, block_sems = scratch
    slots, tile_size = blocks.shape[:2]

    def block_copy(i):
        part = pl.ds(i * GROUP, GROUP)
        return pltpu.make_async_copy(cov.at[0, 0, part], blocks.at[part], block_sems.at[i])

    copies = fetch_index((rows_hbm, cols_hbm), (slot_rows, slot_cols), index_sems)
    load = pltpu.make_async_copy(right_hbm, right, right_sem)
    load.start()
    live = count[0, 0]
    for i in range(slots // GROUP):
        @pl.when(i * GROUP < live)
        def _():
            block_copy(i).start()
    total[...] = jnp.zeros_like(total)
    load.wait()
    for tile in range(right.shape[1] // tile_size):
        load_pair(pairs, tile, right[:, tile * tile_size:(tile + 1) * tile_size])
    for copy in copies:
        copy.wait()
    add_blocks(blocks, slot_rows, slot_cols, live, pairs, total, True, GROUP, lambda i: block_copy(i).wait())


def mirror_second_kernel(rows_any, cols_any, count, near, blocks, total, *scratch):
    slot_rows, slot_cols, pairs, index_sems = scratch
    tile_size = blocks.shape[1]
    copies = fetch_index((rows_any, cols_any), (slot_rows, slot_cols), index_sems)
    total[...] = jnp.zeros_like(total)
    for tile in range(near.shape[1] // tile_size):
        load_pair(pairs, tile, near[:, tile * tile_size:(tile + 1) * tile_size])
    for copy in copies:
        copy.wait()
    add_blocks(blocks, slot_rows, slot_cols, count[0, 0], pairs, total, True, 2 * GROUP)


def finish_direct(total, near, noise, stat, n):
    value = near[...]
    rhs = value.shape[0]
    square = value * value
    share = 1.0 / n
    bend = share * row_sums(square * noise[...]) + 2.0 * cross_sums(total, value)
    stat[...] = pack_stats([share * row_sums(square), bend], rhs)


def direct_first_kernel(n, rows_any, cols_any, count, noise, blocks, near, current, twin, mark, total, stat, far, *scratch):
    slot_rows, slot_cols, pairs, index_sems = scratch
    tile_size = blocks.shape[1]
    pieces = tile_size // LANES
    copies = fetch_index((rows_any, cols_any), (slot_rows, slot_cols), index_sems)
    odd = (lax.axis_index("row") ^ lax.axis_index("col")) & 1
    for o, source in enumerate((current, twin)):
        @pl.when(odd == o)
        def _():
            for tile in range(near.shape[1] // tile_size):
                value = source[:, tile * tile_size:(tile + 1) * tile_size]
                load_pair(pairs, tile, value)
                for i in range(pieces):
                    far[tile * pieces + i] = value[:, i * LANES:(i + 1) * LANES]
    total[...] = jnp.zeros_like(total)
    for copy in copies:
        copy.wait()
    add_blocks(blocks, slot_rows, slot_cols, count[0, 0], pairs, total, False, 2 * GROUP)
    finish_direct(total, near, noise, stat, n)


def direct_second_kernel(n, rows_any, cols_any, count, noise, blocks, near, held, twin, mark, total, stat, *scratch):
    slot_rows, slot_cols, pairs, index_sems = scratch
    tile_size = blocks.shape[1]
    pieces = tile_size // LANES
    per = held.shape[0] // n
    copies = fetch_index((rows_any, cols_any), (slot_rows, slot_cols), index_sems)
    row = lax.axis_index("row")
    offset = row ^ lax.axis_index("col")
    for tile in range(near.shape[1] // tile_size):
        value = []
        for i in range(tile * pieces, (tile + 1) * pieces):
            own = jnp.logical_or(offset == 0, jnp.logical_and(offset >= 2, ((i // per) ^ row) & 1 == 0))
            value.append(jnp.where(own, held[i], twin[i]))
        load_pair(pairs, tile, jnp.concatenate(value, axis=1))
    total[...] = jnp.zeros_like(total)
    for copy in copies:
        copy.wait()
    add_blocks(blocks, slot_rows, slot_cols, count[0, 0], pairs, total, False, 2 * GROUP)
    finish_direct(total, near, noise, stat, n)


def add_kernel(one, two, *refs):
    refs[-1][...] = one[...] + two[...]


def pick_kernel(b, current, arrived, mark, out):
    there = (lax.axis_index("row") ^ lax.axis_index("col")) & b
    out[...] = jnp.where(there != 0, arrived[...], current[...])


def split_kernel(n, mirror, twin, *outs):
    per = mirror.shape[0] // n
    rhs = mirror.shape[1]
    row = lax.axis_index("row")
    for j, out in enumerate(outs):
        first = (row ^ 2 * j) * per
        for i in range(per):
            out[i * rhs:(i + 1) * rhs, :] = mirror[first + i] + twin[first + i]


def merge_kernel(n, direct, mirror, twin, stat, *outs):
    per = direct.shape[0] // n
    rhs = direct.shape[1]
    me = lax.axis_index("col")
    diagonal = lax.axis_index("row") == me
    outs[n][...] = stat[...]
    for d, out in zip([0] + distances(n), outs):
        first = (me ^ d) * per

        @pl.when(diagonal)
        def _():
            for i in range(per):
                out[i * rhs:(i + 1) * rhs, :] = direct[first + i] + (mirror[first + i] + twin[first + i])

        @pl.when(jnp.logical_not(diagonal))
        def _():
            for i in range(per):
                out[i * rhs:(i + 1) * rhs, :] = direct[first + i]


def combine_kernel(n, near, noise, stat, *refs):
    parts, others, chunk = refs[:n], refs[n:-1], refs[-1]
    rhs = near.shape[0]
    data = parts[0].shape[0]
    per = data // rhs
    me = lax.axis_index("col")
    group = (lax.axis_index("row") ^ me) // 2
    value = tree_sum(ref[...] for ref in parts)
    for j, other in enumerate(others):
        value += jnp.where(group == j, 0.0, other[...])
    chunk[:data, :] = value
    chunk[data:, :] = stat[...]
    for k in range(n):
        @pl.when(me == k)
        def _():
            for i in range(per):
                lanes = slice((k * per + i) * LANES, (k * per + i + 1) * LANES)
                chunk[i * rhs:(i + 1) * rhs, :] += near[:, lanes] * noise[:, lanes]


def left_kernel(right, *refs):
    parts, (left, stat) = refs[:-2], refs[-2:]
    rhs, width = right.shape
    data = parts[0].shape[0] - 8
    per = data // rhs
    me = lax.axis_index("col")
    both = stat_sum(parts, data)
    stat[...] = both
    size_now = unpack_stat(both, 0, rhs) / unpack_stat(both, 1, rhs)
    for i in range(width // LANES):
        lanes = slice(i * LANES, (i + 1) * LANES)
        left[:, lanes] = right[:, lanes] - size_now * image_part(parts, me, i, per, rhs)


def held_kernel(n, left, stat, far, mark, *refs):
    parts, held = refs[:-1], refs[-1]
    rhs = left.shape[0]
    per = held.shape[0] // n
    row = lax.axis_index("row")
    diagonal = (row ^ lax.axis_index("col")) < 2
    size_now = unpack_stat(stat[...], 0, rhs) / unpack_stat(stat[...], 1, rhs)

    @pl.when(diagonal)
    def _():
        for i in range(held.shape[0]):
            held[i] = left[:, i * LANES:(i + 1) * LANES]

    @pl.when(jnp.logical_not(diagonal))
    def _():
        for j, part in enumerate(parts):
            first = (row ^ 2 * j) * per
            for i in range(per):
                held[first + i] = far[first + i] - size_now * part[i * rhs:(i + 1) * rhs, :]


def last_kernel(right, left, stat_now, *refs):
    parts, (solution, residual) = refs[:-2], refs[-2:]
    rhs, width = right.shape
    data = parts[0].shape[0] - 8
    per = data // rhs
    me = lax.axis_index("col")
    both = stat_sum(parts, data)
    norm = unpack_stat(stat_now[...], 0, rhs)
    norm_next = unpack_stat(both, 0, rhs)
    size_now = norm / unpack_stat(stat_now[...], 1, rhs)
    ratio = norm_next / norm
    size_next = norm_next / (unpack_stat(both, 1, rhs) - ratio * norm_next / size_now)
    back = ratio / size_now
    for i in range(width // LANES):
        lanes = slice(i * LANES, (i + 1) * LANES)
        first = right[:, lanes]
        now = left[:, lanes]
        solution[:, lanes] = size_now * first + size_next * (now + ratio * first)
        image = image_part(parts, me, i, per, rhs) + back * (first - now)
        residual[:, lanes] = now - size_next * image


def shape_of(*shape):
    return jax.ShapeDtypeStruct(shape, F32)


def on_device(n, right_sides, nugget, cov_blocks, block_rows, block_cols, block_count):
    rhs, width = right_sides.shape
    slots, tile_size = cov_blocks.shape[2:4]
    per = width // n // LANES
    data = per * rhs
    size = data + 8
    noise = nugget.reshape(1, width)
    index = (block_rows, block_cols, block_count)
    pair = pltpu.VMEM((width // tile_size, 2 * rhs, tile_size), BF16)
    index_scratch = [pltpu.SMEM(item.shape, item.dtype) for item in index[:2]]
    index_sems = pltpu.SemaphoreType.DMA((2,))
    vmem = pl.BlockSpec(memory_space=pltpu.VMEM)
    any_spec = pl.BlockSpec(memory_space=pl.ANY)
    smem = pl.BlockSpec(memory_space=pltpu.SMEM)
    hbm = pl.BlockSpec(memory_space=pltpu.HBM)
    params = pltpu.CompilerParams(vmem_limit_bytes=16 * 1024 * 1024)
    cost = pl.CostEstimate(flops=4 * rhs * slots * tile_size * tile_size, transcendentals=0,
                           bytes_accessed=2 * slots * tile_size * tile_size)
    field = shape_of(rhs, width)
    total = shape_of(width // LANES, rhs, LANES)
    chunk = shape_of(data, LANES)
    tile = shape_of(8, LANES)
    loaded = shape_of(size, LANES)

    def call(kernel, name, specs, outs, scratch, args, heavy=False):
        return pl.pallas_call(
            kernel,
            in_specs=specs,
            out_specs=jax.tree.map(lambda _: vmem, outs),
            out_shape=outs,
            scratch_shapes=scratch,
            compiler_params=params,
            cost_estimate=cost if heavy else None,
            name=name,
        )(*args)

    in_hbm = functools.partial(pltpu.with_memory_space_constraint, memory_space=pltpu.HBM)
    kernel_index = index_scratch + [pair, index_sems]

    def to_owners(mirror, twin):
        sent = call(functools.partial(split_kernel, n), "split", [vmem] * 2, [chunk] * (n // 2), [], (mirror, twin))
        return [moved(value, n, far_source(j, n)) for j, value in enumerate(sent)], sent[0]

    def gathered(near, mirror, twin, others, direct, stat):
        merged = call(functools.partial(merge_kernel, n), "merge", [vmem] * 4, [chunk] * n + [tile], [],
                      (direct, mirror, twin, stat))
        parts = [merged[0]] + [shifted(value, "col", d, n) for d, value in zip(distances(n), merged[1:n])]
        stat = merged[n]
        for b in bits(n)[::-1]:
            stat, = call(add_kernel, "add_stat", [vmem] * (2 + n // 2), [tile], [],
                         (stat, shifted(stat, "row", b, n), *others))
        own, = call(functools.partial(combine_kernel, n), "combine", [vmem] * (3 + n + n // 2), [loaded], [],
                    (near, noise, stat, *parts, *others))
        return [own] + [shifted(own, "col", d, n) for d in distances(n)[::-1]]

    current = right_sides
    for b in bits(n)[:0:-1]:
        arrived = moved(current, n, spread_target(b))
        if b == n // 2:
            mirror, blocks = call(
                mirror_first_kernel, "mirror_first", [hbm] * 2 + [smem] + [hbm] * 2,
                [total, jax.ShapeDtypeStruct(cov_blocks.shape[2:], cov_blocks.dtype)],
                index_scratch + [pltpu.VMEM((rhs, width), F32), pair, index_sems,
                                 pltpu.SemaphoreType.DMA, pltpu.SemaphoreType.DMA((slots // GROUP,))],
                (*map(in_hbm, index[:2]), block_count, in_hbm(right_sides), in_hbm(cov_blocks)), True)
            twin_mirror = shifted(mirror, "row", 1, n)
        current, = call(functools.partial(pick_kernel, b), "pick", [vmem] * 3, [field], [], (current, arrived, mirror))
    twin = shifted(current, "row", 1, n)
    others, mark = to_owners(mirror, twin_mirror)
    direct, stat, far = call(
        functools.partial(direct_first_kernel, n), "direct_first", [any_spec] * 2 + [smem] + [vmem] * 6,
        [total, tile, total], kernel_index, (*index, noise, blocks, right_sides, current, twin, mark), True)
    parts = gathered(right_sides, mirror, twin_mirror, others, direct, stat)
    far_parts = [moved(parts[0], n, far_target(j)) for j in range(n // 2)]

    left, stat_now = call(left_kernel, "left", [vmem] * (n + 1), [field, tile], [], (right_sides, *parts))
    mirror, = call(mirror_second_kernel, "mirror_second", [any_spec] * 2 + [smem] + [vmem] * 2,
                   [total], kernel_index, (*index, left, blocks), True)
    twin_mirror = shifted(mirror, "row", 1, n)
    held, = call(functools.partial(held_kernel, n), "held", [vmem] * (4 + n // 2), [total], [],
                 (left, stat_now, far, mirror, *far_parts))
    twin = shifted(held, "row", 1, n)
    others, mark = to_owners(mirror, twin_mirror)
    direct, stat = call(
        functools.partial(direct_second_kernel, n), "direct_second", [any_spec] * 2 + [smem] + [vmem] * 6,
        [total, tile], kernel_index, (*index, noise, blocks, left, held, twin, mark), True)
    parts = gathered(left, mirror, twin_mirror, others, direct, stat)
    return tuple(call(last_kernel, "last", [vmem] * (n + 3), [field, field], [],
                      (right_sides, left, stat_now, *parts)))


def solution(mesh):
    n = mesh.shape["row"]
    assert n == mesh.shape["col"] and n & (n - 1) == 0 and n >= 4
    placed = (
        P(None, ("groups", "row")),
        P(("groups", "row")),
        P(("groups", "row"), "col", None, None, None),
        P(("groups", "row"), "col", None),
        P(("groups", "row"), "col", None),
        P(("groups", "row"), "col"),
    )
    return jax.shard_map(
        functools.partial(on_device, n),
        mesh=mesh,
        in_specs=placed,
        out_specs=(P(None, ("groups", "row")), P(None, ("groups", "row"))),
        check_vma=False,
    )
```

```python
import functools

import jax
import jax.numpy as jnp
from jax import lax
from jax.experimental import pallas as pl
from jax.experimental.pallas import tpu as pltpu
from jax.sharding import PartitionSpec as P

ITERS = 2
LANES = 128
GROUP = 8
BF16 = jnp.bfloat16
F32 = jnp.float32


def shifted(value, axis, d, n):
    return lax.ppermute(value, axis, [(i, i ^ d) for i in range(n)])


def distances(n):
    return list(range(n - 1, 0, -1))


def moved(value, n, target):
    pairs = [(r * n + c, target(r, c)) for r in range(n) for c in range(n)]
    return lax.ppermute(value, ("row", "col"), [(s, t[0] * n + t[1]) for s, t in pairs])


def far_target(j):
    def target(r, c):
        d = r ^ c
        if d ^ 2 * j >= 2:
            return c ^ 2 * j, r
        return c ^ (d & 1) ^ (j == 0), c

    return target


def far_source(j, n):
    back = {far_target(j)(r, c): (r, c) for r in range(n) for c in range(n)}
    return lambda r, c: back[r, c]


def spread_target(b):
    def target(r, c):
        o = r ^ c
        move = {0: b, b: 1, b + 1: b, 1: 1}.get(o % (2 * b), 1)
        return r ^ move, c

    return target


def bits(n):
    return [1 << i for i in range(n.bit_length() - 1)]


def load_pair(dst, tile, value):
    rhs = value.shape[0]
    high = value.astype(BF16)
    dst[tile, :rhs, :] = high
    dst[tile, rhs:, :] = (value - high.astype(F32)).astype(BF16)


def product(pair, block, contract):
    both = lax.dot_general(pair, block, (((1,), (contract,)), ((), ())), preferred_element_type=F32)
    rhs = both.shape[0] // 2
    return both[:rhs] + both[rhs:]


def pack_stats(columns, rhs):
    lane = lax.broadcasted_iota(jnp.int32, (8, LANES), 1)
    tile = jnp.zeros((8, LANES), F32)
    groups = rhs // 8
    for i, column in enumerate(columns):
        for g in range(groups):
            tile = jnp.where(lane == i * groups + g, column[g * 8:(g + 1) * 8], tile)
    return tile


def unpack_stat(tile, i, rhs):
    groups = rhs // 8
    return jnp.concatenate([tile[:, i * groups + g:i * groups + g + 1] for g in range(groups)], axis=0)


def accumulate(total, tile, value):
    width = value.shape[1] // LANES
    for part in range(width):
        total[tile * width + part] += value[:, part * LANES:(part + 1) * LANES]


def add_blocks(blocks, slot_rows, slot_cols, live, pairs, total, mirror, wide, ready=None):
    read, write, contract = (slot_rows, slot_cols, 0) if mirror else (slot_cols, slot_rows, 1)

    def steps(group, base):
        def body(step, carry):
            if ready is not None:
                ready(step)
            for g in range(group):
                slot = base + step * group + g
                value = product(pairs[read[0, 0, slot]], blocks[slot], contract)
                accumulate(total, write[0, 0, slot], jnp.where(slot < live, value, 0.0))
            return carry

        return body

    done = 0
    if wide > GROUP:
        count = live // wide
        lax.fori_loop(0, count, steps(wide, 0), 0)
        done = count * wide
    lax.fori_loop(0, (live - done + GROUP - 1) // GROUP, steps(GROUP, done), 0)


def image_part(parts, me, i, per, rhs):
    rows = slice((i % per) * rhs, (i % per + 1) * rhs)
    value = parts[0][rows, :]
    for d, part in zip(distances(len(parts))[::-1], parts[1:]):
        value = jnp.where(me ^ d == i // per, part[rows, :], value)
    return value


def row_sums(value):
    return jnp.sum(value, axis=1, keepdims=True)


def cross_sums(total, value):
    rhs = value.shape[0]
    cross = jnp.zeros((rhs, LANES), F32)
    for i in range(total.shape[0]):
        cross += total[i] * value[:, i * LANES:(i + 1) * LANES]
    return row_sums(cross)


def tree_sum(values):
    values = list(values)
    while len(values) > 1:
        values = [a + b for a, b in zip(values[::2], values[1::2])]
    return values[0]


def stat_sum(parts, data):
    order = [0] + distances(len(parts))[::-1]
    return tree_sum(parts[order.index(d)][data:, :] for d in range(len(parts)))


def fetch_index(sources, targets, sems):
    copies = [pltpu.make_async_copy(s, t, sems.at[i]) for i, (s, t) in enumerate(zip(sources, targets))]
    for copy in copies:
        copy.start()
    return copies


def mirror_first_kernel(rows_hbm, cols_hbm, count, right_hbm, cov, total, blocks, *scratch):
    slot_rows, slot_cols, right, pairs, index_sems, right_sem, block_sems = scratch
    slots, tile_size = blocks.shape[:2]

    def block_copy(i):
        part = pl.ds(i * GROUP, GROUP)
        return pltpu.make_async_copy(cov.at[0, 0, part], blocks.at[part], block_sems.at[i])

    copies = fetch_index((rows_hbm, cols_hbm), (slot_rows, slot_cols), index_sems)
    load = pltpu.make_async_copy(right_hbm, right, right_sem)
    load.start()
    live = count[0, 0]
    for i in range(slots // GROUP):
        @pl.when(i * GROUP < live)
        def _():
            block_copy(i).start()
    total[...] = jnp.zeros_like(total)
    load.wait()
    for tile in range(right.shape[1] // tile_size):
        load_pair(pairs, tile, right[:, tile * tile_size:(tile + 1) * tile_size])
    for copy in copies:
        copy.wait()
    add_blocks(blocks, slot_rows, slot_cols, live, pairs, total, True, GROUP, lambda i: block_copy(i).wait())


def mirror_second_kernel(rows_any, cols_any, count, near, blocks, total, *scratch):
    slot_rows, slot_cols, pairs, index_sems = scratch
    tile_size = blocks.shape[1]
    copies = fetch_index((rows_any, cols_any), (slot_rows, slot_cols), index_sems)
    total[...] = jnp.zeros_like(total)
    for tile in range(near.shape[1] // tile_size):
        load_pair(pairs, tile, near[:, tile * tile_size:(tile + 1) * tile_size])
    for copy in copies:
        copy.wait()
    add_blocks(blocks, slot_rows, slot_cols, count[0, 0], pairs, total, True, 2 * GROUP)


def finish_direct(total, near, noise, stat, n):
    value = near[...]
    rhs = value.shape[0]
    square = value * value
    share = 1.0 / n
    bend = share * row_sums(square * noise[...]) + 2.0 * cross_sums(total, value)
    stat[...] = pack_stats([share * row_sums(square), bend], rhs)


def direct_first_kernel(n, rows_any, cols_any, count, noise, blocks, near, current, twin, mark, total, stat, far, *scratch):
    slot_rows, slot_cols, pairs, index_sems = scratch
    tile_size = blocks.shape[1]
    pieces = tile_size // LANES
    copies = fetch_index((rows_any, cols_any), (slot_rows, slot_cols), index_sems)
    odd = (lax.axis_index("row") ^ lax.axis_index("col")) & 1
    for o, source in enumerate((current, twin)):
        @pl.when(odd == o)
        def _():
            for tile in range(near.shape[1] // tile_size):
                value = source[:, tile * tile_size:(tile + 1) * tile_size]
                load_pair(pairs, tile, value)
                for i in range(pieces):
                    far[tile * pieces + i] = value[:, i * LANES:(i + 1) * LANES]
    total[...] = jnp.zeros_like(total)
    for copy in copies:
        copy.wait()
    add_blocks(blocks, slot_rows, slot_cols, count[0, 0], pairs, total, False, 2 * GROUP)
    finish_direct(total, near, noise, stat, n)


def direct_second_kernel(n, rows_any, cols_any, count, noise, blocks, near, held, twin, mark, total, stat, *scratch):
    slot_rows, slot_cols, pairs, index_sems = scratch
    tile_size = blocks.shape[1]
    pieces = tile_size // LANES
    per = held.shape[0] // n
    copies = fetch_index((rows_any, cols_any), (slot_rows, slot_cols), index_sems)
    row = lax.axis_index("row")
    offset = row ^ lax.axis_index("col")
    for tile in range(near.shape[1] // tile_size):
        value = []
        for i in range(tile * pieces, (tile + 1) * pieces):
            own = jnp.logical_or(offset == 0, jnp.logical_and(offset >= 2, ((i // per) ^ row) & 1 == 0))
            value.append(jnp.where(own, held[i], twin[i]))
        load_pair(pairs, tile, jnp.concatenate(value, axis=1))
    total[...] = jnp.zeros_like(total)
    for copy in copies:
        copy.wait()
    add_blocks(blocks, slot_rows, slot_cols, count[0, 0], pairs, total, False, 2 * GROUP)
    finish_direct(total, near, noise, stat, n)


def add_kernel(one, two, *refs):
    refs[-1][...] = one[...] + two[...]


def pick_kernel(b, current, arrived, mark, out):
    there = (lax.axis_index("row") ^ lax.axis_index("col")) & b
    out[...] = jnp.where(there != 0, arrived[...], current[...])


def split_kernel(n, mirror, twin, *outs):
    per = mirror.shape[0] // n
    rhs = mirror.shape[1]
    row = lax.axis_index("row")
    for j, out in enumerate(outs):
        first = (row ^ 2 * j) * per
        for i in range(per):
            out[i * rhs:(i + 1) * rhs, :] = mirror[first + i] + twin[first + i]


def merge_kernel(n, direct, mirror, twin, stat, *outs):
    per = direct.shape[0] // n
    rhs = direct.shape[1]
    me = lax.axis_index("col")
    diagonal = lax.axis_index("row") == me
    outs[n][...] = stat[...]
    for d, out in zip([0] + distances(n), outs):
        first = (me ^ d) * per

        @pl.when(diagonal)
        def _():
            for i in range(per):
                out[i * rhs:(i + 1) * rhs, :] = direct[first + i] + (mirror[first + i] + twin[first + i])

        @pl.when(jnp.logical_not(diagonal))
        def _():
            for i in range(per):
                out[i * rhs:(i + 1) * rhs, :] = direct[first + i]


def combine_kernel(n, near, noise, stat, *refs):
    parts, others, chunk = refs[:n], refs[n:-1], refs[-1]
    rhs = near.shape[0]
    data = parts[0].shape[0]
    per = data // rhs
    me = lax.axis_index("col")
    group = (lax.axis_index("row") ^ me) // 2
    value = tree_sum(ref[...] for ref in parts)
    for j, other in enumerate(others):
        value += jnp.where(group == j, 0.0, other[...])
    chunk[:data, :] = value
    chunk[data:, :] = stat[...]
    for k in range(n):
        @pl.when(me == k)
        def _():
            for i in range(per):
                lanes = slice((k * per + i) * LANES, (k * per + i + 1) * LANES)
                chunk[i * rhs:(i + 1) * rhs, :] += near[:, lanes] * noise[:, lanes]


def left_kernel(right, *refs):
    parts, (left, stat) = refs[:-2], refs[-2:]
    rhs, width = right.shape
    data = parts[0].shape[0] - 8
    per = data // rhs
    me = lax.axis_index("col")
    both = stat_sum(parts, data)
    stat[...] = both
    size_now = unpack_stat(both, 0, rhs) / unpack_stat(both, 1, rhs)
    for i in range(width // LANES):
        lanes = slice(i * LANES, (i + 1) * LANES)
        left[:, lanes] = right[:, lanes] - size_now * image_part(parts, me, i, per, rhs)


def held_kernel(n, left, stat, far, mark, *refs):
    parts, held = refs[:-1], refs[-1]
    rhs = left.shape[0]
    per = held.shape[0] // n
    row = lax.axis_index("row")
    diagonal = (row ^ lax.axis_index("col")) < 2
    size_now = unpack_stat(stat[...], 0, rhs) / unpack_stat(stat[...], 1, rhs)

    @pl.when(diagonal)
    def _():
        for i in range(held.shape[0]):
            held[i] = left[:, i * LANES:(i + 1) * LANES]

    @pl.when(jnp.logical_not(diagonal))
    def _():
        for j, part in enumerate(parts):
            first = (row ^ 2 * j) * per
            for i in range(per):
                held[first + i] = far[first + i] - size_now * part[i * rhs:(i + 1) * rhs, :]


def last_kernel(right, left, stat_now, *refs):
    parts, (solution, residual) = refs[:-2], refs[-2:]
    rhs, width = right.shape
    data = parts[0].shape[0] - 8
    per = data // rhs
    me = lax.axis_index("col")
    both = stat_sum(parts, data)
    norm = unpack_stat(stat_now[...], 0, rhs)
    norm_next = unpack_stat(both, 0, rhs)
    size_now = norm / unpack_stat(stat_now[...], 1, rhs)
    ratio = norm_next / norm
    size_next = norm_next / (unpack_stat(both, 1, rhs) - ratio * norm_next / size_now)
    back = ratio / size_now
    for i in range(width // LANES):
        lanes = slice(i * LANES, (i + 1) * LANES)
        first = right[:, lanes]
        now = left[:, lanes]
        solution[:, lanes] = size_now * first + size_next * (now + ratio * first)
        image = image_part(parts, me, i, per, rhs) + back * (first - now)
        residual[:, lanes] = now - size_next * image


def shape_of(*shape):
    return jax.ShapeDtypeStruct(shape, F32)


def on_device(n, right_sides, nugget, cov_blocks, block_rows, block_cols, block_count):
    rhs, width = right_sides.shape
    slots, tile_size = cov_blocks.shape[2:4]
    per = width // n // LANES
    data = per * rhs
    size = data + 8
    noise = nugget.reshape(1, width)
    index = (block_rows, block_cols, block_count)
    pair = pltpu.VMEM((width // tile_size, 2 * rhs, tile_size), BF16)
    index_scratch = [pltpu.SMEM(item.shape, item.dtype) for item in index[:2]]
    index_sems = pltpu.SemaphoreType.DMA((2,))
    vmem = pl.BlockSpec(memory_space=pltpu.VMEM)
    any_spec = pl.BlockSpec(memory_space=pl.ANY)
    smem = pl.BlockSpec(memory_space=pltpu.SMEM)
    hbm = pl.BlockSpec(memory_space=pltpu.HBM)
    params = pltpu.CompilerParams(vmem_limit_bytes=16 * 1024 * 1024)
    cost = pl.CostEstimate(flops=4 * rhs * slots * tile_size * tile_size, transcendentals=0,
                           bytes_accessed=2 * slots * tile_size * tile_size)
    field = shape_of(rhs, width)
    total = shape_of(width // LANES, rhs, LANES)
    chunk = shape_of(data, LANES)
    tile = shape_of(8, LANES)
    loaded = shape_of(size, LANES)

    def call(kernel, name, specs, outs, scratch, args, heavy=False):
        return pl.pallas_call(
            kernel,
            in_specs=specs,
            out_specs=jax.tree.map(lambda _: vmem, outs),
            out_shape=outs,
            scratch_shapes=scratch,
            compiler_params=params,
            cost_estimate=cost if heavy else None,
            name=name,
        )(*args)

    in_hbm = functools.partial(pltpu.with_memory_space_constraint, memory_space=pltpu.HBM)
    kernel_index = index_scratch + [pair, index_sems]

    def to_owners(mirror, twin):
        sent = call(functools.partial(split_kernel, n), "split", [vmem] * 2, [chunk] * (n // 2), [], (mirror, twin))
        return [moved(value, n, far_source(j, n)) for j, value in enumerate(sent)], sent[0]

    def gathered(near, mirror, twin, others, direct, stat):
        merged = call(functools.partial(merge_kernel, n), "merge", [vmem] * 4, [chunk] * n + [tile], [],
                      (direct, mirror, twin, stat))
        parts = [merged[0]] + [shifted(value, "col", d, n) for d, value in zip(distances(n), merged[1:n])]
        stat = merged[n]
        for b in bits(n):
            stat, = call(add_kernel, "add_stat", [vmem] * 3, [tile], [],
                         (stat, shifted(stat, "row", b, n), others[-1]))
        own, = call(functools.partial(combine_kernel, n), "combine", [vmem] * (3 + n + n // 2), [loaded], [],
                    (near, noise, stat, *parts, *others))
        return [own] + [shifted(own, "col", d, n) for d in distances(n)[::-1]]

    current = right_sides
    for b in bits(n)[:0:-1]:
        arrived = moved(current, n, spread_target(b))
        if b == n // 2:
            mirror, blocks = call(
                mirror_first_kernel, "mirror_first", [hbm] * 2 + [smem] + [hbm] * 2,
                [total, jax.ShapeDtypeStruct(cov_blocks.shape[2:], cov_blocks.dtype)],
                index_scratch + [pltpu.VMEM((rhs, width), F32), pair, index_sems,
                                 pltpu.SemaphoreType.DMA, pltpu.SemaphoreType.DMA((slots // GROUP,))],
                (*map(in_hbm, index[:2]), block_count, in_hbm(right_sides), in_hbm(cov_blocks)), True)
            twin_mirror = shifted(mirror, "row", 1, n)
        current, = call(functools.partial(pick_kernel, b), "pick", [vmem] * 3, [field], [], (current, arrived, mirror))
    twin = shifted(current, "row", 1, n)
    others, mark = to_owners(mirror, twin_mirror)
    direct, stat, far = call(
        functools.partial(direct_first_kernel, n), "direct_first", [any_spec] * 2 + [smem] + [vmem] * 6,
        [total, tile, total], kernel_index, (*index, noise, blocks, right_sides, current, twin, mark), True)
    parts = gathered(right_sides, mirror, twin_mirror, others, direct, stat)
    far_parts = [moved(parts[0], n, far_target(j)) for j in range(n // 2)]

    left, stat_now = call(left_kernel, "left", [vmem] * (n + 1), [field, tile], [], (right_sides, *parts))
    mirror, = call(mirror_second_kernel, "mirror_second", [any_spec] * 2 + [smem] + [vmem] * 2,
                   [total], kernel_index, (*index, left, blocks), True)
    twin_mirror = shifted(mirror, "row", 1, n)
    held, = call(functools.partial(held_kernel, n), "held", [vmem] * (4 + n // 2), [total], [],
                 (left, stat_now, far, mirror, *far_parts))
    twin = shifted(held, "row", 1, n)
    others, mark = to_owners(mirror, twin_mirror)
    direct, stat = call(
        functools.partial(direct_second_kernel, n), "direct_second", [any_spec] * 2 + [smem] + [vmem] * 6,
        [total, tile], kernel_index, (*index, noise, blocks, left, held, twin, mark), True)
    parts = gathered(left, mirror, twin_mirror, others, direct, stat)
    return tuple(call(last_kernel, "last", [vmem] * (n + 3), [field, field], [],
                      (right_sides, left, stat_now, *parts)))


def solution(mesh):
    n = mesh.shape["row"]
    assert n == mesh.shape["col"] and n & (n - 1) == 0 and n >= 4
    placed = (
        P(None, ("groups", "row")),
        P(("groups", "row")),
        P(("groups", "row"), "col", None, None, None),
        P(("groups", "row"), "col", None),
        P(("groups", "row"), "col", None),
        P(("groups", "row"), "col"),
    )
    return jax.shard_map(
        functools.partial(on_device, n),
        mesh=mesh,
        in_specs=placed,
        out_specs=(P(None, ("groups", "row")), P(None, ("groups", "row"))),
        check_vma=False,
    )
```

```python
import functools

import jax
import jax.numpy as jnp
from jax import lax
from jax.experimental import pallas as pl
from jax.experimental.pallas import tpu as pltpu
from jax.sharding import PartitionSpec as P

ITERS = 2
LANES = 128
GROUP = 8
WIDTHS = (16, 8, 4)
BF16 = jnp.bfloat16
F32 = jnp.float32


def shifted(value, axis, d, n):
    return lax.ppermute(value, axis, [(i, i ^ d) for i in range(n)])


def distances(n):
    return list(range(n - 1, 0, -1))


def moved(value, n, target):
    pairs = [(r * n + c, target(r, c)) for r in range(n) for c in range(n)]
    return lax.ppermute(value, ("row", "col"), [(s, t[0] * n + t[1]) for s, t in pairs])


def far_target(j):
    def target(r, c):
        d = r ^ c
        if d ^ 2 * j >= 2:
            return c ^ 2 * j, r
        return c ^ (d & 1) ^ (j == 0), c

    return target


def far_source(j, n):
    back = {far_target(j)(r, c): (r, c) for r in range(n) for c in range(n)}
    return lambda r, c: back[r, c]


def spread_target(b):
    def target(r, c):
        o = r ^ c
        move = {0: b, b: 1, b + 1: b, 1: 1}.get(o % (2 * b), 1)
        return r ^ move, c

    return target


def bits(n):
    return [1 << i for i in range(n.bit_length() - 1)]


def load_pair(dst, tile, value):
    rhs = value.shape[0]
    high = value.astype(BF16)
    dst[tile, :rhs, :] = high
    dst[tile, rhs:, :] = (value - high.astype(F32)).astype(BF16)


def product(pair, block, contract):
    both = lax.dot_general(pair, block, (((1,), (contract,)), ((), ())), preferred_element_type=F32)
    rhs = both.shape[0] // 2
    return both[:rhs] + both[rhs:]


def pack_stats(columns, rhs):
    lane = lax.broadcasted_iota(jnp.int32, (8, LANES), 1)
    tile = jnp.zeros((8, LANES), F32)
    groups = rhs // 8
    for i, column in enumerate(columns):
        for g in range(groups):
            tile = jnp.where(lane == i * groups + g, column[g * 8:(g + 1) * 8], tile)
    return tile


def unpack_stat(tile, i, rhs):
    groups = rhs // 8
    return jnp.concatenate([tile[:, i * groups + g:i * groups + g + 1] for g in range(groups)], axis=0)


def accumulate(total, tile, value):
    width = value.shape[1] // LANES
    for part in range(width):
        total[tile * width + part] += value[:, part * LANES:(part + 1) * LANES]


def add_blocks(blocks, slot_rows, slot_cols, live, pairs, total, mirror, widths, ready=None):
    read, write, contract = (slot_rows, slot_cols, 0) if mirror else (slot_cols, slot_rows, 1)

    def steps(group, base):
        def body(step, carry):
            if ready is not None:
                ready(step)
            for g in range(group):
                slot = base + step * group + g
                value = product(pairs[read[0, 0, slot]], blocks[slot], contract)
                accumulate(total, write[0, 0, slot], jnp.where(slot < live, value, 0.0))
            return carry

        return body

    done = 0
    for group in widths[:-1]:
        count = (live - done) // group
        lax.fori_loop(0, count, steps(group, done), 0)
        done += count * group
    lax.fori_loop(0, (live - done + widths[-1] - 1) // widths[-1], steps(widths[-1], done), 0)


def image_part(parts, me, i, per, rhs):
    rows = slice((i % per) * rhs, (i % per + 1) * rhs)
    value = parts[0][rows, :]
    for d, part in zip(distances(len(parts))[::-1], parts[1:]):
        value = jnp.where(me ^ d == i // per, part[rows, :], value)
    return value


def row_sums(value):
    return jnp.sum(value, axis=1, keepdims=True)


def cross_sums(total, value):
    rhs = value.shape[0]
    cross = jnp.zeros((rhs, LANES), F32)
    for i in range(total.shape[0]):
        cross += total[i] * value[:, i * LANES:(i + 1) * LANES]
    return row_sums(cross)


def tree_sum(values):
    values = list(values)
    while len(values) > 1:
        values = [a + b for a, b in zip(values[::2], values[1::2])]
    return values[0]


def stat_sum(parts, data):
    order = [0] + distances(len(parts))[::-1]
    return tree_sum(parts[order.index(d)][data:, :] for d in range(len(parts)))


def fetch_index(sources, targets, sems):
    copies = [pltpu.make_async_copy(s, t, sems.at[i]) for i, (s, t) in enumerate(zip(sources, targets))]
    for copy in copies:
        copy.start()
    return copies


def mirror_first_kernel(rows_hbm, cols_hbm, count, right_hbm, cov, total, blocks, *scratch):
    slot_rows, slot_cols, right, pairs, index_sems, right_sem, block_sems = scratch
    slots, tile_size = blocks.shape[:2]

    def block_copy(i):
        part = pl.ds(i * GROUP, GROUP)
        return pltpu.make_async_copy(cov.at[0, 0, part], blocks.at[part], block_sems.at[i])

    copies = fetch_index((rows_hbm, cols_hbm), (slot_rows, slot_cols), index_sems)
    load = pltpu.make_async_copy(right_hbm, right, right_sem)
    load.start()
    live = count[0, 0]
    for i in range(slots // GROUP):
        @pl.when(i * GROUP < live)
        def _():
            block_copy(i).start()
    total[...] = jnp.zeros_like(total)
    load.wait()
    for tile in range(right.shape[1] // tile_size):
        load_pair(pairs, tile, right[:, tile * tile_size:(tile + 1) * tile_size])
    for copy in copies:
        copy.wait()
    add_blocks(blocks, slot_rows, slot_cols, live, pairs, total, True, (GROUP,), lambda i: block_copy(i).wait())


def mirror_second_kernel(rows_any, cols_any, count, near, blocks, total, *scratch):
    slot_rows, slot_cols, pairs, index_sems = scratch
    tile_size = blocks.shape[1]
    copies = fetch_index((rows_any, cols_any), (slot_rows, slot_cols), index_sems)
    total[...] = jnp.zeros_like(total)
    for tile in range(near.shape[1] // tile_size):
        load_pair(pairs, tile, near[:, tile * tile_size:(tile + 1) * tile_size])
    for copy in copies:
        copy.wait()
    add_blocks(blocks, slot_rows, slot_cols, count[0, 0], pairs, total, True, WIDTHS)


def finish_direct(total, near, noise, stat, n):
    value = near[...]
    rhs = value.shape[0]
    square = value * value
    share = 1.0 / n
    bend = share * row_sums(square * noise[...]) + 2.0 * cross_sums(total, value)
    stat[...] = pack_stats([share * row_sums(square), bend], rhs)


def direct_first_kernel(n, rows_any, cols_any, count, noise, blocks, near, current, twin, mark, total, stat, far, *scratch):
    slot_rows, slot_cols, pairs, index_sems = scratch
    tile_size = blocks.shape[1]
    pieces = tile_size // LANES
    copies = fetch_index((rows_any, cols_any), (slot_rows, slot_cols), index_sems)
    odd = (lax.axis_index("row") ^ lax.axis_index("col")) & 1
    for o, source in enumerate((current, twin)):
        @pl.when(odd == o)
        def _():
            for tile in range(near.shape[1] // tile_size):
                value = source[:, tile * tile_size:(tile + 1) * tile_size]
                load_pair(pairs, tile, value)
                for i in range(pieces):
                    far[tile * pieces + i] = value[:, i * LANES:(i + 1) * LANES]
    total[...] = jnp.zeros_like(total)
    for copy in copies:
        copy.wait()
    add_blocks(blocks, slot_rows, slot_cols, count[0, 0], pairs, total, False, WIDTHS)
    finish_direct(total, near, noise, stat, n)


def direct_second_kernel(n, rows_any, cols_any, count, noise, blocks, near, held, twin, mark, total, stat, *scratch):
    slot_rows, slot_cols, pairs, index_sems = scratch
    tile_size = blocks.shape[1]
    pieces = tile_size // LANES
    per = held.shape[0] // n
    copies = fetch_index((rows_any, cols_any), (slot_rows, slot_cols), index_sems)
    row = lax.axis_index("row")
    offset = row ^ lax.axis_index("col")
    for tile in range(near.shape[1] // tile_size):
        value = []
        for i in range(tile * pieces, (tile + 1) * pieces):
            own = jnp.logical_or(offset == 0, jnp.logical_and(offset >= 2, ((i // per) ^ row) & 1 == 0))
            value.append(jnp.where(own, held[i], twin[i]))
        load_pair(pairs, tile, jnp.concatenate(value, axis=1))
    total[...] = jnp.zeros_like(total)
    for copy in copies:
        copy.wait()
    add_blocks(blocks, slot_rows, slot_cols, count[0, 0], pairs, total, False, WIDTHS)
    finish_direct(total, near, noise, stat, n)


def add_kernel(one, two, *refs):
    refs[-1][...] = one[...] + two[...]


def pick_kernel(b, current, arrived, mark, out):
    there = (lax.axis_index("row") ^ lax.axis_index("col")) & b
    out[...] = jnp.where(there != 0, arrived[...], current[...])


def split_kernel(n, mirror, twin, *outs):
    per = mirror.shape[0] // n
    rhs = mirror.shape[1]
    row = lax.axis_index("row")
    for j, out in enumerate(outs):
        first = (row ^ 2 * j) * per
        for i in range(per):
            out[i * rhs:(i + 1) * rhs, :] = mirror[first + i] + twin[first + i]


def merge_kernel(n, direct, mirror, twin, stat, *outs):
    per = direct.shape[0] // n
    rhs = direct.shape[1]
    me = lax.axis_index("col")
    diagonal = lax.axis_index("row") == me
    outs[n][...] = stat[...]
    for d, out in zip([0] + distances(n), outs):
        first = (me ^ d) * per

        @pl.when(diagonal)
        def _():
            for i in range(per):
                out[i * rhs:(i + 1) * rhs, :] = direct[first + i] + (mirror[first + i] + twin[first + i])

        @pl.when(jnp.logical_not(diagonal))
        def _():
            for i in range(per):
                out[i * rhs:(i + 1) * rhs, :] = direct[first + i]


def combine_kernel(n, near, noise, stat, *refs):
    parts, others, chunk = refs[:n], refs[n:-1], refs[-1]
    rhs = near.shape[0]
    data = parts[0].shape[0]
    per = data // rhs
    me = lax.axis_index("col")
    group = (lax.axis_index("row") ^ me) // 2
    value = tree_sum(ref[...] for ref in parts)
    for j, other in enumerate(others):
        value += jnp.where(group == j, 0.0, other[...])
    chunk[:data, :] = value
    chunk[data:, :] = stat[...]
    for k in range(n):
        @pl.when(me == k)
        def _():
            for i in range(per):
                lanes = slice((k * per + i) * LANES, (k * per + i + 1) * LANES)
                chunk[i * rhs:(i + 1) * rhs, :] += near[:, lanes] * noise[:, lanes]


def left_kernel(right, *refs):
    parts, (left, stat) = refs[:-2], refs[-2:]
    rhs, width = right.shape
    data = parts[0].shape[0] - 8
    per = data // rhs
    me = lax.axis_index("col")
    both = stat_sum(parts, data)
    stat[...] = both
    size_now = unpack_stat(both, 0, rhs) / unpack_stat(both, 1, rhs)
    for i in range(width // LANES):
        lanes = slice(i * LANES, (i + 1) * LANES)
        left[:, lanes] = right[:, lanes] - size_now * image_part(parts, me, i, per, rhs)


def held_kernel(n, left, stat, far, mark, *refs):
    parts, held = refs[:-1], refs[-1]
    rhs = left.shape[0]
    per = held.shape[0] // n
    row = lax.axis_index("row")
    diagonal = (row ^ lax.axis_index("col")) < 2
    size_now = unpack_stat(stat[...], 0, rhs) / unpack_stat(stat[...], 1, rhs)

    @pl.when(diagonal)
    def _():
        for i in range(held.shape[0]):
            held[i] = left[:, i * LANES:(i + 1) * LANES]

    @pl.when(jnp.logical_not(diagonal))
    def _():
        for j, part in enumerate(parts):
            first = (row ^ 2 * j) * per
            for i in range(per):
                held[first + i] = far[first + i] - size_now * part[i * rhs:(i + 1) * rhs, :]


def last_kernel(right, left, stat_now, *refs):
    parts, (solution, residual) = refs[:-2], refs[-2:]
    rhs, width = right.shape
    data = parts[0].shape[0] - 8
    per = data // rhs
    me = lax.axis_index("col")
    both = stat_sum(parts, data)
    norm = unpack_stat(stat_now[...], 0, rhs)
    norm_next = unpack_stat(both, 0, rhs)
    size_now = norm / unpack_stat(stat_now[...], 1, rhs)
    ratio = norm_next / norm
    size_next = norm_next / (unpack_stat(both, 1, rhs) - ratio * norm_next / size_now)
    back = ratio / size_now
    for i in range(width // LANES):
        lanes = slice(i * LANES, (i + 1) * LANES)
        first = right[:, lanes]
        now = left[:, lanes]
        solution[:, lanes] = size_now * first + size_next * (now + ratio * first)
        image = image_part(parts, me, i, per, rhs) + back * (first - now)
        residual[:, lanes] = now - size_next * image


def shape_of(*shape):
    return jax.ShapeDtypeStruct(shape, F32)


def on_device(n, right_sides, nugget, cov_blocks, block_rows, block_cols, block_count):
    rhs, width = right_sides.shape
    slots, tile_size = cov_blocks.shape[2:4]
    per = width // n // LANES
    data = per * rhs
    size = data + 8
    noise = nugget.reshape(1, width)
    index = (block_rows, block_cols, block_count)
    pair = pltpu.VMEM((width // tile_size, 2 * rhs, tile_size), BF16)
    index_scratch = [pltpu.SMEM(item.shape, item.dtype) for item in index[:2]]
    index_sems = pltpu.SemaphoreType.DMA((2,))
    vmem = pl.BlockSpec(memory_space=pltpu.VMEM)
    any_spec = pl.BlockSpec(memory_space=pl.ANY)
    smem = pl.BlockSpec(memory_space=pltpu.SMEM)
    hbm = pl.BlockSpec(memory_space=pltpu.HBM)
    params = pltpu.CompilerParams(vmem_limit_bytes=16 * 1024 * 1024)
    cost = pl.CostEstimate(flops=4 * rhs * slots * tile_size * tile_size, transcendentals=0,
                           bytes_accessed=2 * slots * tile_size * tile_size)
    field = shape_of(rhs, width)
    total = shape_of(width // LANES, rhs, LANES)
    chunk = shape_of(data, LANES)
    tile = shape_of(8, LANES)
    loaded = shape_of(size, LANES)

    def call(kernel, name, specs, outs, scratch, args, heavy=False):
        return pl.pallas_call(
            kernel,
            in_specs=specs,
            out_specs=jax.tree.map(lambda _: vmem, outs),
            out_shape=outs,
            scratch_shapes=scratch,
            compiler_params=params,
            cost_estimate=cost if heavy else None,
            name=name,
        )(*args)

    in_hbm = functools.partial(pltpu.with_memory_space_constraint, memory_space=pltpu.HBM)
    kernel_index = index_scratch + [pair, index_sems]

    def to_owners(mirror, twin):
        sent = call(functools.partial(split_kernel, n), "split", [vmem] * 2, [chunk] * (n // 2), [], (mirror, twin))
        return [moved(value, n, far_source(j, n)) for j, value in enumerate(sent)], sent[0]

    def gathered(near, mirror, twin, others, direct, stat):
        merged = call(functools.partial(merge_kernel, n), "merge", [vmem] * 4, [chunk] * n + [tile], [],
                      (direct, mirror, twin, stat))
        parts = [merged[0]] + [shifted(value, "col", d, n) for d, value in zip(distances(n), merged[1:n])]
        stat = merged[n]
        for b in bits(n)[::-1]:
            stat, = call(add_kernel, "add_stat", [vmem] * (2 + n // 2), [tile], [],
                         (stat, shifted(stat, "row", b, n), *others))
        own, = call(functools.partial(combine_kernel, n), "combine", [vmem] * (3 + n + n // 2), [loaded], [],
                    (near, noise, stat, *parts, *others))
        return [own] + [shifted(own, "col", d, n) for d in distances(n)[::-1]]

    current = right_sides
    for b in bits(n)[:0:-1]:
        arrived = moved(current, n, spread_target(b))
        if b == n // 2:
            mirror, blocks = call(
                mirror_first_kernel, "mirror_first", [hbm] * 2 + [smem] + [hbm] * 2,
                [total, jax.ShapeDtypeStruct(cov_blocks.shape[2:], cov_blocks.dtype)],
                index_scratch + [pltpu.VMEM((rhs, width), F32), pair, index_sems,
                                 pltpu.SemaphoreType.DMA, pltpu.SemaphoreType.DMA((slots // GROUP,))],
                (*map(in_hbm, index[:2]), block_count, in_hbm(right_sides), in_hbm(cov_blocks)), True)
            twin_mirror = shifted(mirror, "row", 1, n)
        current, = call(functools.partial(pick_kernel, b), "pick", [vmem] * 3, [field], [], (current, arrived, mirror))
    twin = shifted(current, "row", 1, n)
    others, mark = to_owners(mirror, twin_mirror)
    direct, stat, far = call(
        functools.partial(direct_first_kernel, n), "direct_first", [any_spec] * 2 + [smem] + [vmem] * 6,
        [total, tile, total], kernel_index, (*index, noise, blocks, right_sides, current, twin, mark), True)
    parts = gathered(right_sides, mirror, twin_mirror, others, direct, stat)
    far_parts = [moved(parts[0], n, far_target(j)) for j in range(n // 2)]

    left, stat_now = call(left_kernel, "left", [vmem] * (n + 1), [field, tile], [], (right_sides, *parts))
    mirror, = call(mirror_second_kernel, "mirror_second", [any_spec] * 2 + [smem] + [vmem] * 2,
                   [total], kernel_index, (*index, left, blocks), True)
    twin_mirror = shifted(mirror, "row", 1, n)
    held, = call(functools.partial(held_kernel, n), "held", [vmem] * (4 + n // 2), [total], [],
                 (left, stat_now, far, mirror, *far_parts))
    twin = shifted(held, "row", 1, n)
    others, mark = to_owners(mirror, twin_mirror)
    direct, stat = call(
        functools.partial(direct_second_kernel, n), "direct_second", [any_spec] * 2 + [smem] + [vmem] * 6,
        [total, tile], kernel_index, (*index, noise, blocks, left, held, twin, mark), True)
    parts = gathered(left, mirror, twin_mirror, others, direct, stat)
    return tuple(call(last_kernel, "last", [vmem] * (n + 3), [field, field], [],
                      (right_sides, left, stat_now, *parts)))


def solution(mesh):
    n = mesh.shape["row"]
    assert n == mesh.shape["col"] and n & (n - 1) == 0 and n >= 4
    placed = (
        P(None, ("groups", "row")),
        P(("groups", "row")),
        P(("groups", "row"), "col", None, None, None),
        P(("groups", "row"), "col", None),
        P(("groups", "row"), "col", None),
        P(("groups", "row"), "col"),
    )
    return jax.shard_map(
        functools.partial(on_device, n),
        mesh=mesh,
        in_specs=placed,
        out_specs=(P(None, ("groups", "row")), P(None, ("groups", "row"))),
        check_vma=False,
    )
```
